32 devices in a mesh: row: 4 (over y, x), col: 8 (over z, core).
Axes of the slice: x: 2, y: 2, z: 4, core: 2. Of those that a mesh axis runs over, the one named last changes fastest.
Arguments:
- embed: float32 [8192, 128], P(('row', 'col')), may hold values from -6 to 6
- cotangent: float32 [8192, 128], P(('col', 'row')), may hold values from -6 to 6
- tile_values: float32 [8, 4, 128, 128, 128], P('col', 'row'), may hold values from 0 to 1
- tile_coords: int32 [2, 8, 4, 128], P(None, 'col', 'row'), may hold values from 0 to 15, as said below
- tile_count: int32 [8, 4], P('col', 'row'), may hold values from 1 to 128, as said below
- row_degree: int32 [8192], P(('col', 'row')), may hold values from 16 to 511
- col_degree: int32 [8192], P(('row', 'col')), may hold values from 16 to 511
Outputs:
- propagated: float32 [8192, 128], P(('col', 'row'))
- embed_grad: float32 [8192, 128], P(('row', 'col'))
The draws below stay inside these ranges and needn't reach their ends.
Inputs may be any that keep to these rules, and one draw needn't show every extreme that they name: `tile_coords`: within one device block the slots hold distinct tile positions; the first component is below 8 and the second below 16. `tile_count`: some device block has all 128 slots live.
All inputs are finite; a program needn't handle non-finite values.
Results may differ from the reference program's by a relative error of at most 0.0003.
Values sent between devices are 32-bit elements; how exact they have to be, the bound alone decides.
No kernel may reach another device: no remote copies, remote signals or barrier semaphores. Data moves between devices by JAX's collectives and lax.ppermute only.
A program may use at most 128 MiB of HBM per device.

```python
import jax
import jax.numpy as jnp
from jax import lax

D = 128
TILE = 128
NODES_DEV = 256
TILE_CAP = 128
NODES = 8192
N_ROW = 4
N_COL = 8


def draw_tile_coords(key, part):
    row_tiles = NODES_DEV * N_ROW // TILE
    col_tiles = NODES_DEV * N_COL // TILE
    keys = jax.random.split(jax.random.fold_in(key, 11), N_COL * N_ROW)

    def one_block(block_key):
        order = jax.random.permutation(block_key, row_tiles * col_tiles)[:TILE_CAP]
        return jnp.stack([order // col_tiles, order % col_tiles]).astype(jnp.int32)
    blocks = jax.vmap(one_block)(keys)
    return jnp.transpose(blocks, (1, 0, 2)).reshape(2, N_COL, N_ROW, TILE_CAP)


def draw_tile_count(key, part):
    first_key, second_key, third_key, fourth_key = jax.random.split(jax.random.fold_in(key, 23), 4)
    shape = (N_COL, N_ROW)
    light = jax.random.randint(first_key, shape, TILE_CAP // 4, TILE_CAP // 2 + 1)
    hub_flag = jax.random.randint(second_key, shape, 0, 4) == 0
    heavy = TILE_CAP - jax.random.randint(third_key, shape, 0, TILE_CAP // 8 + 1)
    counts = jnp.where(hub_flag, heavy, light).reshape(-1)
    fullest = jax.random.randint(fourth_key, (), 0, N_COL * N_ROW)
    counts = counts.at[fullest].set(TILE_CAP)
    return counts.reshape(shape).astype(jnp.int32)


def place_ends(result, own_key, least, largest):
    longest = result.shape.index(max(result.shape))
    spots = []
    for shift in (0, 1):
        where = [jax.random.randint(jax.random.fold_in(own_key, axis), (), 0, length) for axis, length in enumerate(result.shape)]
        where[longest] = (where[longest] + shift) % result.shape[longest]
        spots.append(tuple(where))
    return result.at[spots[0]].set(least).at[spots[1]].set(largest)


def block_levels(rng, dims, cuts, least, largest):
    factor_of, own = 1.0, jax.random.fold_in(rng, 6)
    for dim, shards_of in cuts:
        draws = jnp.exp(jax.random.uniform(jax.random.fold_in(own, dim), (shards_of,), jnp.float32, least / len(cuts), largest / len(cuts)))
        factor_of = factor_of * jnp.repeat(draws, dims[dim] // shards_of).reshape([-1 if axis == dim else 1 for axis in range(len(dims))])
    return factor_of


def centred(key, extent, deviation, limit, shards=(), kind=jnp.bfloat16):
    result = jax.random.normal(key, extent, jnp.float32) * deviation
    if len(shards) > 0:
        result = block_levels(key, extent, shards, -0.22, 0.18) * result
    return jnp.clip(result, min=-limit, max=limit).astype(kind)


def setup_inputs(seed: int = 0) -> dict:
    seeds = jax.random.split(jax.random.key(seed), 8)
    embed = centred(seeds[0], (NODES, D), 1.0, 6.0, ((0, 32),), jnp.float32)
    cotangent = centred(seeds[1], (NODES, D), 1.0, 6.0, ((0, 32),), jnp.float32)
    tile_values = jnp.clip(1.0 * jax.random.uniform(seeds[2], (N_COL, N_ROW, TILE_CAP, TILE, TILE), jnp.float32) ** block_levels(seeds[2], (N_COL, N_ROW, TILE_CAP, TILE, TILE), ((0, 8), (1, 4)), -0.2, 0.2), 0.0, 1.0)
    tile_coords = draw_tile_coords(jax.random.fold_in(seeds[7], 71), 0)
    tile_count = draw_tile_count(jax.random.fold_in(seeds[7], 71), 0)
    row_degree = place_ends(jax.random.randint(seeds[5], (NODES,), 16, 512), jax.random.fold_in(seeds[5], 1), 16, 511).astype(jnp.int32)
    col_degree = place_ends(jax.random.randint(seeds[6], (NODES,), 16, 512), jax.random.fold_in(seeds[6], 1), 16, 511).astype(jnp.int32)
    return dict(embed=embed, cotangent=cotangent, tile_values=tile_values, tile_coords=tile_coords, tile_count=tile_count, row_degree=row_degree, col_degree=col_degree)


def block_terms(values, rows_at, cols_at, live_count, embed_panel, grad_panel):
    tile_size = values.shape[-1]
    feature_width = embed_panel.shape[1]
    panel_tiles = embed_panel.reshape(-1, tile_size, feature_width)
    grad_tiles = grad_panel.reshape(-1, tile_size, feature_width)
    live_mask = jnp.arange(values.shape[0], dtype=jnp.int32) < live_count
    picked = jnp.take(panel_tiles, cols_at, axis=0)
    forward_each = jnp.einsum('tij,tjd->tid', values, picked, precision=lax.Precision.HIGHEST)
    row_hot = ((rows_at[None, :] == jnp.arange(grad_tiles.shape[0], dtype=jnp.int32)[:, None]) & live_mask[None, :]).astype(values.dtype)
    forward = jnp.einsum('at,tid->aid', row_hot, forward_each, precision=lax.Precision.HIGHEST)
    grad_picked = jnp.take(grad_tiles, rows_at, axis=0)
    backward_each = jnp.einsum('tij,tid->tjd', values, grad_picked, precision=lax.Precision.HIGHEST)
    col_hot = ((cols_at[None, :] == jnp.arange(panel_tiles.shape[0], dtype=jnp.int32)[:, None]) & live_mask[None, :]).astype(values.dtype)
    backward = jnp.einsum('bt,tjd->bjd', col_hot, backward_each, precision=lax.Precision.HIGHEST)
    return (forward.reshape(-1, feature_width), backward.reshape(-1, feature_width))

def reference(embed, cotangent, tile_values, tile_coords, tile_count, row_degree, col_degree):
    rows_block = NODES // N_COL
    cols_block = NODES // N_ROW
    scaled = embed * lax.rsqrt(col_degree.astype(jnp.float32))[:, None]
    grad_scaled = cotangent * lax.rsqrt(row_degree.astype(jnp.float32))[:, None]

    def outer(grad_total, block_col):
        grad_panel = lax.dynamic_slice_in_dim(grad_scaled, block_col * rows_block, rows_block, 0)

        def inner(carry, block_row):
            forward_total, grad_inner = carry
            embed_panel = lax.dynamic_slice_in_dim(scaled, block_row * cols_block, cols_block, 0)
            forward, backward = block_terms(tile_values[block_col, block_row], tile_coords[0, block_col, block_row], tile_coords[1, block_col, block_row], tile_count[block_col, block_row], embed_panel, grad_panel)
            first_row = (block_row * cols_block).astype(jnp.int32)
            current = lax.dynamic_slice_in_dim(grad_inner, first_row, cols_block, 0)
            grad_inner = lax.dynamic_update_slice_in_dim(grad_inner, current + backward, first_row, 0)
            return ((forward_total + forward, grad_inner), None)
        start_forward = jnp.zeros((rows_block, embed.shape[1]), embed.dtype)
        (forward_total, grad_total), unused = lax.scan(inner, (start_forward, grad_total), jnp.arange(N_ROW, dtype=jnp.int32))
        return (grad_total, forward_total)
    grad_total, forward_blocks = lax.scan(outer, jnp.zeros_like(embed), jnp.arange(N_COL, dtype=jnp.int32))
    propagated = forward_blocks.reshape(NODES, embed.shape[1]) * lax.rsqrt(row_degree.astype(jnp.float32))[:, None]
    embed_grad = grad_total * lax.rsqrt(col_degree.astype(jnp.float32))[:, None]
    return (propagated, embed_grad)
```

```python
import functools

import jax
import jax.numpy as jnp
from jax import lax
from jax.experimental import pallas as pl
from jax.experimental.pallas import tpu as pltpu
from jax.sharding import PartitionSpec as P

F32 = jnp.float32
BF16 = jnp.bfloat16
WHOLE = pl.BlockSpec(memory_space=pltpu.VMEM)
SCALARS = pl.BlockSpec(memory_space=pltpu.SMEM)


def params(mebibytes):
    return pltpu.CompilerParams(vmem_limit_bytes=mebibytes * 2**20)


def cost(flops, moved):
    return pl.CostEstimate(flops=flops, bytes_accessed=moved, transcendentals=0)


def halves(x):
    high = x.astype(BF16)
    return high, (x - high.astype(F32)).astype(BF16)


def product(left, right):
    return jnp.dot(left, right, preferred_element_type=F32)


def row_factors(degree_ref, at, width):
    factors = lax.rsqrt(degree_ref[at : at + 1, :].astype(F32))
    return jnp.broadcast_to(factors, (width, factors.shape[1])).T


def scale_kernel(embed_ref, col_degree_ref, cotangent_ref, row_degree_ref, scaled_ref, grad_ref):
    tile = col_degree_ref.shape[1]
    for x_ref, degree_ref, out_ref in (
        (cotangent_ref, row_degree_ref, grad_ref),
        (embed_ref, col_degree_ref, scaled_ref),
    ):
        for at in range(degree_ref.shape[0]):
            rows = pl.ds(at * tile, tile)
            out_ref[rows, :] = x_ref[rows, :] * row_factors(degree_ref, at, x_ref.shape[1])


def finish_kernel(*refs):
    *part_refs, degree_ref, out_ref = refs
    tile = degree_ref.shape[1]
    for at in range(degree_ref.shape[0]):
        rows = pl.ds(at * tile, tile)
        total = part_refs[0][rows, :]
        for part_ref in part_refs[1:]:
            total = total + part_ref[rows, :]
        out_ref[rows, :] = total * row_factors(degree_ref, at, out_ref.shape[1])


def pair_kernel(kept_ref, got_ref, *out_refs):
    for at, out_ref in enumerate(out_refs):
        out_ref[...] = kept_ref[at] + got_ref[at]


def place(tile_at, shard, tiles):
    return ((tile_at // tiles) ^ shard) * tiles + tile_at % tiles


def split_kernel(tiles, coords_ref, count_ref, values_ref, high_ref, low_ref):
    group, tile, _ = values_ref.shape
    first = pl.program_id(0) * group
    my_row, my_col = lax.axis_index("row"), lax.axis_index("col")
    for slot in range(group):
        row_at = place(coords_ref[0, 0, 0, first + slot], my_row, tiles)
        col_at = place(coords_ref[1, 0, 0, first + slot], my_col, tiles)
        live = first + slot < count_ref[0, 0]
        high, low = halves(jnp.where(live, values_ref[slot], 0.0))
        rows = pl.ds(pl.multiple_of(row_at * tile, tile), tile)
        cols = pl.ds(pl.multiple_of(col_at * tile, tile), tile)
        high_ref[rows, cols] = high
        low_ref[rows, cols] = low


def backward_kernel(tile, *refs):
    *grad_refs, high_ref, low_ref, kept_ref, sent_ref, grads = refs
    width = grad_refs[0].shape[1]
    shard = grad_refs[0].shape[0]

    @pl.when(pl.program_id(0) == 0)
    def _():
        for at, grad_ref in enumerate(grad_refs):
            for first in range(0, shard, tile):
                high, low = halves(grad_ref[pl.ds(first, tile), :].T)
                cols = pl.ds(at * shard + first, tile)
                grads[:width, cols] = high
                grads[width:, cols] = low

    both = product(grads[...], high_ref[...])
    total = both[:width] + both[width:] + product(grads[:width, :], low_ref[...])
    for first in range(0, shard, tile):
        rows = pl.ds(first, tile)
        kept_ref[0, rows, :] = total[:, first : first + tile].T
        sent_ref[0, rows, :] = total[:, shard + first : shard + first + tile].T


def forward_kernel(count, *refs):
    embed_refs, (high_ref, low_ref), out_refs, panel = refs[:count], refs[count : count + 2], refs[count + 2 : -1], refs[-1]
    shard, width = embed_refs[0].shape

    @pl.when(pl.program_id(0) == 0)
    def _():
        for at, embed_ref in enumerate(embed_refs):
            high, low = halves(embed_ref[...])
            panel[pl.ds(at * shard, shard), :width] = high
            panel[pl.ds(at * shard, shard), width:] = low

    both = product(high_ref[...], panel[...])
    total = both[:, :width] + both[:, width:] + product(low_ref[...], panel[:, :width])
    for at, out_ref in enumerate(out_refs):

        @pl.when(pl.program_id(0) == at)
        def _():
            out_ref[...] = total


def slots_kernel(tiles, coords_ref, count_ref, values_ref, embed_ref, grad_ref, forward_ref, backward_ref):
    group, tile, _ = values_ref.shape
    first = pl.program_id(0) * group
    my_row, my_col = lax.axis_index("row"), lax.axis_index("col")

    @pl.when(pl.program_id(0) == 0)
    def _():
        forward_ref[...] = jnp.zeros_like(forward_ref)
        backward_ref[...] = jnp.zeros_like(backward_ref)

    for slot in range(group):

        @pl.when(first + slot < count_ref[0, 0])
        def _():
            row_at = place(coords_ref[0, 0, 0, first + slot], my_row, tiles)
            col_at = place(coords_ref[1, 0, 0, first + slot], my_col, tiles)
            rows = pl.ds(pl.multiple_of(row_at * tile, tile), tile)
            cols = pl.ds(pl.multiple_of(col_at * tile, tile), tile)
            high, low = halves(values_ref[slot])
            embed_high, embed_low = halves(embed_ref[cols, :])
            forward_ref[rows, :] += product(high, embed_high) + product(high, embed_low) + product(low, embed_high)
            high, low = halves(values_ref[slot].T)
            grad_high, grad_low = halves(grad_ref[rows, :])
            backward_ref[cols, :] += product(high, grad_high) + product(high, grad_low) + product(low, grad_high)


def swap(x, axis, mask):
    size = lax.axis_size(axis)
    return lax.ppermute(x, axis, [(at, at ^ mask) for at in range(size)])


def per_device(embed, cotangent, tile_values, tile_coords, tile_count, row_degree, col_degree):
    shard, width = embed.shape
    capacity, tile = tile_values.shape[2:4]
    n_row, n_col = lax.axis_size("row"), lax.axis_size("col")
    pairs = n_col // 2
    tiles = shard // tile
    n_rows, n_cols = shard * n_row, shard * n_col
    values = tile_values.reshape(tile_values.shape[2:])
    row_degree = row_degree.reshape(-1, tile)
    col_degree = col_degree.reshape(-1, tile)
    block = jax.ShapeDtypeStruct((shard, width), F32)
    group = 8
    slot_specs = [SCALARS, SCALARS, pl.BlockSpec((group, tile, tile), lambda at: (at, 0, 0))]

    with jax.named_scope("scale"):
        scaled, grad_scaled = pl.pallas_call(
            scale_kernel,
            out_shape=(block, block),
            in_specs=[WHOLE] * 4,
            out_specs=(WHOLE, WHOLE),
            cost_estimate=cost(0, 4 * shard * width * 4),
        )(embed, col_degree, cotangent, row_degree)

    with jax.named_scope("gather"):
        grads = [grad_scaled] + [swap(grad_scaled, "row", k) for k in range(1, n_row)]
        own = [scaled] + [swap(scaled, "col", 2 * k) for k in range(1, pairs)]
        embeds = [x for mine in own for x in (mine, swap(mine, "col", 1))]

    dense = (n_rows // tile) * (n_cols // tile) <= capacity
    if dense:
        with jax.named_scope("split"):
            table = jax.ShapeDtypeStruct((n_rows, n_cols), BF16)
            table_spec = pl.BlockSpec((n_rows, n_cols), lambda at: (0, 0), pipeline_mode=pl.Buffered(1))
            high, low = pl.pallas_call(
                functools.partial(split_kernel, tiles),
                out_shape=(table, table),
                grid=(capacity // group,),
                in_specs=slot_specs,
                out_specs=(table_spec, table_spec),
                compiler_params=params(24),
                cost_estimate=cost(0, 2 * values.size * 4),
            )(tile_coords, tile_count, values)
        flops = 6 * n_rows * n_cols * width
        with jax.named_scope("backward"):
            halved = jax.ShapeDtypeStruct((pairs, shard, width), F32)
            strip = pl.BlockSpec((n_rows, 2 * shard), lambda at: (0, at))
            halved_spec = pl.BlockSpec((1, shard, width), lambda at: (at, 0, 0))
            kept, sent = pl.pallas_call(
                functools.partial(backward_kernel, tile),
                out_shape=(halved, halved),
                grid=(pairs,),
                in_specs=[WHOLE] * n_row + [strip, strip],
                out_specs=(halved_spec, halved_spec),
                scratch_shapes=[pltpu.VMEM((2 * width, n_rows), BF16)],
                compiler_params=params(24),
                cost_estimate=cost(flops, values.size * 4),
            )(*grads, high, low)
        with jax.named_scope("forward"):
            band = pl.BlockSpec((shard, n_cols), lambda at: (at, 0))
            forwards = pl.pallas_call(
                functools.partial(forward_kernel, n_col),
                out_shape=(block,) * n_row,
                grid=(n_row,),
                in_specs=[WHOLE] * n_col + [band, band],
                out_specs=(WHOLE,) * n_row,
                scratch_shapes=[pltpu.VMEM((n_cols, 2 * width), BF16)],
                compiler_params=params(24),
                cost_estimate=cost(flops, values.size * 4),
            )(*embeds, high, low)
    else:
        with jax.named_scope("slots"):
            forward, backward = pl.pallas_call(
                functools.partial(slots_kernel, tiles),
                out_shape=(
                    jax.ShapeDtypeStruct((n_rows, width), F32),
                    jax.ShapeDtypeStruct((n_cols, width), F32),
                ),
                grid=(capacity // group,),
                in_specs=slot_specs + [WHOLE, WHOLE],
                out_specs=(WHOLE, WHOLE),
                compiler_params=params(40),
                cost_estimate=cost(12 * values.size * width, values.size * 4),
            )(tile_coords, tile_count, values, jnp.concatenate(embeds), jnp.concatenate(grads))
            forwards = list(forward.reshape(n_row, shard, width))
            backward = backward.reshape(pairs, 2, shard, width)
            kept, sent = backward[:, 0], backward[:, 1]

    with jax.named_scope("reduce"):
        paired = pl.pallas_call(
            pair_kernel,
            out_shape=(block,) * pairs,
            in_specs=[WHOLE] * 2,
            out_specs=(WHOLE,) * pairs,
            compiler_params=params(16),
            cost_estimate=cost(0, 3 * pairs * shard * width * 4),
        )(kept, swap(sent, "col", 1))
        grad_parts = [paired[0]] + [swap(paired[k], "col", 2 * k) for k in range(1, pairs)]
        row_parts = [forwards[0]] + [swap(forwards[k], "row", k) for k in range(1, n_row)]

    def finish(parts, degree):
        return pl.pallas_call(
            finish_kernel,
            out_shape=block,
            in_specs=[WHOLE] * (len(parts) + 1),
            out_specs=WHOLE,
            cost_estimate=cost(0, (len(parts) + 1) * shard * width * 4),
        )(*parts, degree)

    with jax.named_scope("finish"):
        return finish(row_parts, row_degree), finish(grad_parts, col_degree)


def solution(mesh):
    return jax.shard_map(
        per_device,
        mesh=mesh,
        in_specs=(
            P(("row", "col"), None),
            P(("col", "row"), None),
            P("col", "row", None, None, None),
            P(None, "col", "row", None),
            P("col", "row"),
            P(("col", "row")),
            P(("row", "col")),
        ),
        out_specs=(P(("col", "row"), None), P(("row", "col"), None)),
        check_vma=False,
    )
```

```python
import functools

import jax
import jax.numpy as jnp
from jax import lax
from jax.experimental import pallas as pl
from jax.experimental.pallas import tpu as pltpu
from jax.sharding import PartitionSpec as P

F32 = jnp.float32
BF16 = jnp.bfloat16
WHOLE = pl.BlockSpec(memory_space=pltpu.VMEM)
SCALARS = pl.BlockSpec(memory_space=pltpu.SMEM)


def params(mebibytes):
    return pltpu.CompilerParams(vmem_limit_bytes=mebibytes * 2**20)


def cost(flops, moved):
    return pl.CostEstimate(flops=flops, bytes_accessed=moved, transcendentals=0)


def halves(x):
    high = x.astype(BF16)
    return high, (x - high.astype(F32)).astype(BF16)


def product(left, right):
    return jnp.dot(left, right, preferred_element_type=F32)


def row_factors(degree_ref, at, width):
    factors = lax.rsqrt(degree_ref[at : at + 1, :].astype(F32))
    return jnp.broadcast_to(factors, (width, factors.shape[1])).T


def scale_kernel(embed_ref, col_degree_ref, cotangent_ref, row_degree_ref, scaled_ref, grad_ref):
    tile = col_degree_ref.shape[1]
    for x_ref, degree_ref, out_ref in (
        (cotangent_ref, row_degree_ref, grad_ref),
        (embed_ref, col_degree_ref, scaled_ref),
    ):
        for at in range(degree_ref.shape[0]):
            rows = pl.ds(at * tile, tile)
            scaled = x_ref[rows, :] * row_factors(degree_ref, at, x_ref.shape[1])
            for copy in range(out_ref.shape[0]):
                out_ref[copy, rows, :] = scaled


def finish_kernel(parts_ref, degree_ref, out_ref):
    tile = degree_ref.shape[1]
    for at in range(degree_ref.shape[0]):
        rows = pl.ds(at * tile, tile)
        total = parts_ref[0, rows, :]
        for part in range(1, parts_ref.shape[0]):
            total = total + parts_ref[part, rows, :]
        out_ref[rows, :] = total * row_factors(degree_ref, at, out_ref.shape[1])


def pair_kernel(kept_ref, got_ref, out_ref):
    out_ref[...] = kept_ref[...] + got_ref[...]


def col_place(tile_at, tiles, my_core, pairs):
    shard = tile_at // tiles
    return (((shard % 2) ^ my_core) * pairs + shard // 2) * tiles + tile_at % tiles


def split_kernel(tiles, pairs, coords_ref, count_ref, values_ref, high_ref, low_ref):
    group, tile, _ = values_ref.shape
    first = pl.program_id(0) * group
    my_core = lax.axis_index("col") % 2
    for slot in range(group):
        row_at = coords_ref[0, 0, 0, first + slot]
        col_at = col_place(coords_ref[1, 0, 0, first + slot], tiles, my_core, pairs)
        live = first + slot < count_ref[0, 0]
        high, low = halves(jnp.where(live, values_ref[slot], 0.0))
        rows = pl.ds(pl.multiple_of(row_at * tile, tile), tile)
        cols = pl.ds(pl.multiple_of(col_at * tile, tile), tile)
        high_ref[rows, cols] = high
        low_ref[rows, cols] = low


def backward_kernel(tile, grads_ref, high_ref, low_ref, out_ref, grads):
    n_row, shard, width = grads_ref.shape

    @pl.when(pl.program_id(0) == 0)
    def _():
        for at in range(n_row):
            for first in range(0, shard, tile):
                high, low = halves(grads_ref[at, pl.ds(first, tile), :].T)
                cols = pl.ds(at * shard + first, tile)
                grads[:width, cols] = high
                grads[width:, cols] = low

    both = product(grads[...], high_ref[...])
    total = both[:width] + both[width:] + product(grads[:width, :], low_ref[...])
    for first in range(0, shard, tile):
        out_ref[0, pl.ds(first, tile), :] = total[:, first : first + tile].T


def forward_kernel(embeds_ref, high_ref, low_ref, *refs):
    before_refs, out_ref, panel = refs[:-2], refs[-2], refs[-1]
    count, shard, width = embeds_ref.shape

    @pl.when(pl.program_id(0) == 0)
    def _():
        for at in range(count):
            high, low = halves(embeds_ref[at])
            panel[pl.ds(at * shard, shard), :width] = high
            panel[pl.ds(at * shard, shard), width:] = low

    both = product(high_ref[...], panel[...])
    total = both[:, :width] + both[:, width:] + product(low_ref[...], panel[:, :width])
    for before_ref in before_refs:
        total = total + before_ref[0]
    out_ref[0] = total


def slots_kernel(tiles, pairs, coords_ref, count_ref, values_ref, embed_ref, grad_ref, forward_ref, backward_ref):
    group, tile, _ = values_ref.shape
    first = pl.program_id(0) * group
    my_core = lax.axis_index("col") % 2

    @pl.when(pl.program_id(0) == 0)
    def _():
        forward_ref[...] = jnp.zeros_like(forward_ref)
        backward_ref[...] = jnp.zeros_like(backward_ref)

    for slot in range(group):

        @pl.when(first + slot < count_ref[0, 0])
        def _():
            row_at = coords_ref[0, 0, 0, first + slot]
            col_at = col_place(coords_ref[1, 0, 0, first + slot], tiles, my_core, pairs)
            rows = pl.ds(pl.multiple_of(row_at * tile, tile), tile)
            cols = pl.ds(pl.multiple_of(col_at * tile, tile), tile)
            high, low = halves(values_ref[slot])
            embed_high, embed_low = halves(embed_ref[cols, :])
            forward_ref[rows, :] += product(high, embed_high) + product(high, embed_low) + product(low, embed_high)
            high, low = halves(values_ref[slot].T)
            grad_high, grad_low = halves(grad_ref[rows, :])
            backward_ref[cols, :] += product(high, grad_high) + product(high, grad_low) + product(low, grad_high)


def exchange(x, axis, groups=None):
    return lax.all_to_all(x, axis, split_axis=0, concat_axis=0, axis_index_groups=groups, tiled=True)


def per_device(embed, cotangent, tile_values, tile_coords, tile_count, row_degree, col_degree):
    shard, width = embed.shape
    capacity, tile = tile_values.shape[2:4]
    n_row, n_col = lax.axis_size("row"), lax.axis_size("col")
    pairs = n_col // 2
    same_core = [list(range(core, n_col, 2)) for core in range(2)]
    tiles = shard // tile
    n_rows, n_cols = shard * n_row, shard * n_col
    values = tile_values.reshape(tile_values.shape[2:])
    row_degree = row_degree.reshape(-1, tile)
    col_degree = col_degree.reshape(-1, tile)
    in_row = jax.ShapeDtypeStruct((n_row, shard, width), F32)
    in_col = jax.ShapeDtypeStruct((pairs, shard, width), F32)
    group = 8
    slot_specs = [SCALARS, SCALARS, pl.BlockSpec((group, tile, tile), lambda at: (at, 0, 0))]
    one_block = pl.BlockSpec((1, shard, width), lambda at: (at, 0, 0))

    def swap_cores(x):
        return lax.ppermute(x, "col", [(at, at ^ 1) for at in range(n_col)])

    with jax.named_scope("scale"):
        scaled, grad_scaled = pl.pallas_call(
            scale_kernel,
            out_shape=(in_col, in_row),
            in_specs=[WHOLE] * 4,
            out_specs=(WHOLE, WHOLE),
            compiler_params=params(8),
            cost_estimate=cost(0, 2 * (n_row + pairs) * shard * width * 4),
        )(embed, col_degree, cotangent, row_degree)

    with jax.named_scope("gather"):
        grads = exchange(grad_scaled, "row")
        own = exchange(scaled, "col", same_core)
        other = swap_cores(own)

    dense = (n_rows // tile) * (n_cols // tile) <= capacity
    if dense:
        with jax.named_scope("split"):
            table = jax.ShapeDtypeStruct((n_rows, n_cols), BF16)
            table_spec = pl.BlockSpec((n_rows, n_cols), lambda at: (0, 0), pipeline_mode=pl.Buffered(1))
            high, low = pl.pallas_call(
                functools.partial(split_kernel, tiles, pairs),
                out_shape=(table, table),
                grid=(capacity // group,),
                in_specs=slot_specs,
                out_specs=(table_spec, table_spec),
                compiler_params=params(24),
                cost_estimate=cost(0, 2 * values.size * 4),
            )(tile_coords, tile_count, pltpu.with_memory_space_constraint(values, pltpu.HBM))
        flops = 3 * n_rows * n_cols * width

        def backward_half(first):
            strip = pl.BlockSpec((n_rows, shard), lambda at: (0, first + at))
            return pl.pallas_call(
                functools.partial(backward_kernel, tile),
                out_shape=in_col,
                grid=(pairs,),
                in_specs=[WHOLE, strip, strip],
                out_specs=one_block,
                scratch_shapes=[pltpu.VMEM((2 * width, n_rows), BF16)],
                compiler_params=params(16),
                cost_estimate=cost(flops, values.size * 2),
            )(grads, high, low)

        def forward_half(embeds, half, before):
            band = pl.BlockSpec((shard, n_cols // 2), lambda at: (at, half))
            return pl.pallas_call(
                forward_kernel,
                out_shape=in_row,
                grid=(n_row,),
                in_specs=[WHOLE, band, band] + [one_block] * len(before),
                out_specs=one_block,
                scratch_shapes=[pltpu.VMEM((n_cols // 2, 2 * width), BF16)],
                compiler_params=params(16),
                cost_estimate=cost(flops, values.size * 2),
            )(embeds, high, low, *before)

        with jax.named_scope("backward"):
            sent = backward_half(pairs)
            kept = backward_half(0)
        with jax.named_scope("forward"):
            forward = forward_half(other, 1, [forward_half(own, 0, [])])
    else:
        with jax.named_scope("slots"):
            forward, backward = pl.pallas_call(
                functools.partial(slots_kernel, tiles, pairs),
                out_shape=(
                    jax.ShapeDtypeStruct((n_rows, width), F32),
                    jax.ShapeDtypeStruct((n_cols, width), F32),
                ),
                grid=(capacity // group,),
                in_specs=slot_specs + [WHOLE, WHOLE],
                out_specs=(WHOLE, WHOLE),
                compiler_params=params(40),
                cost_estimate=cost(12 * values.size * width, values.size * 4),
            )(tile_coords, tile_count, values, jnp.concatenate([own, other]).reshape(n_cols, width), grads.reshape(n_rows, width))
            forward = forward.reshape(n_row, shard, width)
            kept, sent = backward.reshape(2, pairs, shard, width)

    with jax.named_scope("reduce"):
        paired = pl.pallas_call(
            pair_kernel,
            out_shape=in_col,
            in_specs=[WHOLE] * 2,
            out_specs=WHOLE,
            compiler_params=params(16),
            cost_estimate=cost(0, 3 * pairs * shard * width * 4),
        )(kept, swap_cores(sent))
        grad_parts = exchange(paired, "col", same_core)
        row_parts = exchange(forward, "row")

    def finish(parts, degree):
        return pl.pallas_call(
            finish_kernel,
            out_shape=jax.ShapeDtypeStruct((shard, width), F32),
            in_specs=[WHOLE] * 2,
            out_specs=WHOLE,
            compiler_params=params(8),
            cost_estimate=cost(0, parts.size * 4),
        )(parts, degree)

    with jax.named_scope("finish"):
        return finish(row_parts, row_degree), finish(grad_parts, col_degree)


def solution(mesh):
    return jax.shard_map(
        per_device,
        mesh=mesh,
        in_specs=(
            P(("row", "col"), None),
            P(("col", "row"), None),
            P("col", "row", None, None, None),
            P(None, "col", "row", None),
            P("col", "row"),
            P(("col", "row")),
            P(("row", "col")),
        ),
        out_specs=(P(("col", "row"), None), P(("row", "col"), None)),
        check_vma=False,
    )
```

```python
import functools
import math

import jax
import jax.numpy as jnp
from jax import lax
from jax.experimental import pallas as pl
from jax.experimental.pallas import tpu as pltpu
from jax.sharding import PartitionSpec as P

F32 = jnp.float32
BF16 = jnp.bfloat16
WHOLE = pl.BlockSpec(memory_space=pltpu.VMEM)
ANYWHERE = pl.BlockSpec(memory_space=pl.ANY)
SCALARS = pl.BlockSpec(memory_space=pltpu.SMEM)


def params(mebibytes):
    return pltpu.CompilerParams(vmem_limit_bytes=mebibytes * 2**20)


def cost(flops, moved):
    return pl.CostEstimate(flops=flops, bytes_accessed=moved, transcendentals=0)


def halves(x):
    high = x.astype(BF16)
    return high, (x - high.astype(F32)).astype(BF16)


def product(left, right):
    return jnp.dot(left, right, preferred_element_type=F32)


def row_factors(degree_ref, at, width):
    factors = lax.rsqrt(degree_ref[at : at + 1, :].astype(F32))
    return jnp.broadcast_to(factors, (width, factors.shape[1])).T


def scale_kernel(tiles, pairs, *refs):
    count_ref, in_refs, (grad_ref, scaled_ref, row_factor_ref, col_factor_ref, plan_ref) = refs[0], refs[1:6], refs[6:11]
    bufs, sems = refs[11:16], refs[16]
    copies = [pltpu.make_async_copy(*pair, sems.at[at]) for at, pair in enumerate(zip(in_refs, bufs))]
    for copy in copies:
        copy.start()
    for copy in copies:
        copy.wait()
    cotangent, embed, row_degree, col_degree, coords = bufs
    for x_buf, degree_buf, out_ref, factor_ref in (
        (embed, col_degree, scaled_ref, col_factor_ref),
        (cotangent, row_degree, grad_ref, row_factor_ref),
    ):
        tile = degree_buf.shape[1]
        for at in range(degree_buf.shape[0]):
            rows = pl.ds(at * tile, tile)
            factors = row_factors(degree_buf, at, x_buf.shape[1])
            factor_ref[rows, :] = factors
            out_ref[rows, :] = x_buf[rows, :] * factors
    capacity = coords.shape[-1]
    plan_ref[0:1, :] = row_place(coords[0, 0], tiles) * tile
    plan_ref[1:2, :] = col_place(coords[1, 0], tiles, pairs) * tile
    live = lax.broadcasted_iota(jnp.int32, (1, capacity), 1) < count_ref[0, 0]
    plan_ref[2:3, :] = live.astype(jnp.int32)


def finish_kernel(*refs):
    *part_refs, factor_ref, out_ref = refs
    total = part_refs[0][...]
    for part_ref in part_refs[1:]:
        total = total + part_ref[...]
    out_ref[...] = total * factor_ref[...]


def add_kernel(x_ref, y_ref, out_ref):
    out_ref[...] = x_ref[...] + y_ref[...]


def pair_kernel(kept_ref, got_ref, *out_refs):
    for at, out_ref in enumerate(out_refs):
        out_ref[...] = kept_ref[at] + got_ref[at]


def stack_kernel(*refs):
    *part_refs, out_ref = refs
    for at, part_ref in enumerate(part_refs):
        out_ref[at] = part_ref[...]


def row_place(tile_at, tiles):
    return tile_at ^ (lax.axis_index("row") * tiles)


def col_place(tile_at, tiles, pairs):
    tile_at = tile_at ^ (lax.axis_index("col") * tiles)
    shard = lax.shift_right_logical(tile_at, tiles.bit_length() - 1)
    return ((shard & 1) * pairs + lax.shift_right_logical(shard, 1)) * tiles + (tile_at & (tiles - 1))


def split_kernel(plan_ref, values_ref, high_ref, low_ref, buf, sems):
    capacity, tile, _ = values_ref.shape
    groups = sems.shape[0]
    group = capacity // groups
    copies = []
    for at in range(groups):
        slots = pl.ds(at * group, group)
        copies.append(pltpu.make_async_copy(values_ref.at[slots], buf.at[slots], sems.at[at]))
        copies[-1].start()
    for at, copy in enumerate(copies):
        copy.wait()

        @pl.loop(at * group, (at + 1) * group, unroll=2)
        def _(slot):
            rows = pl.ds(pl.multiple_of(plan_ref[0, slot], tile), tile)
            cols = pl.ds(pl.multiple_of(plan_ref[1, slot], tile), tile)
            high, low = halves(jnp.where(plan_ref[2, slot] > 0, buf[slot], 0.0))
            high_ref[rows, cols] = high
            low_ref[rows, cols] = low


def flip_kernel(tile, *refs):
    *grad_refs, block_ref, out_ref, copy_ref = refs
    copy_ref[...] = block_ref[...]
    shard, width = grad_refs[0].shape
    for at, grad_ref in enumerate(grad_refs):
        for first in range(0, shard, tile):
            high, low = halves(grad_ref[pl.ds(first, tile), :].T)
            cols = pl.ds(at * shard + first, tile)
            out_ref[:width, cols] = high
            out_ref[width:, cols] = low


def backward_kernel(first, tile, grads_ref, high_ref, low_ref, out_ref):
    count, shard, width = out_ref.shape
    for at in range(count):
        cols = pl.ds((first + at) * shard, shard)
        both = product(grads_ref[...], high_ref[:, cols])
        total = both[:width] + both[width:] + product(grads_ref[:width, :], low_ref[:, cols])
        for row in range(0, shard, tile):
            out_ref[at, pl.ds(row, tile), :] = total[:, row : row + tile].T


def forward_kernel(first, bands, embeds_ref, high_ref, low_ref, *refs):
    before_refs, out_refs, panel = refs[: -1 - bands], refs[-1 - bands : -1], refs[-1]
    count, shard, width = embeds_ref.shape
    for at in range(count):
        high, low = halves(embeds_ref[at])
        panel[pl.ds(at * shard, shard), :width] = high
        panel[pl.ds(at * shard, shard), width:] = low
    cols = pl.ds(first * shard, count * shard)
    for at, out_ref in enumerate(out_refs):
        rows = pl.ds(at * shard, shard)
        both = product(high_ref[rows, cols], panel[...])
        total = both[:, :width] + both[:, width:] + product(low_ref[rows, cols], panel[:, :width])
        if before_refs:
            total = total + before_refs[at][...]
        out_ref[...] = total


def slots_kernel(tiles, pairs, coords_ref, count_ref, values_ref, embed_ref, grad_ref, forward_ref, backward_ref):
    group, tile, _ = values_ref.shape
    first = pl.program_id(0) * group

    @pl.when(pl.program_id(0) == 0)
    def _():
        forward_ref[...] = jnp.zeros_like(forward_ref)
        backward_ref[...] = jnp.zeros_like(backward_ref)

    for slot in range(group):

        @pl.when(first + slot < count_ref[0, 0])
        def _():
            row_at = row_place(coords_ref[0, 0, 0, first + slot], tiles)
            col_at = col_place(coords_ref[1, 0, 0, first + slot], tiles, pairs)
            rows = pl.ds(pl.multiple_of(row_at * tile, tile), tile)
            cols = pl.ds(pl.multiple_of(col_at * tile, tile), tile)
            high, low = halves(values_ref[slot])
            embed_high, embed_low = halves(embed_ref[cols, :])
            forward_ref[rows, :] += product(high, embed_high) + product(high, embed_low) + product(low, embed_high)
            high, low = halves(values_ref[slot].T)
            grad_high, grad_low = halves(grad_ref[rows, :])
            backward_ref[cols, :] += product(high, grad_high) + product(high, grad_low) + product(low, grad_high)


def swap(x, axis, mask):
    return lax.ppermute(x, axis, [(at, at ^ mask) for at in range(lax.axis_size(axis))])


def call(kernel, out_shape, args, mebibytes=16, flops=0, scratch=(), specs=None, after=None):
    outs = out_shape if isinstance(out_shape, tuple) else (out_shape,)
    moved = sum(x.size * x.dtype.itemsize for x in (*args, *outs))
    specs = specs or [WHOLE] * len(args)
    body = kernel
    if after is not None:
        args, specs = (after, *args), [ANYWHERE, *specs]

        def body(_, *refs):
            kernel(*refs)

    return pl.pallas_call(
        body,
        out_shape=out_shape,
        in_specs=specs,
        out_specs=tuple(WHOLE for _ in outs) if isinstance(out_shape, tuple) else WHOLE,
        scratch_shapes=scratch,
        compiler_params=params(mebibytes),
        cost_estimate=cost(20 * flops, 20 * moved),
    )(*args)


def per_device(embed, cotangent, tile_values, tile_coords, tile_count, row_degree, col_degree):
    shard, width = embed.shape
    capacity, tile = tile_values.shape[2:4]
    n_row, n_col = lax.axis_size("row"), lax.axis_size("col")
    pairs = n_col // 2
    tiles = shard // tile
    n_rows, n_cols = shard * n_row, shard * n_col
    values = tile_values.reshape(tile_values.shape[2:])
    block = jax.ShapeDtypeStruct((shard, width), F32)

    def blocks(count):
        return jax.ShapeDtypeStruct((count, shard, width), F32)

    with jax.named_scope("scale"):
        args = (cotangent, embed, row_degree.reshape(-1, tile), col_degree.reshape(-1, tile), tile_coords)
        grad_scaled, scaled, row_factor, col_factor, plan = call(
            functools.partial(scale_kernel, tiles, pairs),
            (block,) * 4 + (jax.ShapeDtypeStruct((3, capacity), jnp.int32),),
            (tile_count, *(pltpu.with_memory_space_constraint(x, pltpu.HBM) for x in args)),
            mebibytes=4,
            specs=[SCALARS] + [pl.BlockSpec(memory_space=pltpu.HBM)] * len(args),
            scratch=[pltpu.VMEM(x.shape, x.dtype) for x in args] + [pltpu.SemaphoreType.DMA((len(args),))],
        )

    far = pairs // 2
    with jax.named_scope("gather"):
        crossed = swap(scaled, "col", 2 * far)
        grads = [grad_scaled] + [swap(grad_scaled, "row", k) for k in range(1, n_row)]
    dense = (n_rows // tile) * (n_cols // tile) <= capacity
    if dense:
        table = jax.ShapeDtypeStruct((n_rows, n_cols), BF16)
        groups = math.gcd(capacity, 8)
        with jax.named_scope("split"):
            high, low = call(
                split_kernel,
                (table, table),
                (plan, pltpu.with_memory_space_constraint(values, pltpu.HBM)),
                mebibytes=32,
                specs=[SCALARS, pl.BlockSpec(memory_space=pltpu.HBM)],
                scratch=[pltpu.VMEM(values.shape, F32), pltpu.SemaphoreType.DMA((groups,))],
            )
        with jax.named_scope("flip"):
            flipped, crossed = call(
                functools.partial(flip_kernel, tile),
                (jax.ShapeDtypeStruct((2 * width, n_rows), BF16), block),
                (*grads, crossed),
                after=low,
            )
    with jax.named_scope("gather"):
        own = {0: scaled, far: crossed}
        mask = far // 2
        while mask:
            own.update({at | mask: swap(x, "col", 2 * mask) for at, x in own.items()})
            mask //= 2
        own = [own[at] for at in range(pairs)]

    def stacked(after):
        return call(stack_kernel, blocks(pairs), own, after=after)

    def reduced(parts, after):
        mask, got = 1, []
        while mask < pairs:
            for at in reversed(range(0, pairs, 2 * mask)):
                arrived = swap(parts.pop(at + mask), "col", 2 * mask)
                if at:
                    after = parts[at] = call(add_kernel, block, (parts[at], arrived), after=after)
                else:
                    got.append(arrived)
            mask *= 2
        return parts[0], got, after

    def paired(kept, sent):
        return call(pair_kernel, (block,) * kept.shape[0], (kept, swap(sent, "col", 1)))

    if dense:

        def backward_part(first, count, after):
            return call(
                functools.partial(backward_kernel, first, tile),
                blocks(count),
                (flipped, high, low),
                mebibytes=24,
                after=after,
                flops=6 * n_rows * count * shard * width,
            )

        def forward_half(embeds, first, before=(), after=None):
            return call(
                functools.partial(forward_kernel, first, n_row),
                (block,) * n_row,
                (embeds, high, low, *before),
                mebibytes=24,
                flops=3 * n_rows * n_cols * width,
                scratch=[pltpu.VMEM((pairs * shard, 2 * width), BF16)],
                after=after,
            )

        with jax.named_scope("backward"):
            parts = {}
            after = plan
            for first, count in ((far, pairs - far), (0, far)):
                sent = backward_part(pairs + first, count, after)
                kept = backward_part(first, count, sent)
                added = paired(kept, sent)
                parts.update({first + at: x for at, x in enumerate(added)})
                after = added[0]
        with jax.named_scope("gather"):
            own = stacked(after)
            other = swap(own, "col", 1)
        with jax.named_scope("forward"):
            forwards = forward_half(own, 0)
        with jax.named_scope("reduce"):
            *parts, after = reduced(parts, forwards[0])
        with jax.named_scope("forward"):
            forwards = forward_half(other, pairs, forwards, after)
    else:
        group = 8
        with jax.named_scope("gather"):
            own = stacked(plan)
            other = swap(own, "col", 1)
        with jax.named_scope("slots"):
            forward, backward = pl.pallas_call(
                functools.partial(slots_kernel, tiles, pairs),
                out_shape=(
                    jax.ShapeDtypeStruct((n_rows, width), F32),
                    jax.ShapeDtypeStruct((n_cols, width), F32),
                ),
                grid=(capacity // group,),
                in_specs=[SCALARS, SCALARS, pl.BlockSpec((group, tile, tile), lambda at: (at, 0, 0)), WHOLE, WHOLE],
                out_specs=(WHOLE, WHOLE),
                compiler_params=params(40),
                cost_estimate=cost(12 * values.size * width, values.size * 4),
            )(tile_coords, tile_count, values, jnp.concatenate([own, other]).reshape(-1, width), jnp.concatenate(grads))
            forwards = list(forward.reshape(n_row, shard, width))
            *parts, _ = reduced(dict(enumerate(paired(*backward.reshape(2, pairs, shard, width)))), forward)

    with jax.named_scope("reduce"):
        row_parts = [forwards[0]] + [swap(forwards[k], "row", k) for k in range(1, n_row)]

    with jax.named_scope("finish"):
        propagated = call(finish_kernel, block, (*row_parts, row_factor), mebibytes=4)
        embed_grad = call(finish_kernel, block, (parts[0], *parts[1], col_factor), mebibytes=4)
    return propagated, embed_grad


def solution(mesh):
    return jax.shard_map(
        per_device,
        mesh=mesh,
        in_specs=(
            P(("row", "col"), None),
            P(("col", "row"), None),
            P("col", "row", None, None, None),
            P(None, "col", "row", None),
            P("col", "row"),
            P(("col", "row")),
            P(("row", "col")),
        ),
        out_specs=(P(("col", "row"), None), P(("row", "col"), None)),
        check_vma=False,
    )
```

```python
import functools

import jax
import jax.numpy as jnp
from jax import lax
from jax.experimental import pallas as pl
from jax.experimental.pallas import tpu as pltpu
from jax.sharding import PartitionSpec as P

F32 = jnp.float32
BF16 = jnp.bfloat16
WHOLE = pl.BlockSpec(memory_space=pltpu.VMEM)
ANYWHERE = pl.BlockSpec(memory_space=pl.ANY)
SCALARS = pl.BlockSpec(memory_space=pltpu.SMEM)


def params(mebibytes):
    return pltpu.CompilerParams(vmem_limit_bytes=mebibytes * 2**20)


def cost(flops, moved):
    return pl.CostEstimate(flops=flops, bytes_accessed=moved, transcendentals=0)


def halves(x):
    high = x.astype(BF16)
    return high, (x - high.astype(F32)).astype(BF16)


def product(left, right):
    return jnp.dot(left, right, preferred_element_type=F32)


def row_factors(degree_ref, at, width):
    factors = lax.rsqrt(degree_ref[at : at + 1, :].astype(F32))
    return jnp.broadcast_to(factors, (width, factors.shape[1])).T


def scale_kernel(tiles, n_row, pairs, *refs):
    in_refs, (grad_ref, scaled_ref, row_factor_ref, col_factor_ref, plan_ref) = refs[:5], refs[5:10]
    bufs, sems = refs[10:15], refs[15]
    copies = [pltpu.make_async_copy(*pair, sems.at[at]) for at, pair in enumerate(zip(in_refs, bufs))]
    for copy in copies:
        copy.start()
    for copy in copies:
        copy.wait()
    cotangent, embed, row_degree, col_degree, coords = bufs
    for x_buf, degree_buf, out_ref, factor_ref in (
        (embed, col_degree, scaled_ref, col_factor_ref),
        (cotangent, row_degree, grad_ref, row_factor_ref),
    ):
        tile = degree_buf.shape[1]
        for at in range(degree_buf.shape[0]):
            rows = pl.ds(at * tile, tile)
            factors = row_factors(degree_buf, at, x_buf.shape[1])
            factor_ref[rows, :] = factors
            out_ref[0, rows, :] = x_buf[rows, :] * factors
    plan_ref[0:1, :] = row_place(coords[0, 0], tiles, n_row) * tile
    plan_ref[1:2, :] = col_place(coords[1, 0], tiles, pairs) * tile


def finish_kernel(*refs):
    *part_refs, factor_ref, out_ref = refs
    total = part_refs[0][0]
    for part_ref in part_refs[1:]:
        total = total + part_ref[0]
    out_ref[...] = total * factor_ref[...]


def add_kernel(x_ref, y_ref, *out_refs):
    count = out_refs[0].shape[0]
    for at, out_ref in enumerate(out_refs):
        part = pl.ds(at * count, count)
        out_ref[...] = x_ref[part] + y_ref[part]


def copy_kernel(x_ref, out_ref):
    out_ref[...] = x_ref[...]


def join_kernel(x_ref, y_ref, out_ref):
    count = x_ref.shape[0]
    out_ref[:count] = x_ref[...]
    out_ref[count:] = y_ref[...]


def bits_of(count):
    return count.bit_length() - 1


def reversed_bits(x, bits):
    out = jnp.zeros_like(x)
    for bit in range(bits):
        out = out | ((lax.shift_right_logical(x, bit) & 1) << (bits - 1 - bit))
    return out


def row_place(tile_at, tiles, n_row):
    tile_at = tile_at ^ (lax.axis_index("row") * tiles)
    shard = lax.shift_right_logical(tile_at, bits_of(tiles))
    order = jnp.where(lax.axis_index("col") % 2 == 0, reversed_bits(shard, bits_of(n_row)), shard)
    return order * tiles + (tile_at & (tiles - 1))


def col_place(tile_at, tiles, pairs):
    tile_at = tile_at ^ (lax.axis_index("col") * tiles)
    shard = lax.shift_right_logical(tile_at, bits_of(tiles))
    order = reversed_bits(lax.shift_right_logical(shard, 1), bits_of(pairs))
    half = pairs // 2
    second = (order >= half).astype(jnp.int32)
    order = second * pairs + (shard & 1) * half + (order & (half - 1))
    return order * tiles + (tile_at & (tiles - 1))


def split_kernel(plan_ref, count_ref, values_ref, high_ref, low_ref):
    capacity, tile, _ = values_ref.shape

    @pl.loop(0, capacity, unroll=4)
    def _(slot):
        rows = pl.ds(pl.multiple_of(plan_ref[0, slot], tile), tile)
        cols = pl.ds(pl.multiple_of(plan_ref[1, slot], tile), tile)
        high, low = halves(jnp.where(slot < count_ref[0, 0], values_ref[slot], 0.0))
        high_ref[rows, cols] = high
        low_ref[rows, cols] = low


def flip_kernel(tile, *refs):
    *grad_refs, out_ref = refs
    _, shard, width = grad_refs[0].shape
    done = 0
    for grad_ref in grad_refs:
        for at in range(grad_ref.shape[0]):
            for first in range(0, shard, tile):
                high, low = halves(grad_ref[at, pl.ds(first, tile), :].T)
                out_ref[:width, pl.ds(done + first, tile)] = high
                out_ref[width:, pl.ds(done + first, tile)] = low
            done += shard


def backward_kernel(firsts, tile, grads_ref, high_ref, low_ref, out_ref):
    _, shard, width = out_ref.shape
    for at, first in enumerate(firsts):
        cols = pl.ds(first * shard, shard)
        both = product(grads_ref[...], high_ref[:, cols])
        total = both[:width] + both[width:] + product(grads_ref[:width, :], low_ref[:, cols])
        for row in range(0, shard, tile):
            out_ref[at, pl.ds(row, tile), :] = total[:, row : row + tile].T


def forward_kernel(first, count, *refs):
    embed_refs, (high_ref, low_ref) = refs[:count], refs[count : count + 2]
    before_refs, out_refs, panel = refs[count + 2 : -3], refs[-3:-1], refs[-1]
    bands, shard, width = out_refs[0].shape
    done = 0
    for embeds_ref in embed_refs:
        for at in range(embeds_ref.shape[0]):
            high, low = halves(embeds_ref[at])
            panel[pl.ds(done, shard), :width] = high
            panel[pl.ds(done, shard), width:] = low
            done += shard
    cols = pl.ds(first * shard, done)
    for part, out_ref in enumerate(out_refs):
        for at in range(bands):
            rows = pl.ds((part * bands + at) * shard, shard)
            both = product(high_ref[rows, cols], panel[...])
            total = both[:, :width] + both[:, width:] + product(low_ref[rows, cols], panel[:, :width])
            if before_refs:
                total = total + before_refs[part][at]
            out_ref[at] = total


def slots_kernel(tiles, n_row, pairs, coords_ref, count_ref, values_ref, embed_ref, grad_ref, forward_ref, backward_ref):
    group, tile, _ = values_ref.shape
    first = pl.program_id(0) * group

    @pl.when(pl.program_id(0) == 0)
    def _():
        forward_ref[...] = jnp.zeros_like(forward_ref)
        backward_ref[...] = jnp.zeros_like(backward_ref)

    for slot in range(group):

        @pl.when(first + slot < count_ref[0, 0])
        def _():
            row_at = row_place(coords_ref[0, 0, 0, first + slot], tiles, n_row)
            col_at = col_place(coords_ref[1, 0, 0, first + slot], tiles, pairs)
            rows = pl.ds(pl.multiple_of(row_at * tile, tile), tile)
            cols = pl.ds(pl.multiple_of(col_at * tile, tile), tile)
            high, low = halves(values_ref[slot])
            embed_high, embed_low = halves(embed_ref[cols, :])
            forward_ref[rows, :] += product(high, embed_high) + product(high, embed_low) + product(low, embed_high)
            high, low = halves(values_ref[slot].T)
            grad_high, grad_low = halves(grad_ref[rows, :])
            backward_ref[cols, :] += product(high, grad_high) + product(high, grad_low) + product(low, grad_high)


def swap(x, axis, mask):
    return lax.ppermute(x, axis, [(at, at ^ mask) for at in range(lax.axis_size(axis))])


def call(kernel, out_shape, args, mebibytes=16, flops=0, scratch=(), specs=None, after=None):
    outs = out_shape if isinstance(out_shape, tuple) else (out_shape,)
    moved = sum(x.size * x.dtype.itemsize for x in (*args, *outs))
    specs = specs or [WHOLE] * len(args)
    body = kernel
    if after is not None:
        args, specs = (after, *args), [ANYWHERE, *specs]

        def body(_, *refs):
            kernel(*refs)

    return pl.pallas_call(
        body,
        out_shape=out_shape,
        in_specs=specs,
        out_specs=tuple(WHOLE for _ in outs) if isinstance(out_shape, tuple) else WHOLE,
        scratch_shapes=scratch,
        compiler_params=params(mebibytes),
        cost_estimate=cost(20 * flops, 20 * moved),
    )(*args)


def per_device(embed, cotangent, tile_values, tile_coords, tile_count, row_degree, col_degree):
    shard, width = embed.shape
    capacity, tile = tile_values.shape[2:4]
    n_row, n_col = lax.axis_size("row"), lax.axis_size("col")
    pairs = n_col // 2
    half = pairs // 2
    tiles = shard // tile
    n_rows, n_cols = shard * n_row, shard * n_col
    dense = (n_rows // tile) * (n_cols // tile) <= capacity
    block = jax.ShapeDtypeStruct((shard, width), F32)

    def blocks(count):
        return jax.ShapeDtypeStruct((count, shard, width), F32)

    def joined(x, y, after=None):
        flops = n_rows * n_cols * width
        return call(join_kernel, blocks(x.shape[0] + y.shape[0]), (x, y), after=after, flops=flops)

    values = tile_values.reshape(tile_values.shape[2:])
    if dense:
        with jax.named_scope("fetch"):
            values = swap(values, "col", 0)

    with jax.named_scope("scale"):
        args = (cotangent, embed, row_degree.reshape(-1, tile), col_degree.reshape(-1, tile), tile_coords)
        grad_scaled, scaled, row_factor, col_factor, plan = call(
            functools.partial(scale_kernel, tiles, n_row, pairs),
            (blocks(1), blocks(1), block, block, jax.ShapeDtypeStruct((2, capacity), jnp.int32)),
            [pltpu.with_memory_space_constraint(x, pltpu.HBM) for x in args],
            mebibytes=4,
            specs=[pl.BlockSpec(memory_space=pltpu.HBM)] * len(args),
            scratch=[pltpu.VMEM(x.shape, x.dtype) for x in args] + [pltpu.SemaphoreType.DMA((len(args),))],
        )

    def cross(x, mask, mirrored):
        masks = (mask, mirrored)
        at = [(row, col) for row in range(n_row) for col in range(n_col)]
        return lax.ppermute(
            x, ("row", "col"), [(row * n_col + col, (row ^ masks[col % 2]) * n_col + col) for row, col in at]
        )

    def row_steps():
        return [(1 << bit, n_row >> (bit + 1)) for bit in range(bits_of(n_row))]

    crossed = swap(scaled, "col", 2 * half)

    def gathered_grads(after):
        grads = [grad_scaled]
        for step, masks in enumerate(reversed(row_steps())):
            if step:
                grads = [joined(*grads, after=after)]
            grads.append(cross(grads[0], *masks))
        return grads

    def gathered_embeds(after):
        own, got, mask = scaled, crossed, half
        while mask > 1:
            own, mask = joined(own, got, after), mask // 2
            got = swap(own, "col", 2 * mask)
        return own, got

    def chip_sums(kept, sent, after=None):
        count = kept.shape[0] // 2
        return call(add_kernel, (blocks(count), blocks(count)), (kept, swap(sent, "col", 1)), after=after)

    def halved(kept, sent, after):
        mask = 1
        while kept.shape[0] > 1:
            count = kept.shape[0] // 2
            kept, sent = call(
                add_kernel, (blocks(count), blocks(count)), (kept, swap(sent, "col", 2 * mask)), after=after
            )
            mask *= 2
        return kept, swap(sent, "col", 2 * mask)

    def reduced_rows(kept, sent, after):
        for step, masks in enumerate(row_steps()):
            got = cross(sent, *masks)
            if kept.shape[0] == 1:
                return kept, got
            count = kept.shape[0] // 2
            kept, sent = call(add_kernel, (blocks(count), blocks(count)), (kept, got), after=after)

    far, near = range(1, pairs, 2), range(0, pairs, 2)
    if dense:
        table = jax.ShapeDtypeStruct((n_rows, n_cols), BF16)
        with jax.named_scope("split"):
            high, low = call(
                split_kernel,
                (table, table),
                (plan, tile_count, values),
                mebibytes=24,
                specs=[SCALARS, SCALARS, WHOLE],
            )
        with jax.named_scope("gather"):
            grads = gathered_grads(high)
            embeds, last_embeds = gathered_embeds(grads[0])
            other_embeds = swap(embeds, "col", 1)
        with jax.named_scope("flip"):
            flipped = call(
                functools.partial(flip_kernel, tile),
                jax.ShapeDtypeStruct((2 * width, n_rows), BF16),
                grads,
                after=embeds,
            )

        def backward_part(orders, core, after):
            shards = [order // half * pairs + core * half + order % half for order in orders]
            return call(
                functools.partial(backward_kernel, shards, tile),
                blocks(len(shards)),
                (flipped, high, low),
                mebibytes=24,
                after=after,
                flops=6 * n_rows * len(shards) * shard * width,
            )

        def forward_part(embeds, first, before=(), after=None):
            count = sum(x.shape[0] for x in embeds)
            return call(
                functools.partial(forward_kernel, first, len(embeds)),
                (blocks(n_row // 2), blocks(n_row // 2)),
                (*embeds, high, low, *before),
                mebibytes=24,
                flops=6 * n_rows * count * shard * width,
                scratch=[pltpu.VMEM((count * shard, 2 * width), BF16)],
                after=after,
            )

        with jax.named_scope("backward"):
            sent = backward_part(far, 1, plan)
            far_sums = chip_sums(backward_part(far, 0, sent), sent)
            sent = backward_part(near, 1, far_sums[0])
            kept = backward_part(near, 0, sent)
        with jax.named_scope("forward"):
            passed = call(copy_kernel, blocks(half), [last_embeds], after=kept)
            forwards = forward_part([embeds, other_embeds], 0, after=passed)
        with jax.named_scope("reduce"):
            crossing = call(add_kernel, (blocks(1),), halved(*far_sums, passed), after=forwards[0])[0]
        with jax.named_scope("forward"):
            forwards = forward_part([passed, swap(passed, "col", 1)], pairs, forwards, after=crossing)
        with jax.named_scope("reduce"):
            near_sums = chip_sums(kept, sent, after=forwards[0])
            after = near_sums[0]
    else:
        group = 8
        with jax.named_scope("gather"):
            grads = gathered_grads(plan)
            embeds, last_embeds = gathered_embeds(plan)
            panel = joined(joined(embeds, swap(embeds, "col", 1)), joined(last_embeds, swap(last_embeds, "col", 1)))
        with jax.named_scope("slots"):
            forward, backward = pl.pallas_call(
                functools.partial(slots_kernel, tiles, n_row, pairs),
                out_shape=(
                    jax.ShapeDtypeStruct((n_rows, width), F32),
                    jax.ShapeDtypeStruct((n_cols, width), F32),
                ),
                grid=(capacity // group,),
                in_specs=[SCALARS, SCALARS, pl.BlockSpec((group, tile, tile), lambda at: (at, 0, 0)), WHOLE, WHOLE],
                out_specs=(WHOLE, WHOLE),
                compiler_params=params(40),
                cost_estimate=cost(12 * values.size * width, values.size * 4),
            )(tile_coords, tile_count, values, panel.reshape(-1, width), joined(*grads).reshape(-1, width))
            forwards = forward.reshape(2, n_row // 2, shard, width)
            backward = backward.reshape(2, 2, half, shard, width)
            kept, sent = (backward[:, at].reshape(pairs, shard, width) for at in range(2))
        with jax.named_scope("reduce"):
            far_sums, near_sums = (chip_sums(kept[at::2], sent[at::2]) for at in (1, 0))
            crossing = call(add_kernel, (blocks(1),), halved(*far_sums, forward))[0]
            after = forward

    with jax.named_scope("reduce"):
        grad_parts = (*halved(*near_sums, after), swap(crossing, "col", 2 * half))
        row_parts = reduced_rows(*forwards, after)

    with jax.named_scope("finish"):
        propagated = call(finish_kernel, block, (*row_parts, row_factor), mebibytes=4)
        embed_grad = call(finish_kernel, block, (*grad_parts, col_factor), mebibytes=4)
    return propagated, embed_grad


def solution(mesh):
    return jax.shard_map(
        per_device,
        mesh=mesh,
        in_specs=(
            P(("row", "col"), None),
            P(("col", "row"), None),
            P("col", "row", None, None, None),
            P(None, "col", "row", None),
            P("col", "row"),
            P(("col", "row")),
            P(("row", "col")),
        ),
        out_specs=(P(("col", "row"), None), P(("row", "col"), None)),
        check_vma=False,
    )
```

```python
import functools
import math

import jax
import jax.numpy as jnp
from jax import lax
from jax.experimental import pallas as pl
from jax.experimental.pallas import tpu as pltpu
from jax.sharding import PartitionSpec as P

F32 = jnp.float32
BF16 = jnp.bfloat16
WHOLE = pl.BlockSpec(memory_space=pltpu.VMEM)
ANYWHERE = pl.BlockSpec(memory_space=pl.ANY)
SCALARS = pl.BlockSpec(memory_space=pltpu.SMEM)


def params(mebibytes):
    return pltpu.CompilerParams(vmem_limit_bytes=mebibytes * 2**20)


def cost(flops, moved):
    return pl.CostEstimate(flops=flops, bytes_accessed=moved, transcendentals=0)


def halves(x):
    high = x.astype(BF16)
    return high, (x - high.astype(F32)).astype(BF16)


def product(left, right):
    return jnp.dot(left, right, preferred_element_type=F32)


def row_factors(degree_ref, at, width):
    factors = lax.rsqrt(degree_ref[at : at + 1, :].astype(F32))
    return jnp.broadcast_to(factors, (width, factors.shape[1])).T


def scale_kernel(tiles, pairs, *refs):
    in_refs, (grad_ref, scaled_ref, row_factor_ref, col_factor_ref, plan_ref) = refs[:5], refs[5:10]
    bufs, sems = refs[10:15], refs[15]
    copies = [pltpu.make_async_copy(*pair, sems.at[at]) for at, pair in enumerate(zip(in_refs, bufs))]
    for copy in copies:
        copy.start()
    for copy in copies:
        copy.wait()
    cotangent, embed, row_degree, col_degree, coords = bufs
    for x_buf, degree_buf, out_ref, factor_ref in (
        (embed, col_degree, scaled_ref, col_factor_ref),
        (cotangent, row_degree, grad_ref, row_factor_ref),
    ):
        tile = degree_buf.shape[1]
        for at in range(degree_buf.shape[0]):
            rows = pl.ds(at * tile, tile)
            factors = row_factors(degree_buf, at, x_buf.shape[1])
            factor_ref[rows, :] = factors
            out_ref[rows, :] = x_buf[rows, :] * factors
    plan_ref[0:1, :] = row_place(coords[0, 0], tiles) * tile
    plan_ref[1:2, :] = col_place(coords[1, 0], tiles, pairs) * tile


def finish_kernel(*refs):
    *part_refs, factor_ref, out_ref, token_ref = refs
    token_ref[...] = jnp.zeros_like(token_ref)
    total = part_refs[0][...]
    for part_ref in part_refs[1:]:
        total = total + part_ref[...]
    out_ref[...] = total * factor_ref[...]


def add_kernel(x_ref, y_ref, out_ref):
    out_ref[...] = x_ref[...] + y_ref[...]


def pair_kernel(kept_ref, got_ref, *out_refs):
    for at, out_ref in enumerate(out_refs):
        out_ref[...] = kept_ref[at] + got_ref[at]


def stack_kernel(*refs):
    *part_refs, out_ref, last_ref = refs
    for at, part_ref in enumerate(part_refs):
        out_ref[at] = part_ref[...]
    last_ref[...] = part_refs[-1][...]


def copy_kernel(*refs):
    *part_refs, out_ref = refs
    for at, part_ref in enumerate(part_refs):
        out_ref[at] = part_ref[...]


def row_place(tile_at, tiles):
    return tile_at ^ (lax.axis_index("row") * tiles)


def col_shard(distance, core, pairs):
    early = pairs // 2 + 1
    late = 2 * early + core * (pairs - early) + distance - early
    return jnp.where(distance < early, core * early + distance, late)


def col_place(tile_at, tiles, pairs):
    tile_at = tile_at ^ (lax.axis_index("col") * tiles)
    shard = lax.shift_right_logical(tile_at, tiles.bit_length() - 1)
    return col_shard(lax.shift_right_logical(shard, 1), shard & 1, pairs) * tiles + (tile_at & (tiles - 1))


def split_kernel(plan_ref, count_ref, values_ref, high_ref, low_ref, buf, sems):
    capacity, tile, _ = values_ref.shape
    groups = sems.shape[0]
    group = capacity // groups
    together = math.gcd(group, 2)
    copies = []
    for at in range(groups):
        slots = pl.ds(at * group, group)
        copies.append(pltpu.make_async_copy(values_ref.at[slots], buf.at[slots], sems.at[at]))
        copies[-1].start()
    for at, copy in enumerate(copies):
        copy.wait()

        @pl.loop(at * group, (at + 1) * group, step=together, unroll=2)
        def _(first):
            parts = []
            for slot in range(together):
                rows = pl.ds(pl.multiple_of(plan_ref[0, first + slot], tile), tile)
                cols = pl.ds(pl.multiple_of(plan_ref[1, first + slot], tile), tile)
                live = first + slot < count_ref[0, 0]
                parts.append((rows, cols, *halves(jnp.where(live, buf[first + slot], 0.0))))
            for rows, cols, high, low in parts:
                high_ref[rows, cols] = high
                low_ref[rows, cols] = low


def flip_kernel(tile, *refs):
    *grad_refs, out_ref = refs
    shard, width = grad_refs[0].shape
    for at, grad_ref in enumerate(grad_refs):
        for first in range(0, shard, tile):
            high, low = halves(grad_ref[pl.ds(first, tile), :].T)
            cols = pl.ds(at * shard + first, tile)
            out_ref[:width, cols] = high
            out_ref[width:, cols] = low


def backward_kernel(firsts, tile, grads_ref, high_ref, low_ref, out_ref):
    _, shard, width = out_ref.shape
    for at, first in enumerate(firsts):
        cols = pl.ds(first * shard, shard)
        both = product(grads_ref[...], high_ref[:, cols])
        total = both[:width] + both[width:] + product(grads_ref[:width, :], low_ref[:, cols])
        for row in range(0, shard, tile):
            out_ref[at, pl.ds(row, tile), :] = total[:, row : row + tile].T


def forward_kernel(first, count, bands, *refs):
    embed_refs, (high_ref, low_ref) = refs[:count], refs[count : count + 2]
    before_refs, out_refs, panel = refs[count + 2 : -1 - bands], refs[-1 - bands : -1], refs[-1]
    _, shard, width = embed_refs[0].shape
    done = 0
    for embeds_ref in embed_refs:
        for at in range(embeds_ref.shape[0]):
            high, low = halves(embeds_ref[at])
            panel[pl.ds(done, shard), :width] = high
            panel[pl.ds(done, shard), width:] = low
            done += shard
    cols = pl.ds(first * shard, done)
    for at, out_ref in enumerate(out_refs):
        rows = pl.ds(at * shard, shard)
        both = product(high_ref[rows, cols], panel[...])
        total = both[:, :width] + both[:, width:] + product(low_ref[rows, cols], panel[:, :width])
        if before_refs:
            total = total + before_refs[at][...]
        out_ref[...] = total


def slots_kernel(tiles, pairs, coords_ref, count_ref, values_ref, embed_ref, grad_ref, forward_ref, backward_ref):
    group, tile, _ = values_ref.shape
    first = pl.program_id(0) * group

    @pl.when(pl.program_id(0) == 0)
    def _():
        forward_ref[...] = jnp.zeros_like(forward_ref)
        backward_ref[...] = jnp.zeros_like(backward_ref)

    for slot in range(group):

        @pl.when(first + slot < count_ref[0, 0])
        def _():
            row_at = row_place(coords_ref[0, 0, 0, first + slot], tiles)
            col_at = col_place(coords_ref[1, 0, 0, first + slot], tiles, pairs)
            rows = pl.ds(pl.multiple_of(row_at * tile, tile), tile)
            cols = pl.ds(pl.multiple_of(col_at * tile, tile), tile)
            high, low = halves(values_ref[slot])
            embed_high, embed_low = halves(embed_ref[cols, :])
            forward_ref[rows, :] += product(high, embed_high) + product(high, embed_low) + product(low, embed_high)
            high, low = halves(values_ref[slot].T)
            grad_high, grad_low = halves(grad_ref[rows, :])
            backward_ref[cols, :] += product(high, grad_high) + product(high, grad_low) + product(low, grad_high)


def swap(x, axis, mask):
    return lax.ppermute(x, axis, [(at, at ^ mask) for at in range(lax.axis_size(axis))])


def call(kernel, out_shape, args, mebibytes=16, scratch=(), specs=None, after=None):
    outs = out_shape if isinstance(out_shape, tuple) else (out_shape,)
    specs = specs or [WHOLE] * len(args)
    body = kernel
    if after is not None:
        args, specs = (after, *args), [ANYWHERE, *specs]

        def body(_, *refs):
            kernel(*refs)

    return pl.pallas_call(
        body,
        out_shape=out_shape,
        in_specs=specs,
        out_specs=tuple(WHOLE for _ in outs) if isinstance(out_shape, tuple) else WHOLE,
        scratch_shapes=scratch,
        compiler_params=params(mebibytes),
        cost_estimate=cost(0, 1024),
    )(*args)


def per_device(embed, cotangent, tile_values, tile_coords, tile_count, row_degree, col_degree):
    shard, width = embed.shape
    capacity, tile = tile_values.shape[2:4]
    n_row, n_col = lax.axis_size("row"), lax.axis_size("col")
    pairs = n_col // 2
    half = pairs // 2
    tiles = shard // tile
    n_rows, n_cols = shard * n_row, shard * n_col
    dense = (n_rows // tile) * (n_cols // tile) <= capacity
    values = tile_values.reshape(tile_values.shape[2:])
    block = jax.ShapeDtypeStruct((shard, width), F32)

    def blocks(count):
        return jax.ShapeDtypeStruct((count, shard, width), F32)

    with jax.named_scope("scale"):
        args = (cotangent, embed, row_degree.reshape(-1, tile), col_degree.reshape(-1, tile), tile_coords)
        grad_scaled, scaled, row_factor, col_factor, plan = call(
            functools.partial(scale_kernel, tiles, pairs),
            (block,) * 4 + (jax.ShapeDtypeStruct((2, capacity), jnp.int32),),
            [pltpu.with_memory_space_constraint(x, pltpu.HBM) for x in args],
            mebibytes=4,
            specs=[pl.BlockSpec(memory_space=pltpu.HBM)] * len(args),
            scratch=[pltpu.VMEM(x.shape, x.dtype) for x in args] + [pltpu.SemaphoreType.DMA((len(args),))],
        )

    with jax.named_scope("gather"):
        crossed = swap(scaled, "col", 2 * half)
        grads = [grad_scaled] + [swap(grad_scaled, "row", k) for k in range(1, n_row)]
        near = {0: scaled}
        mask = half // 2
        while mask:
            near.update({at | mask: swap(x, "col", 2 * mask) for at, x in near.items()})
            mask //= 2

    def gathered(after):
        early, passed = call(
            stack_kernel,
            (blocks(half + 1), block),
            [near[at] for at in range(half)] + [crossed],
            after=after,
        )
        late, mask = {0: passed}, half // 2
        while mask:
            late.update({at | mask: swap(x, "col", 2 * mask) for at, x in late.items()})
            mask //= 2
        return early, [late[at] for at in range(1, half)]

    def chip_sums(kept, sent, after=None):
        return call(
            pair_kernel,
            (block,) * kept.shape[0],
            (kept, swap(sent, "col", 1)),
            after=after,
        )

    def halved(parts, after):
        parts, got, mask = dict(enumerate(parts)), [], 1
        while mask < half:
            for at in reversed(range(0, half, 2 * mask)):
                arrived = swap(parts.pop(at + mask), "col", 2 * mask)
                if at:
                    parts[at] = call(add_kernel, block, (parts[at], arrived), after=after)
                else:
                    got.append(arrived)
            mask *= 2
        return [parts[0], *got]

    def total(parts, after):
        out, *rest = parts
        for part in rest:
            out = call(add_kernel, block, (out, part), after=after)
        return out

    if dense:
        table = jax.ShapeDtypeStruct((n_rows, n_cols), BF16)
        groups = math.gcd(capacity, 8)
        with jax.named_scope("split"):
            high, low = call(
                split_kernel,
                (table, table),
                (plan, tile_count, pltpu.with_memory_space_constraint(values, pltpu.HBM)),
                mebibytes=32,
                specs=[SCALARS, SCALARS, pl.BlockSpec(memory_space=pltpu.HBM)],
                scratch=[pltpu.VMEM(values.shape, F32), pltpu.SemaphoreType.DMA((groups,))],
            )
        with jax.named_scope("gather"):
            early, late = gathered(high)
            other_early = swap(early, "col", 1)
        with jax.named_scope("flip"):
            flipped = call(
                functools.partial(flip_kernel, tile),
                jax.ShapeDtypeStruct((2 * width, n_rows), BF16),
                grads,
                after=early,
            )

        def backward_part(distances, core, after):
            shards = [shard_at(distance, core) for distance in distances]
            return call(
                functools.partial(backward_kernel, shards, tile),
                blocks(len(shards)),
                (flipped, high, low),
                mebibytes=24,
                after=after,
            )

        def shard_at(distance, core):
            count = half + 1
            if distance < count:
                return core * count + distance
            return 2 * count + core * (pairs - count) + distance - count

        def forward_part(embeds, first, before=(), after=None):
            count = sum(x.shape[0] for x in embeds)
            return call(
                functools.partial(forward_kernel, first, len(embeds), n_row),
                (block,) * n_row,
                (*embeds, high, low, *before),
                mebibytes=24,
                scratch=[pltpu.VMEM((count * shard, 2 * width), BF16)],
                after=after,
            )

        with jax.named_scope("backward"):
            far, close = range(half, pairs), range(half)
            far_sent = backward_part(far, 1, plan)
            sent = backward_part(close, 1, far_sent)
            far_sums = chip_sums(backward_part(far, 0, sent), far_sent)
            kept = backward_part(close, 0, far_sums[0])
        with jax.named_scope("gather"):
            late = call(copy_kernel, blocks(half - 1), late, after=kept)
            other_late = swap(late, "col", 1)
        with jax.named_scope("forward"):
            forwards = forward_part([early, other_early], 0, after=late)
        with jax.named_scope("reduce"):
            crossing = total(halved(far_sums, forwards[0]), forwards[0])
        with jax.named_scope("forward"):
            forwards = forward_part([late, other_late], 2 * (half + 1), forwards, crossing)
        with jax.named_scope("reduce"):
            close_sums = chip_sums(kept, sent)
            after = None
    else:
        group = 8
        with jax.named_scope("gather"):
            early, late = gathered(plan)
            late = call(copy_kernel, blocks(half - 1), late)
            panel = jnp.concatenate([early, swap(early, "col", 1), late, swap(late, "col", 1)])
        with jax.named_scope("slots"):
            forward, backward = pl.pallas_call(
                functools.partial(slots_kernel, tiles, pairs),
                out_shape=(
                    jax.ShapeDtypeStruct((n_rows, width), F32),
                    jax.ShapeDtypeStruct((n_cols, width), F32),
                ),
                grid=(capacity // group,),
                in_specs=[SCALARS, SCALARS, pl.BlockSpec((group, tile, tile), lambda at: (at, 0, 0)), WHOLE, WHOLE],
                out_specs=(WHOLE, WHOLE),
                compiler_params=params(40),
                cost_estimate=cost(12 * values.size * width, values.size * 4),
            )(tile_coords, tile_count, values, panel.reshape(-1, width), jnp.concatenate(grads))
            forwards = list(forward.reshape(n_row, shard, width))
            backward = backward.reshape(n_col, shard, width)
            count = half + 1
            kept, sent = (
                jnp.concatenate(
                    [
                        backward[core * count : (core + 1) * count],
                        backward[2 * count + core * (half - 1) : 2 * count + (core + 1) * (half - 1)],
                    ]
                )
                for core in range(2)
            )
        with jax.named_scope("reduce"):
            far_sums, close_sums = (chip_sums(kept[at : at + half], sent[at : at + half]) for at in (half, 0))
            crossing = total(halved(far_sums, forward), forward)
            after = forward

    with jax.named_scope("reduce"):
        mine, *grad_parts = halved(close_sums, after)
        mine = total([mine, swap(crossing, "col", 2 * half)], None)
        row_parts = [forwards[0]] + [swap(forwards[k], "row", k) for k in range(1, n_row)]

    with jax.named_scope("finish"):
        outs = (block, jax.ShapeDtypeStruct((8, tile), F32))
        propagated, token = call(finish_kernel, outs, (*row_parts, row_factor), mebibytes=4, after=mine)
        embed_grad, _ = call(finish_kernel, outs, (mine, *grad_parts, col_factor), mebibytes=4, after=token)
    return propagated, embed_grad


def solution(mesh):
    return jax.shard_map(
        per_device,
        mesh=mesh,
        in_specs=(
            P(("row", "col"), None),
            P(("col", "row"), None),
            P("col", "row", None, None, None),
            P(None, "col", "row", None),
            P("col", "row"),
            P(("col", "row")),
            P(("row", "col")),
        ),
        out_specs=(P(("col", "row"), None), P(("row", "col"), None)),
        check_vma=False,
    )
```

```python
import functools
import math

import jax
import jax.numpy as jnp
from jax import lax
from jax.experimental import pallas as pl
from jax.experimental.pallas import tpu as pltpu
from jax.sharding import PartitionSpec as P

F32 = jnp.float32
BF16 = jnp.bfloat16
WHOLE = pl.BlockSpec(memory_space=pltpu.VMEM)
ANYWHERE = pl.BlockSpec(memory_space=pl.ANY)
SCALARS = pl.BlockSpec(memory_space=pltpu.SMEM)


def params(mebibytes):
    return pltpu.CompilerParams(vmem_limit_bytes=mebibytes * 2**20)


def cost(flops, moved):
    return pl.CostEstimate(flops=flops, bytes_accessed=moved, transcendentals=0)


def halves(x):
    high = x.astype(BF16)
    return high, (x - high.astype(F32)).astype(BF16)


def product(left, right):
    return jnp.dot(left, right, preferred_element_type=F32)


def row_factors(degree_ref, at, width):
    factors = lax.rsqrt(degree_ref[at : at + 1, :].astype(F32))
    return jnp.broadcast_to(factors, (width, factors.shape[1])).T


def scale_kernel(tiles, pairs, *refs):
    in_refs, (grad_ref, scaled_ref, row_factor_ref, col_factor_ref, plan_ref) = refs[:5], refs[5:10]
    bufs, sems = refs[10:15], refs[15]
    copies = [pltpu.make_async_copy(*pair, sems.at[at]) for at, pair in enumerate(zip(in_refs, bufs))]
    for copy in copies:
        copy.start()
    for copy in copies:
        copy.wait()
    cotangent, embed, row_degree, col_degree, coords = bufs
    for x_buf, degree_buf, out_ref, factor_ref in (
        (embed, col_degree, scaled_ref, col_factor_ref),
        (cotangent, row_degree, grad_ref, row_factor_ref),
    ):
        tile = degree_buf.shape[1]
        for at in range(degree_buf.shape[0]):
            rows = pl.ds(at * tile, tile)
            factors = row_factors(degree_buf, at, x_buf.shape[1])
            factor_ref[rows, :] = factors
            out_ref[rows, :] = x_buf[rows, :] * factors
    plan_ref[0:1, :] = row_place(coords[0, 0], tiles) * tile
    plan_ref[1:2, :] = col_place(coords[1, 0], tiles, pairs) * tile


def sum_kernel(*refs):
    *part_refs, out_ref = refs
    total = part_refs[0][...]
    for part_ref in part_refs[1:]:
        total = total + part_ref[...]
    out_ref[...] = total


def finish_kernel(row_ref, row_factor_ref, col_factor_ref, *refs):
    *part_refs, row_out_ref, col_out_ref = refs
    row_out_ref[...] = row_ref[...] * row_factor_ref[...]
    sum_kernel(*part_refs, col_out_ref)
    col_out_ref[...] = col_out_ref[...] * col_factor_ref[...]


def add_kernel(x_ref, y_ref, out_ref):
    out_ref[...] = x_ref[...] + y_ref[...]


def pair_kernel(kept_ref, got_ref, *out_refs):
    for at, out_ref in enumerate(out_refs):
        out_ref[...] = kept_ref[at] + got_ref[at]


def stack_kernel(*refs):
    *part_refs, out_ref, last_ref = refs
    for at, part_ref in enumerate(part_refs):
        out_ref[at] = part_ref[...]
    last_ref[...] = part_refs[-1][...]


def copy_kernel(*refs):
    *part_refs, out_ref = refs
    for at, part_ref in enumerate(part_refs):
        out_ref[at] = part_ref[...]


def row_place(tile_at, tiles):
    return tile_at ^ (lax.axis_index("row") * tiles)


def col_shard(distance, core, pairs):
    early = pairs // 2 + 1
    late = 2 * early + core * (pairs - early) + distance - early
    return jnp.where(distance < early, core * early + distance, late)


def col_place(tile_at, tiles, pairs):
    tile_at = tile_at ^ (lax.axis_index("col") * tiles)
    shard = lax.shift_right_logical(tile_at, tiles.bit_length() - 1)
    return col_shard(lax.shift_right_logical(shard, 1), shard & 1, pairs) * tiles + (tile_at & (tiles - 1))


def split_kernel(plan_ref, count_ref, values_ref, high_ref, low_ref, buf, sems):
    capacity, tile, _ = values_ref.shape
    groups = sems.shape[0]
    group = capacity // groups
    count = count_ref[0, 0]

    def copy(at):
        slots = pl.ds(at * group, group)
        return pltpu.make_async_copy(values_ref.at[slots], buf.at[slots], sems.at[at])

    def store(slot, high, low):
        rows = pl.ds(pl.multiple_of(plan_ref[0, slot], tile), tile)
        cols = pl.ds(pl.multiple_of(plan_ref[1, slot], tile), tile)
        high_ref[rows, cols] = high
        low_ref[rows, cols] = low

    for at in range(groups):

        @pl.when(at * group < count)
        def _():
            copy(at).start()

    @pl.loop(count, capacity)
    def _(slot):
        zeros = jnp.zeros((tile, tile), BF16)
        store(slot, zeros, zeros)

    for at in range(groups):

        @pl.when(at * group < count)
        def _():
            copy(at).wait()

        @pl.when((at + 1) * group <= count)
        def _():
            @pl.loop(at * group, (at + 1) * group, unroll=4)
            def _(slot):
                store(slot, *halves(buf[slot]))

        @pl.when((at * group < count) & ((at + 1) * group > count))
        def _():
            @pl.loop(at * group, count)
            def _(slot):
                store(slot, *halves(buf[slot]))


def flip_kernel(tile, *refs):
    *grad_refs, out_ref = refs
    shard, width = grad_refs[0].shape
    for at, grad_ref in enumerate(grad_refs):
        for first in range(0, shard, tile):
            high, low = halves(grad_ref[pl.ds(first, tile), :].T)
            cols = pl.ds(at * shard + first, tile)
            out_ref[:width, cols] = high
            out_ref[width:, cols] = low


def backward_kernel(firsts, tile, grads_ref, high_ref, low_ref, out_ref):
    _, shard, width = out_ref.shape
    for at, first in enumerate(firsts):
        cols = pl.ds(first * shard, shard)
        both = product(grads_ref[...], high_ref[:, cols])
        total = both[:width] + both[width:] + product(grads_ref[:width, :], low_ref[:, cols])
        for row in range(0, shard, tile):
            out_ref[at, pl.ds(row, tile), :] = total[:, row : row + tile].T


def forward_kernel(first, count, bands, *refs):
    embed_refs, (high_ref, low_ref) = refs[:count], refs[count : count + 2]
    before_refs, out_refs, panel = refs[count + 2 : -1 - bands], refs[-1 - bands : -1], refs[-1]
    _, shard, width = embed_refs[0].shape
    done = 0
    for embeds_ref in embed_refs:
        for at in range(embeds_ref.shape[0]):
            high, low = halves(embeds_ref[at])
            panel[pl.ds(done, shard), :width] = high
            panel[pl.ds(done, shard), width:] = low
            done += shard
    cols = pl.ds(first * shard, done)
    for at, out_ref in enumerate(out_refs):
        rows = pl.ds(at * shard, shard)
        both = product(high_ref[rows, cols], panel[...])
        total = both[:, :width] + both[:, width:] + product(low_ref[rows, cols], panel[:, :width])
        if before_refs:
            total = total + before_refs[at][...]
        out_ref[...] = total


def slots_kernel(tiles, pairs, coords_ref, count_ref, values_ref, embed_ref, grad_ref, forward_ref, backward_ref):
    group, tile, _ = values_ref.shape
    first = pl.program_id(0) * group

    @pl.when(pl.program_id(0) == 0)
    def _():
        forward_ref[...] = jnp.zeros_like(forward_ref)
        backward_ref[...] = jnp.zeros_like(backward_ref)

    for slot in range(group):

        @pl.when(first + slot < count_ref[0, 0])
        def _():
            row_at = row_place(coords_ref[0, 0, 0, first + slot], tiles)
            col_at = col_place(coords_ref[1, 0, 0, first + slot], tiles, pairs)
            rows = pl.ds(pl.multiple_of(row_at * tile, tile), tile)
            cols = pl.ds(pl.multiple_of(col_at * tile, tile), tile)
            high, low = halves(values_ref[slot])
            embed_high, embed_low = halves(embed_ref[cols, :])
            forward_ref[rows, :] += product(high, embed_high) + product(high, embed_low) + product(low, embed_high)
            high, low = halves(values_ref[slot].T)
            grad_high, grad_low = halves(grad_ref[rows, :])
            backward_ref[cols, :] += product(high, grad_high) + product(high, grad_low) + product(low, grad_high)


def swap(x, axis, mask):
    return lax.ppermute(x, axis, [(at, at ^ mask) for at in range(lax.axis_size(axis))])


def call(kernel, out_shape, args, mebibytes=16, scratch=(), specs=None, after=None):
    outs = out_shape if isinstance(out_shape, tuple) else (out_shape,)
    specs = specs or [WHOLE] * len(args)
    body = kernel
    if after is not None:
        args, specs = (after, *args), [ANYWHERE, *specs]

        def body(_, *refs):
            kernel(*refs)

    return pl.pallas_call(
        body,
        out_shape=out_shape,
        in_specs=specs,
        out_specs=tuple(WHOLE for _ in outs) if isinstance(out_shape, tuple) else WHOLE,
        scratch_shapes=scratch,
        compiler_params=params(mebibytes),
        cost_estimate=cost(0, 1024),
    )(*args)


def per_device(embed, cotangent, tile_values, tile_coords, tile_count, row_degree, col_degree):
    shard, width = embed.shape
    capacity, tile = tile_values.shape[2:4]
    n_row, n_col = lax.axis_size("row"), lax.axis_size("col")
    pairs = n_col // 2
    half = pairs // 2
    tiles = shard // tile
    n_rows, n_cols = shard * n_row, shard * n_col
    dense = (n_rows // tile) * (n_cols // tile) <= capacity
    values = tile_values.reshape(tile_values.shape[2:])
    block = jax.ShapeDtypeStruct((shard, width), F32)

    def blocks(count):
        return jax.ShapeDtypeStruct((count, shard, width), F32)

    with jax.named_scope("scale"):
        args = (cotangent, embed, row_degree.reshape(-1, tile), col_degree.reshape(-1, tile), tile_coords)
        grad_scaled, scaled, row_factor, col_factor, plan = call(
            functools.partial(scale_kernel, tiles, pairs),
            (block,) * 4 + (jax.ShapeDtypeStruct((2, capacity), jnp.int32),),
            [pltpu.with_memory_space_constraint(x, pltpu.HBM) for x in args],
            mebibytes=4,
            specs=[pl.BlockSpec(memory_space=pltpu.HBM)] * len(args),
            scratch=[pltpu.VMEM(x.shape, x.dtype) for x in args] + [pltpu.SemaphoreType.DMA((len(args),))],
        )

    with jax.named_scope("gather"):
        crossed = swap(scaled, "col", 2 * half)
        grads = [grad_scaled] + [swap(grad_scaled, "row", k) for k in range(1, n_row)]
        near = {0: scaled}
        mask = half // 2
        while mask:
            near.update({at | mask: swap(x, "col", 2 * mask) for at, x in near.items()})
            mask //= 2

    def gathered(after):
        early, passed = call(
            stack_kernel,
            (blocks(half + 1), block),
            [near[at] for at in range(half)] + [crossed],
            after=after,
        )
        late, mask = {0: passed}, half // 2
        while mask:
            late.update({at | mask: swap(x, "col", 2 * mask) for at, x in late.items()})
            mask //= 2
        return early, [late[at] for at in range(1, half)]

    def chip_sums(kept, sent, after=None):
        return call(
            pair_kernel,
            (block,) * kept.shape[0],
            (kept, swap(sent, "col", 1)),
            after=after,
        )

    def halved(parts, after):
        parts, got, mask = dict(enumerate(parts)), [], 1
        while mask < half:
            for at in reversed(range(0, half, 2 * mask)):
                arrived = swap(parts.pop(at + mask), "col", 2 * mask)
                if at:
                    parts[at] = call(add_kernel, block, (parts[at], arrived), after=after)
                else:
                    got.append(arrived)
            mask *= 2
        return [parts[0], *got]

    def total(parts, after):
        out, *rest = parts
        for part in rest:
            out = call(add_kernel, block, (out, part), after=after)
        return out

    if dense:
        table = jax.ShapeDtypeStruct((n_rows, n_cols), BF16)
        groups = math.gcd(capacity, 16)
        with jax.named_scope("split"):
            high, low = call(
                split_kernel,
                (table, table),
                (plan, tile_count, pltpu.with_memory_space_constraint(values, pltpu.HBM)),
                mebibytes=32,
                specs=[SCALARS, SCALARS, pl.BlockSpec(memory_space=pltpu.HBM)],
                scratch=[pltpu.VMEM(values.shape, F32), pltpu.SemaphoreType.DMA((groups,))],
            )
        with jax.named_scope("gather"):
            early, late = gathered(high)
            other_early = swap(early, "col", 1)
        with jax.named_scope("flip"):
            flipped = call(
                functools.partial(flip_kernel, tile),
                jax.ShapeDtypeStruct((2 * width, n_rows), BF16),
                grads,
                after=early,
            )

        def backward_part(distances, core, after):
            shards = [shard_at(distance, core) for distance in distances]
            return call(
                functools.partial(backward_kernel, shards, tile),
                blocks(len(shards)),
                (flipped, high, low),
                mebibytes=24,
                after=after,
            )

        def shard_at(distance, core):
            count = half + 1
            if distance < count:
                return core * count + distance
            return 2 * count + core * (pairs - count) + distance - count

        def forward_part(embeds, first, before=(), after=None):
            count = sum(x.shape[0] for x in embeds)
            return call(
                functools.partial(forward_kernel, first, len(embeds), n_row),
                (block,) * n_row,
                (*embeds, high, low, *before),
                mebibytes=24,
                scratch=[pltpu.VMEM((count * shard, 2 * width), BF16)],
                after=after,
            )

        with jax.named_scope("backward"):
            far, close = range(half, pairs), range(half)
            far_sent = backward_part(far, 1, plan)
            sent = backward_part(close, 1, far_sent)
            far_sums = chip_sums(backward_part(far, 0, sent), far_sent)
            kept = backward_part(close, 0, far_sums[0])
        with jax.named_scope("gather"):
            late = call(copy_kernel, blocks(half - 1), late, after=kept)
            other_late = swap(late, "col", 1)
        with jax.named_scope("forward"):
            forwards = forward_part([early, other_early], 0, after=late)
        with jax.named_scope("reduce"):
            crossing = total(halved(far_sums, forwards[0]), forwards[0])
        with jax.named_scope("forward"):
            forwards = forward_part([late, other_late], 2 * (half + 1), forwards, crossing)
        with jax.named_scope("reduce"):
            close_sums = chip_sums(kept, sent)
            after = None
    else:
        group = 8
        with jax.named_scope("gather"):
            early, late = gathered(plan)
            late = call(copy_kernel, blocks(half - 1), late)
            panel = jnp.concatenate([early, swap(early, "col", 1), late, swap(late, "col", 1)])
        with jax.named_scope("slots"):
            forward, backward = pl.pallas_call(
                functools.partial(slots_kernel, tiles, pairs),
                out_shape=(
                    jax.ShapeDtypeStruct((n_rows, width), F32),
                    jax.ShapeDtypeStruct((n_cols, width), F32),
                ),
                grid=(capacity // group,),
                in_specs=[SCALARS, SCALARS, pl.BlockSpec((group, tile, tile), lambda at: (at, 0, 0)), WHOLE, WHOLE],
                out_specs=(WHOLE, WHOLE),
                compiler_params=params(40),
                cost_estimate=cost(12 * values.size * width, values.size * 4),
            )(tile_coords, tile_count, values, panel.reshape(-1, width), jnp.concatenate(grads))
            forwards = list(forward.reshape(n_row, shard, width))
            backward = backward.reshape(n_col, shard, width)
            count = half + 1
            kept, sent = (
                jnp.concatenate(
                    [
                        backward[core * count : (core + 1) * count],
                        backward[2 * count + core * (half - 1) : 2 * count + (core + 1) * (half - 1)],
                    ]
                )
                for core in range(2)
            )
        with jax.named_scope("reduce"):
            far_sums, close_sums = (chip_sums(kept[at : at + half], sent[at : at + half]) for at in (half, 0))
            crossing = total(halved(far_sums, forward), forward)
            after = forward

    with jax.named_scope("reduce"):
        mine, *grad_parts = halved(close_sums, after)
        mine = total([mine, swap(crossing, "col", 2 * half)], None)
        row_parts = [forwards[0]] + [swap(forwards[k], "row", k) for k in range(1, n_row)]

    with jax.named_scope("finish"):
        row_sum = call(sum_kernel, block, row_parts, after=mine)
        return call(
            finish_kernel, (block, block), (row_sum, row_factor, col_factor, mine, *grad_parts), mebibytes=4
        )


def solution(mesh):
    return jax.shard_map(
        per_device,
        mesh=mesh,
        in_specs=(
            P(("row", "col"), None),
            P(("col", "row"), None),
            P("col", "row", None, None, None),
            P(None, "col", "row", None),
            P("col", "row"),
            P(("col", "row")),
            P(("row", "col")),
        ),
        out_specs=(P(("col", "row"), None), P(("row", "col"), None)),
        check_vma=False,
    )
```

```python
import functools
import math

import jax
import jax.numpy as jnp
from jax import lax
from jax.experimental import pallas as pl
from jax.experimental.pallas import tpu as pltpu
from jax.sharding import PartitionSpec as P

F32 = jnp.float32
BF16 = jnp.bfloat16
WHOLE = pl.BlockSpec(memory_space=pltpu.VMEM)
ANYWHERE = pl.BlockSpec(memory_space=pl.ANY)
SCALARS = pl.BlockSpec(memory_space=pltpu.SMEM)


def params(mebibytes):
    return pltpu.CompilerParams(vmem_limit_bytes=mebibytes * 2**20)


def cost(flops, moved):
    return pl.CostEstimate(flops=flops, bytes_accessed=moved, transcendentals=0)


def halves(x):
    high = x.astype(BF16)
    return high, (x - high.astype(F32)).astype(BF16)


def product(left, right):
    return jnp.dot(left, right, preferred_element_type=F32)


def row_factors(degree_ref, at, width):
    factors = lax.rsqrt(degree_ref[at : at + 1, :].astype(F32))
    return jnp.broadcast_to(factors, (width, factors.shape[1])).T


def scale_kernel(tiles, pairs, *refs):
    in_refs, (grad_ref, scaled_ref, row_factor_ref, col_factor_ref, plan_ref) = refs[:5], refs[5:10]
    bufs, sems = refs[10:15], refs[15]
    copies = [pltpu.make_async_copy(*pair, sems.at[at]) for at, pair in enumerate(zip(in_refs, bufs))]
    for copy in copies:
        copy.start()
    for copy in copies:
        copy.wait()
    cotangent, embed, row_degree, col_degree, coords = bufs
    for x_buf, degree_buf, out_ref, factor_ref in (
        (embed, col_degree, scaled_ref, col_factor_ref),
        (cotangent, row_degree, grad_ref, row_factor_ref),
    ):
        tile = degree_buf.shape[1]
        for at in range(degree_buf.shape[0]):
            rows = pl.ds(at * tile, tile)
            factors = row_factors(degree_buf, at, x_buf.shape[1])
            factor_ref[rows, :] = factors
            out_ref[rows, :] = x_buf[rows, :] * factors
    plan_ref[0:1, :] = row_place(coords[0, 0], tiles) * tile
    plan_ref[1:2, :] = col_place(coords[1, 0], tiles, pairs) * tile


def sum_kernel(*refs):
    *part_refs, out_ref = refs
    total = part_refs[0][...]
    for part_ref in part_refs[1:]:
        total = total + part_ref[...]
    out_ref[...] = total


def finish_kernel(row_ref, row_factor_ref, col_factor_ref, *refs):
    *part_refs, row_out_ref, col_out_ref = refs
    row_out_ref[...] = row_ref[...] * row_factor_ref[...]
    sum_kernel(*part_refs, col_out_ref)
    col_out_ref[...] = col_out_ref[...] * col_factor_ref[...]


def add_kernel(x_ref, y_ref, out_ref):
    out_ref[...] = x_ref[...] + y_ref[...]


def pair_kernel(kept_ref, got_ref, *out_refs):
    for at, out_ref in enumerate(out_refs):
        out_ref[...] = kept_ref[at] + got_ref[at]


def stack_kernel(*refs):
    *part_refs, out_ref, last_ref = refs
    for at, part_ref in enumerate(part_refs):
        out_ref[at] = part_ref[...]
    last_ref[...] = part_refs[-1][...]


def pass_kernel(x_ref, out_ref):
    out_ref[...] = x_ref[...]


def copy_kernel(*refs):
    *part_refs, out_ref = refs
    for at, part_ref in enumerate(part_refs):
        out_ref[at] = part_ref[...]


def row_place(tile_at, tiles):
    return tile_at ^ (lax.axis_index("row") * tiles)


def col_shard(distance, core, pairs):
    early = pairs // 2 + 1
    late = 2 * early + core * (pairs - early) + distance - early
    return jnp.where(distance < early, core * early + distance, late)


def col_place(tile_at, tiles, pairs):
    tile_at = tile_at ^ (lax.axis_index("col") * tiles)
    shard = lax.shift_right_logical(tile_at, tiles.bit_length() - 1)
    return col_shard(lax.shift_right_logical(shard, 1), shard & 1, pairs) * tiles + (tile_at & (tiles - 1))


def split_kernel(plan_ref, count_ref, values_ref, high_ref, low_ref, buf, sems):
    capacity, tile, _ = values_ref.shape
    groups = sems.shape[0]
    group = capacity // groups
    count = count_ref[0, 0]

    def copy(at):
        slots = pl.ds(at * group, group)
        return pltpu.make_async_copy(values_ref.at[slots], buf.at[slots], sems.at[at])

    def store(slot, high, low):
        rows = pl.ds(pl.multiple_of(plan_ref[0, slot], tile), tile)
        cols = pl.ds(pl.multiple_of(plan_ref[1, slot], tile), tile)
        high_ref[rows, cols] = high
        low_ref[rows, cols] = low

    for at in range(groups):

        @pl.when(at * group < count)
        def _():
            copy(at).start()

    @pl.loop(count, capacity)
    def _(slot):
        zeros = jnp.zeros((tile, tile), BF16)
        store(slot, zeros, zeros)

    for at in range(groups):

        @pl.when(at * group < count)
        def _():
            copy(at).wait()

        @pl.when((at + 1) * group <= count)
        def _():
            @pl.loop(at * group, (at + 1) * group, unroll=4)
            def _(slot):
                store(slot, *halves(buf[slot]))

        @pl.when((at * group < count) & ((at + 1) * group > count))
        def _():
            @pl.loop(at * group, count)
            def _(slot):
                store(slot, *halves(buf[slot]))


def flip_kernel(tile, *refs):
    *grad_refs, out_ref = refs
    shard, width = grad_refs[0].shape
    for at, grad_ref in enumerate(grad_refs):
        for first in range(0, shard, tile):
            high, low = halves(grad_ref[pl.ds(first, tile), :].T)
            cols = pl.ds(at * shard + first, tile)
            out_ref[:width, cols] = high
            out_ref[width:, cols] = low


def backward_kernel(firsts, tile, grads_ref, high_ref, low_ref, out_ref):
    _, shard, width = out_ref.shape
    for at, first in enumerate(firsts):
        cols = pl.ds(first * shard, shard)
        both = product(grads_ref[...], high_ref[:, cols])
        total = both[:width] + both[width:] + product(grads_ref[:width, :], low_ref[:, cols])
        for row in range(0, shard, tile):
            out_ref[at, pl.ds(row, tile), :] = total[:, row : row + tile].T


def forward_kernel(first, count, bands, *refs):
    embed_refs, (high_ref, low_ref) = refs[:count], refs[count : count + 2]
    before_refs, out_refs, panel = refs[count + 2 : -1 - len(bands)], refs[-1 - len(bands) : -1], refs[-1]
    _, shard, width = embed_refs[0].shape
    done = 0
    for embeds_ref in embed_refs:
        for at in range(embeds_ref.shape[0]):
            high, low = halves(embeds_ref[at])
            panel[pl.ds(done, shard), :width] = high
            panel[pl.ds(done, shard), width:] = low
            done += shard
    cols = pl.ds(first * shard, done)
    for at, (band, out_ref) in enumerate(zip(bands, out_refs)):
        rows = pl.ds(band * shard, shard)
        both = product(high_ref[rows, cols], panel[...])
        total = both[:, :width] + both[:, width:] + product(low_ref[rows, cols], panel[:, :width])
        if before_refs:
            total = total + before_refs[at][...]
        out_ref[...] = total


def slots_kernel(tiles, pairs, coords_ref, count_ref, values_ref, embed_ref, grad_ref, forward_ref, backward_ref):
    group, tile, _ = values_ref.shape
    first = pl.program_id(0) * group

    @pl.when(pl.program_id(0) == 0)
    def _():
        forward_ref[...] = jnp.zeros_like(forward_ref)
        backward_ref[...] = jnp.zeros_like(backward_ref)

    for slot in range(group):

        @pl.when(first + slot < count_ref[0, 0])
        def _():
            row_at = row_place(coords_ref[0, 0, 0, first + slot], tiles)
            col_at = col_place(coords_ref[1, 0, 0, first + slot], tiles, pairs)
            rows = pl.ds(pl.multiple_of(row_at * tile, tile), tile)
            cols = pl.ds(pl.multiple_of(col_at * tile, tile), tile)
            high, low = halves(values_ref[slot])
            embed_high, embed_low = halves(embed_ref[cols, :])
            forward_ref[rows, :] += product(high, embed_high) + product(high, embed_low) + product(low, embed_high)
            high, low = halves(values_ref[slot].T)
            grad_high, grad_low = halves(grad_ref[rows, :])
            backward_ref[cols, :] += product(high, grad_high) + product(high, grad_low) + product(low, grad_high)


def swap(x, axis, mask):
    return lax.ppermute(x, axis, [(at, at ^ mask) for at in range(lax.axis_size(axis))])


def call(kernel, out_shape, args, mebibytes=16, scratch=(), specs=None, after=None):
    outs = out_shape if isinstance(out_shape, tuple) else (out_shape,)
    specs = specs or [WHOLE] * len(args)
    body = kernel
    if after is not None:
        args, specs = (after, *args), [ANYWHERE, *specs]

        def body(_, *refs):
            kernel(*refs)

    return pl.pallas_call(
        body,
        out_shape=out_shape,
        in_specs=specs,
        out_specs=tuple(WHOLE for _ in outs) if isinstance(out_shape, tuple) else WHOLE,
        scratch_shapes=scratch,
        compiler_params=params(mebibytes),
        cost_estimate=cost(0, 1024),
    )(*args)


def per_device(embed, cotangent, tile_values, tile_coords, tile_count, row_degree, col_degree):
    shard, width = embed.shape
    capacity, tile = tile_values.shape[2:4]
    n_row, n_col = lax.axis_size("row"), lax.axis_size("col")
    pairs = n_col // 2
    half = pairs // 2
    tiles = shard // tile
    n_rows, n_cols = shard * n_row, shard * n_col
    dense = (n_rows // tile) * (n_cols // tile) <= capacity
    values = tile_values.reshape(tile_values.shape[2:])
    block = jax.ShapeDtypeStruct((shard, width), F32)

    def blocks(count):
        return jax.ShapeDtypeStruct((count, shard, width), F32)

    with jax.named_scope("scale"):
        args = (cotangent, embed, row_degree.reshape(-1, tile), col_degree.reshape(-1, tile), tile_coords)
        grad_scaled, scaled, row_factor, col_factor, plan = call(
            functools.partial(scale_kernel, tiles, pairs),
            (block,) * 4 + (jax.ShapeDtypeStruct((2, capacity), jnp.int32),),
            [pltpu.with_memory_space_constraint(x, pltpu.HBM) for x in args],
            mebibytes=4,
            specs=[pl.BlockSpec(memory_space=pltpu.HBM)] * len(args),
            scratch=[pltpu.VMEM(x.shape, x.dtype) for x in args] + [pltpu.SemaphoreType.DMA((len(args),))],
        )

    with jax.named_scope("gather"):
        crossed = swap(scaled, "col", 2 * half)
        grads = [grad_scaled] + [swap(grad_scaled, "row", k) for k in range(1, n_row)]
        near = {0: scaled}
        mask = half // 2
        while mask:
            near.update({at | mask: swap(x, "col", 2 * mask) for at, x in near.items()})
            mask //= 2

    def gathered(after):
        early, passed = call(
            stack_kernel,
            (blocks(half + 1), block),
            [near[at] for at in range(half)] + [crossed],
            after=after,
        )
        late, mask = {0: passed}, half // 2
        while mask:
            late.update({at | mask: swap(x, "col", 2 * mask) for at, x in late.items()})
            mask //= 2
        return early, [late[at] for at in range(1, half)]

    def chip_sums(kept, sent, after=None):
        return call(
            pair_kernel,
            (block,) * kept.shape[0],
            (kept, swap(sent, "col", 1)),
            after=after,
        )

    def halved(parts, after):
        parts, got, mask = dict(enumerate(parts)), [], 1
        while mask < half:
            for at in reversed(range(0, half, 2 * mask)):
                arrived = swap(parts.pop(at + mask), "col", 2 * mask)
                if at:
                    parts[at] = call(add_kernel, block, (parts[at], arrived), after=after)
                else:
                    got.append(arrived)
            mask *= 2
        return [parts[0], *got]

    def total(parts, after):
        out, *rest = parts
        for part in rest:
            out = call(add_kernel, block, (out, part), after=after)
        return out

    if dense:
        table = jax.ShapeDtypeStruct((n_rows, n_cols), BF16)
        groups = math.gcd(capacity, 16)
        with jax.named_scope("split"):
            high, low = call(
                split_kernel,
                (table, table),
                (plan, tile_count, pltpu.with_memory_space_constraint(values, pltpu.HBM)),
                mebibytes=32,
                specs=[SCALARS, SCALARS, pl.BlockSpec(memory_space=pltpu.HBM)],
                scratch=[pltpu.VMEM(values.shape, F32), pltpu.SemaphoreType.DMA((groups,))],
            )
        with jax.named_scope("flip"):
            flipped = call(
                functools.partial(flip_kernel, tile),
                jax.ShapeDtypeStruct((2 * width, n_rows), BF16),
                grads,
                after=high,
            )

        def backward_part(distances, core, after):
            shards = [shard_at(distance, core) for distance in distances]
            return call(
                functools.partial(backward_kernel, shards, tile),
                blocks(len(shards)),
                (flipped, high, low),
                mebibytes=24,
                after=after,
            )

        def shard_at(distance, core):
            count = half + 1
            if distance < count:
                return core * count + distance
            return 2 * count + core * (pairs - count) + distance - count

        def forward_part(embeds, first, bands, before=(), after=None):
            count = sum(x.shape[0] for x in embeds)
            return call(
                functools.partial(forward_kernel, first, len(embeds), bands),
                (block,) * len(bands),
                (*embeds, high, low, *before),
                mebibytes=24,
                scratch=[pltpu.VMEM((count * shard, 2 * width), BF16)],
                after=after,
            )

        with jax.named_scope("backward"):
            far, close = range(half, pairs), range(half)
            far_sent = backward_part(far, 1, plan)
            sent = backward_part(close, 1, far_sent)
        with jax.named_scope("gather"):
            early, late = gathered(sent)
            other_early = swap(early, "col", 1)
        with jax.named_scope("backward"):
            far_sums = chip_sums(backward_part(far, 0, early), far_sent)
            kept = backward_part(close, 0, far_sums[0])
        with jax.named_scope("gather"):
            late = call(copy_kernel, blocks(half - 1), late, after=kept)
            other_late = swap(late, "col", 1)
        with jax.named_scope("forward"):
            bands = range(n_row)
            before = forward_part([early, other_early], 0, bands, after=late)
        with jax.named_scope("reduce"):
            *far_parts, arrived = halved(far_sums, before[0])
            arrived = call(pass_kernel, block, [arrived], after=before[0])
        with jax.named_scope("forward"):
            last = forward_part([late, other_late], 2 * (half + 1), bands[-1:], before[-1:], arrived)
        with jax.named_scope("reduce"):
            crossing = total([*far_parts, arrived], last[0])
        with jax.named_scope("forward"):
            forwards = forward_part([late, other_late], 2 * (half + 1), bands[:-1], before[:-1], crossing) + last
        with jax.named_scope("reduce"):
            close_sums = chip_sums(kept, sent)
            after = None
    else:
        group = 8
        with jax.named_scope("gather"):
            early, late = gathered(plan)
            late = call(copy_kernel, blocks(half - 1), late)
            panel = jnp.concatenate([early, swap(early, "col", 1), late, swap(late, "col", 1)])
        with jax.named_scope("slots"):
            forward, backward = pl.pallas_call(
                functools.partial(slots_kernel, tiles, pairs),
                out_shape=(
                    jax.ShapeDtypeStruct((n_rows, width), F32),
                    jax.ShapeDtypeStruct((n_cols, width), F32),
                ),
                grid=(capacity // group,),
                in_specs=[SCALARS, SCALARS, pl.BlockSpec((group, tile, tile), lambda at: (at, 0, 0)), WHOLE, WHOLE],
                out_specs=(WHOLE, WHOLE),
                compiler_params=params(40),
                cost_estimate=cost(12 * values.size * width, values.size * 4),
            )(tile_coords, tile_count, values, panel.reshape(-1, width), jnp.concatenate(grads))
            forwards = list(forward.reshape(n_row, shard, width))
            backward = backward.reshape(n_col, shard, width)
            count = half + 1
            kept, sent = (
                jnp.concatenate(
                    [
                        backward[core * count : (core + 1) * count],
                        backward[2 * count + core * (half - 1) : 2 * count + (core + 1) * (half - 1)],
                    ]
                )
                for core in range(2)
            )
        with jax.named_scope("reduce"):
            far_sums, close_sums = (chip_sums(kept[at : at + half], sent[at : at + half]) for at in (half, 0))
            crossing = total(halved(far_sums, forward), forward)
            after = forward

    with jax.named_scope("reduce"):
        mine, *grad_parts = halved(close_sums, after)
        row_sum = call(add_kernel, block, (forwards[0], swap(forwards[-1], "row", n_row - 1)))
        mine = total([mine, swap(crossing, "col", 2 * half)], row_sum)
        row_parts = [row_sum] + [swap(forwards[k], "row", k) for k in range(1, n_row - 1)]

    with jax.named_scope("finish"):
        row_sum = call(sum_kernel, block, row_parts, after=mine)
        return call(
            finish_kernel, (block, block), (row_sum, row_factor, col_factor, mine, *grad_parts), mebibytes=4
        )


def solution(mesh):
    return jax.shard_map(
        per_device,
        mesh=mesh,
        in_specs=(
            P(("row", "col"), None),
            P(("col", "row"), None),
            P("col", "row", None, None, None),
            P(None, "col", "row", None),
            P("col", "row"),
            P(("col", "row")),
            P(("row", "col")),
        ),
        out_specs=(P(("col", "row"), None), P(("row", "col"), None)),
        check_vma=False,
    )
```

```python
import functools
import math

import jax
import jax.numpy as jnp
from jax import lax
from jax.experimental import pallas as pl
from jax.experimental.pallas import tpu as pltpu
from jax.sharding import PartitionSpec as P

F32 = jnp.float32
BF16 = jnp.bfloat16
WHOLE = pl.BlockSpec(memory_space=pltpu.VMEM)
ANYWHERE = pl.BlockSpec(memory_space=pl.ANY)
SCALARS = pl.BlockSpec(memory_space=pltpu.SMEM)


def params(mebibytes):
    return pltpu.CompilerParams(vmem_limit_bytes=mebibytes * 2**20)


def cost(flops, moved):
    return pl.CostEstimate(flops=flops, bytes_accessed=moved, transcendentals=0)


def halves(x):
    high = x.astype(BF16)
    return high, (x - high.astype(F32)).astype(BF16)


def product(left, right):
    return jnp.dot(left, right, preferred_element_type=F32)


def row_factors(degree_ref, at, width):
    factors = lax.rsqrt(degree_ref[at : at + 1, :].astype(F32))
    return jnp.broadcast_to(factors, (width, factors.shape[1])).T


def scale_kernel(tiles, pairs, *refs):
    in_refs, (grad_ref, scaled_ref, row_factor_ref, col_factor_ref, plan_ref) = refs[:5], refs[5:10]
    bufs, sems = refs[10:15], refs[15]
    copies = [pltpu.make_async_copy(*pair, sems.at[at]) for at, pair in enumerate(zip(in_refs, bufs))]
    for copy in copies:
        copy.start()
    for copy in copies:
        copy.wait()
    cotangent, embed, row_degree, col_degree, coords = bufs
    for x_buf, degree_buf, out_ref, factor_ref in (
        (embed, col_degree, scaled_ref, col_factor_ref),
        (cotangent, row_degree, grad_ref, row_factor_ref),
    ):
        tile = degree_buf.shape[1]
        for at in range(degree_buf.shape[0]):
            rows = pl.ds(at * tile, tile)
            factors = row_factors(degree_buf, at, x_buf.shape[1])
            factor_ref[rows, :] = factors
            out_ref[rows, :] = x_buf[rows, :] * factors
    plan_ref[0:1, :] = row_place(coords[0, 0], tiles) * tile
    plan_ref[1:2, :] = col_place(coords[1, 0], tiles, pairs) * tile


def sum_kernel(*refs):
    *part_refs, out_ref = refs
    total = part_refs[0][...]
    for part_ref in part_refs[1:]:
        total = total + part_ref[...]
    out_ref[...] = total


def finish_kernel(row_ref, row_factor_ref, col_factor_ref, *refs):
    *part_refs, row_out_ref, col_out_ref = refs
    row_out_ref[...] = row_ref[...] * row_factor_ref[...]
    sum_kernel(*part_refs, col_out_ref)
    col_out_ref[...] = col_out_ref[...] * col_factor_ref[...]


def add_kernel(x_ref, y_ref, out_ref):
    out_ref[...] = x_ref[...] + y_ref[...]


def pair_kernel(kept_ref, got_ref, *out_refs):
    for at, out_ref in enumerate(out_refs):
        out_ref[...] = kept_ref[at] + got_ref[at]


def pass_kernel(x_ref, out_ref):
    out_ref[...] = x_ref[...]


def copy_kernel(*refs):
    *part_refs, out_ref = refs
    for at, part_ref in enumerate(part_refs):
        out_ref[at] = part_ref[...]


def row_place(tile_at, tiles):
    return tile_at ^ (lax.axis_index("row") * tiles)


def col_shard(distance, core, pairs):
    early = pairs // 2 + 1
    late = 2 * early + core * (pairs - early) + distance - early
    return jnp.where(distance < early, core * early + distance, late)


def col_place(tile_at, tiles, pairs):
    tile_at = tile_at ^ (lax.axis_index("col") * tiles)
    shard = lax.shift_right_logical(tile_at, tiles.bit_length() - 1)
    return col_shard(lax.shift_right_logical(shard, 1), shard & 1, pairs) * tiles + (tile_at & (tiles - 1))


def split_kernel(plan_ref, count_ref, values_ref, high_ref, low_ref, buf, sems):
    capacity, tile, _ = values_ref.shape
    groups = sems.shape[0]
    group = capacity // groups
    count = count_ref[0, 0]

    def copy(at):
        slots = pl.ds(at * group, group)
        return pltpu.make_async_copy(values_ref.at[slots], buf.at[slots], sems.at[at])

    def store(slot, high, low):
        rows = pl.ds(pl.multiple_of(plan_ref[0, slot], tile), tile)
        cols = pl.ds(pl.multiple_of(plan_ref[1, slot], tile), tile)
        high_ref[rows, cols] = high
        low_ref[rows, cols] = low

    for at in range(groups):

        @pl.when(at * group < count)
        def _():
            copy(at).start()

    @pl.loop(count, capacity)
    def _(slot):
        zeros = jnp.zeros((tile, tile), BF16)
        store(slot, zeros, zeros)

    for at in range(groups):

        @pl.when(at * group < count)
        def _():
            copy(at).wait()

        @pl.when((at + 1) * group <= count)
        def _():
            @pl.loop(at * group, (at + 1) * group, unroll=4)
            def _(slot):
                store(slot, *halves(buf[slot]))

        @pl.when((at * group < count) & ((at + 1) * group > count))
        def _():
            @pl.loop(at * group, count)
            def _(slot):
                store(slot, *halves(buf[slot]))


def flip_kernel(tile, *refs):
    *grad_refs, out_ref = refs
    shard, width = grad_refs[0].shape
    for at, grad_ref in enumerate(grad_refs):
        for first in range(0, shard, tile):
            high, low = halves(grad_ref[pl.ds(first, tile), :].T)
            cols = pl.ds(at * shard + first, tile)
            out_ref[:width, cols] = high
            out_ref[width:, cols] = low


def backward_kernel(firsts, tile, grads_ref, high_ref, low_ref, out_ref):
    _, shard, width = out_ref.shape
    for at, first in enumerate(firsts):
        cols = pl.ds(first * shard, shard)
        both = product(grads_ref[...], high_ref[:, cols])
        total = both[:width] + both[width:] + product(grads_ref[:width, :], low_ref[:, cols])
        for row in range(0, shard, tile):
            out_ref[at, pl.ds(row, tile), :] = total[:, row : row + tile].T


def forward_kernel(first, count, bands, *refs):
    embed_refs, (high_ref, low_ref) = refs[:count], refs[count : count + 2]
    before_refs, out_refs, panel = refs[count + 2 : -1 - bands], refs[-1 - bands : -1], refs[-1]
    _, shard, width = embed_refs[0].shape
    done = 0
    for embeds_ref in embed_refs:
        for at in range(embeds_ref.shape[0]):
            high, low = halves(embeds_ref[at])
            panel[pl.ds(done, shard), :width] = high
            panel[pl.ds(done, shard), width:] = low
            done += shard
    cols = pl.ds(first * shard, done)
    for at, out_ref in enumerate(out_refs):
        rows = pl.ds(at * shard, shard)
        both = product(high_ref[rows, cols], panel[...])
        total = both[:, :width] + both[:, width:] + product(low_ref[rows, cols], panel[:, :width])
        if before_refs:
            total = total + before_refs[at][...]
        out_ref[...] = total


def slots_kernel(tiles, pairs, coords_ref, count_ref, values_ref, embed_ref, grad_ref, forward_ref, backward_ref):
    group, tile, _ = values_ref.shape
    first = pl.program_id(0) * group

    @pl.when(pl.program_id(0) == 0)
    def _():
        forward_ref[...] = jnp.zeros_like(forward_ref)
        backward_ref[...] = jnp.zeros_like(backward_ref)

    for slot in range(group):

        @pl.when(first + slot < count_ref[0, 0])
        def _():
            row_at = row_place(coords_ref[0, 0, 0, first + slot], tiles)
            col_at = col_place(coords_ref[1, 0, 0, first + slot], tiles, pairs)
            rows = pl.ds(pl.multiple_of(row_at * tile, tile), tile)
            cols = pl.ds(pl.multiple_of(col_at * tile, tile), tile)
            high, low = halves(values_ref[slot])
            embed_high, embed_low = halves(embed_ref[cols, :])
            forward_ref[rows, :] += product(high, embed_high) + product(high, embed_low) + product(low, embed_high)
            high, low = halves(values_ref[slot].T)
            grad_high, grad_low = halves(grad_ref[rows, :])
            backward_ref[cols, :] += product(high, grad_high) + product(high, grad_low) + product(low, grad_high)


def swap(x, axis, mask):
    return lax.ppermute(x, axis, [(at, at ^ mask) for at in range(lax.axis_size(axis))])


def call(kernel, out_shape, args, mebibytes=16, flops=0, scratch=(), specs=None, after=None):
    outs = out_shape if isinstance(out_shape, tuple) else (out_shape,)
    specs = specs or [WHOLE] * len(args)
    body = kernel
    if after is not None:
        args, specs = (after, *args), [ANYWHERE, *specs]

        def body(_, *refs):
            kernel(*refs)

    return pl.pallas_call(
        body,
        out_shape=out_shape,
        in_specs=specs,
        out_specs=tuple(WHOLE for _ in outs) if isinstance(out_shape, tuple) else WHOLE,
        scratch_shapes=scratch,
        compiler_params=params(mebibytes),
        cost_estimate=cost(flops, 1024),
    )(*args)


def per_device(embed, cotangent, tile_values, tile_coords, tile_count, row_degree, col_degree):
    shard, width = embed.shape
    capacity, tile = tile_values.shape[2:4]
    n_row, n_col = lax.axis_size("row"), lax.axis_size("col")
    pairs = n_col // 2
    half = pairs // 2
    tiles = shard // tile
    n_rows, n_cols = shard * n_row, shard * n_col
    dense = (n_rows // tile) * (n_cols // tile) <= capacity
    values = tile_values.reshape(tile_values.shape[2:])
    block = jax.ShapeDtypeStruct((shard, width), F32)

    def blocks(count):
        return jax.ShapeDtypeStruct((count, shard, width), F32)

    with jax.named_scope("scale"):
        args = (cotangent, embed, row_degree.reshape(-1, tile), col_degree.reshape(-1, tile), tile_coords)
        grad_scaled, scaled, row_factor, col_factor, plan = call(
            functools.partial(scale_kernel, tiles, pairs),
            (block,) * 4 + (jax.ShapeDtypeStruct((2, capacity), jnp.int32),),
            [pltpu.with_memory_space_constraint(x, pltpu.HBM) for x in args],
            mebibytes=4,
            specs=[pl.BlockSpec(memory_space=pltpu.HBM)] * len(args),
            scratch=[pltpu.VMEM(x.shape, x.dtype) for x in args] + [pltpu.SemaphoreType.DMA((len(args),))],
        )

    with jax.named_scope("gather"):
        crossed = swap(scaled, "col", 2 * half)
        grads = [grad_scaled] + [swap(grad_scaled, "row", k) for k in range(1, n_row)]
        near = {0: scaled}
        mask = half // 2
        while mask:
            near.update({at | mask: swap(x, "col", 2 * mask) for at, x in near.items()})
            mask //= 2

    def gathered(after):
        passed = call(pass_kernel, block, [crossed], after=after)
        early = call(copy_kernel, blocks(half + 1), [near[at] for at in range(half)] + [passed], after=passed)
        late, mask = {0: passed}, half // 2
        while mask:
            late.update({at | mask: swap(x, "col", 2 * mask) for at, x in late.items()})
            mask //= 2
        return early, [late[at] for at in range(1, half)]

    def chip_sums(kept, sent, after=None):
        return call(
            pair_kernel,
            (block,) * kept.shape[0],
            (kept, swap(sent, "col", 1)),
            after=after,
        )

    def halved(parts, after):
        parts, got, mask = dict(enumerate(parts)), [], 1
        while mask < half:
            for at in reversed(range(0, half, 2 * mask)):
                arrived = swap(parts.pop(at + mask), "col", 2 * mask)
                if at:
                    parts[at] = call(add_kernel, block, (parts[at], arrived), after=after)
                else:
                    got.append(arrived)
            mask *= 2
        return [parts[0], *got]

    def total(parts, after):
        out, *rest = parts
        for part in rest:
            out = call(add_kernel, block, (out, part), after=after)
        return out

    if dense:
        table = jax.ShapeDtypeStruct((n_rows, n_cols), BF16)
        groups = math.gcd(capacity, 16)
        with jax.named_scope("split"):
            high, low = call(
                split_kernel,
                (table, table),
                (plan, tile_count, pltpu.with_memory_space_constraint(values, pltpu.HBM)),
                mebibytes=32,
                specs=[SCALARS, SCALARS, pl.BlockSpec(memory_space=pltpu.HBM)],
                scratch=[pltpu.VMEM(values.shape, F32), pltpu.SemaphoreType.DMA((groups,))],
            )
        with jax.named_scope("gather"):
            early, late = gathered(high)
            other_early = swap(early, "col", 1)
        with jax.named_scope("flip"):
            flipped = call(
                functools.partial(flip_kernel, tile),
                jax.ShapeDtypeStruct((2 * width, n_rows), BF16),
                grads,
                after=early,
            )

        def backward_part(distances, core, after):
            shards = [shard_at(distance, core) for distance in distances]
            return call(
                functools.partial(backward_kernel, shards, tile),
                blocks(len(shards)),
                (flipped, high, low),
                mebibytes=24,
                after=after,
            )

        def shard_at(distance, core):
            count = half + 1
            if distance < count:
                return core * count + distance
            return 2 * count + core * (pairs - count) + distance - count

        def forward_part(embeds, first, before=(), after=None, flops=0):
            count = sum(x.shape[0] for x in embeds)
            return call(
                functools.partial(forward_kernel, first, len(embeds), n_row),
                (block,) * n_row,
                (*embeds, high, low, *before),
                mebibytes=24,
                scratch=[pltpu.VMEM((count * shard, 2 * width), BF16)],
                after=after,
                flops=flops,
            )

        with jax.named_scope("backward"):
            far, close = range(half, pairs), range(half)
            far_sent = backward_part(far, 1, plan)
            far_kept = backward_part(far, 0, far_sent)
        with jax.named_scope("gather"):
            late = call(copy_kernel, blocks(half - 1), late, after=far_kept, flops=2 * 10**9)
            other_late = swap(late, "col", 1)
        with jax.named_scope("backward"):
            far_sums = chip_sums(far_kept, far_sent, late)
            sent = backward_part(close, 1, far_sums[0])
            kept = backward_part(close, 0, sent)
        with jax.named_scope("forward"):
            forwards = forward_part([early, other_early], 0, after=kept)
        with jax.named_scope("reduce"):
            crossing = total(halved(far_sums, forwards[0]), forwards[0])
        with jax.named_scope("forward"):
            forwards = forward_part([late, other_late], 2 * (half + 1), forwards, crossing, 2 * 10**9)
        with jax.named_scope("reduce"):
            close_sums = chip_sums(kept, sent, forwards[0])
            after = None
    else:
        group = 8
        with jax.named_scope("gather"):
            early, late = gathered(plan)
            late = call(copy_kernel, blocks(half - 1), late)
            panel = jnp.concatenate([early, swap(early, "col", 1), late, swap(late, "col", 1)])
        with jax.named_scope("slots"):
            forward, backward = pl.pallas_call(
                functools.partial(slots_kernel, tiles, pairs),
                out_shape=(
                    jax.ShapeDtypeStruct((n_rows, width), F32),
                    jax.ShapeDtypeStruct((n_cols, width), F32),
                ),
                grid=(capacity // group,),
                in_specs=[SCALARS, SCALARS, pl.BlockSpec((group, tile, tile), lambda at: (at, 0, 0)), WHOLE, WHOLE],
                out_specs=(WHOLE, WHOLE),
                compiler_params=params(40),
                cost_estimate=cost(12 * values.size * width, values.size * 4),
            )(tile_coords, tile_count, values, panel.reshape(-1, width), jnp.concatenate(grads))
            forwards = list(forward.reshape(n_row, shard, width))
            backward = backward.reshape(n_col, shard, width)
            count = half + 1
            kept, sent = (
                jnp.concatenate(
                    [
                        backward[core * count : (core + 1) * count],
                        backward[2 * count + core * (half - 1) : 2 * count + (core + 1) * (half - 1)],
                    ]
                )
                for core in range(2)
            )
        with jax.named_scope("reduce"):
            far_sums, close_sums = (chip_sums(kept[at : at + half], sent[at : at + half]) for at in (half, 0))
            crossing = total(halved(far_sums, forward), forward)
            after = forward

    with jax.named_scope("reduce"):
        mine, *grad_parts = halved(close_sums, after)
        mine = total([mine, swap(crossing, "col", 2 * half)], None)
        row_parts = [forwards[0]] + [swap(forwards[k], "row", k) for k in range(1, n_row)]

    with jax.named_scope("finish"):
        row_sum = call(sum_kernel, block, [row_parts[0], row_parts[-1]], after=mine)
        row_sum = call(sum_kernel, block, [row_sum, *row_parts[1:-1]])
        return call(
            finish_kernel, (block, block), (row_sum, row_factor, col_factor, mine, *grad_parts), mebibytes=4
        )


def solution(mesh):
    return jax.shard_map(
        per_device,
        mesh=mesh,
        in_specs=(
            P(("row", "col"), None),
            P(("col", "row"), None),
            P("col", "row", None, None, None),
            P(None, "col", "row", None),
            P("col", "row"),
            P(("col", "row")),
            P(("row", "col")),
        ),
        out_specs=(P(("col", "row"), None), P(("row", "col"), None)),
        check_vma=False,
    )
```

```python
import functools
import math

import jax
import jax.numpy as jnp
from jax import lax
from jax.experimental import pallas as pl
from jax.experimental.pallas import tpu as pltpu
from jax.sharding import PartitionSpec as P

F32 = jnp.float32
BF16 = jnp.bfloat16
WHOLE = pl.BlockSpec(memory_space=pltpu.VMEM)
ANYWHERE = pl.BlockSpec(memory_space=pl.ANY)
SCALARS = pl.BlockSpec(memory_space=pltpu.SMEM)


def params(mebibytes):
    return pltpu.CompilerParams(vmem_limit_bytes=mebibytes * 2**20)


def cost(flops, moved):
    return pl.CostEstimate(flops=flops, bytes_accessed=moved, transcendentals=0)


def halves(x):
    high = x.astype(BF16)
    return high, (x - high.astype(F32)).astype(BF16)


def product(left, right):
    return jnp.dot(left, right, preferred_element_type=F32)


def row_factors(degree_ref, at, width):
    factors = lax.rsqrt(degree_ref[at : at + 1, :].astype(F32))
    return jnp.broadcast_to(factors, (width, factors.shape[1])).T


def scale_kernel(tiles, pairs, *refs):
    in_refs, (grad_ref, scaled_ref, row_factor_ref, col_factor_ref, plan_ref) = refs[:5], refs[5:10]
    bufs, sems = refs[10:15], refs[15]
    copies = [pltpu.make_async_copy(*pair, sems.at[at]) for at, pair in enumerate(zip(in_refs, bufs))]
    for copy in copies:
        copy.start()
    for copy in copies:
        copy.wait()
    cotangent, embed, row_degree, col_degree, coords = bufs
    for x_buf, degree_buf, out_ref, factor_ref in (
        (embed, col_degree, scaled_ref, col_factor_ref),
        (cotangent, row_degree, grad_ref, row_factor_ref),
    ):
        tile = degree_buf.shape[1]
        for at in range(degree_buf.shape[0]):
            rows = pl.ds(at * tile, tile)
            factors = row_factors(degree_buf, at, x_buf.shape[1])
            factor_ref[rows, :] = factors
            out_ref[rows, :] = x_buf[rows, :] * factors
    plan_ref[0:1, :] = row_place(coords[0, 0], tiles) * tile
    plan_ref[1:2, :] = col_place(coords[1, 0], tiles, pairs) * tile


def sum_kernel(*refs):
    *part_refs, out_ref = refs
    total = part_refs[0][...]
    for part_ref in part_refs[1:]:
        total = total + part_ref[...]
    out_ref[...] = total


def finish_kernel(row_ref, row_factor_ref, col_factor_ref, *refs):
    *part_refs, row_out_ref, col_out_ref = refs
    row_out_ref[...] = row_ref[...] * row_factor_ref[...]
    sum_kernel(*part_refs, col_out_ref)
    col_out_ref[...] = col_out_ref[...] * col_factor_ref[...]


def add_kernel(x_ref, y_ref, out_ref):
    out_ref[...] = x_ref[...] + y_ref[...]


def pair_kernel(kept_ref, got_ref, *out_refs):
    for at, out_ref in enumerate(out_refs):
        out_ref[...] = kept_ref[at] + got_ref[at]


def pass_kernel(x_ref, out_ref):
    out_ref[...] = x_ref[...]


def copy_kernel(*refs):
    *part_refs, out_ref = refs
    for at, part_ref in enumerate(part_refs):
        out_ref[at] = part_ref[...]


def row_place(tile_at, tiles):
    return tile_at ^ (lax.axis_index("row") * tiles)


def col_shard(distance, core, pairs):
    early = pairs // 2 + 1
    late = 2 * early + core * (pairs - early) + distance - early
    return jnp.where(distance < early, core * early + distance, late)


def col_place(tile_at, tiles, pairs):
    tile_at = tile_at ^ (lax.axis_index("col") * tiles)
    shard = lax.shift_right_logical(tile_at, tiles.bit_length() - 1)
    return col_shard(lax.shift_right_logical(shard, 1), shard & 1, pairs) * tiles + (tile_at & (tiles - 1))


def split_kernel(plan_ref, count_ref, values_ref, high_ref, low_ref, buf, sems):
    capacity, tile, _ = values_ref.shape
    groups = sems.shape[0]
    group = capacity // groups
    count = count_ref[0, 0]

    def copy(at):
        slots = pl.ds(at * group, group)
        return pltpu.make_async_copy(values_ref.at[slots], buf.at[slots], sems.at[at])

    def store(slot, high, low):
        rows = pl.ds(pl.multiple_of(plan_ref[0, slot], tile), tile)
        cols = pl.ds(pl.multiple_of(plan_ref[1, slot], tile), tile)
        high_ref[rows, cols] = high
        low_ref[rows, cols] = low

    for at in range(groups):

        @pl.when(at * group < count)
        def _():
            copy(at).start()

    @pl.loop(count, capacity)
    def _(slot):
        zeros = jnp.zeros((tile, tile), BF16)
        store(slot, zeros, zeros)

    for at in range(groups):

        @pl.when(at * group < count)
        def _():
            copy(at).wait()

        @pl.when((at + 1) * group <= count)
        def _():
            @pl.loop(at * group, (at + 1) * group, unroll=4)
            def _(slot):
                store(slot, *halves(buf[slot]))

        @pl.when((at * group < count) & ((at + 1) * group > count))
        def _():
            @pl.loop(at * group, count)
            def _(slot):
                store(slot, *halves(buf[slot]))


def flip_kernel(tile, *refs):
    *grad_refs, out_ref = refs
    shard, width = grad_refs[0].shape
    for at, grad_ref in enumerate(grad_refs):
        for first in range(0, shard, tile):
            high, low = halves(grad_ref[pl.ds(first, tile), :].T)
            cols = pl.ds(at * shard + first, tile)
            out_ref[:width, cols] = high
            out_ref[width:, cols] = low


def backward_kernel(firsts, tile, grads_ref, high_ref, low_ref, out_ref):
    _, shard, width = out_ref.shape
    for at, first in enumerate(firsts):
        cols = pl.ds(first * shard, shard)
        both = product(grads_ref[...], high_ref[:, cols])
        total = both[:width] + both[width:] + product(grads_ref[:width, :], low_ref[:, cols])
        for row in range(0, shard, tile):
            out_ref[at, pl.ds(row, tile), :] = total[:, row : row + tile].T


def forward_kernel(first, count, bands, *refs):
    embed_refs, (high_ref, low_ref) = refs[:count], refs[count : count + 2]
    before_refs, out_refs, panel = refs[count + 2 : -1 - bands], refs[-1 - bands : -1], refs[-1]
    _, shard, width = embed_refs[0].shape
    done = 0
    for embeds_ref in embed_refs:
        for at in range(embeds_ref.shape[0]):
            high, low = halves(embeds_ref[at])
            panel[pl.ds(done, shard), :width] = high
            panel[pl.ds(done, shard), width:] = low
            done += shard
    cols = pl.ds(first * shard, done)
    for at, out_ref in enumerate(out_refs):
        rows = pl.ds(at * shard, shard)
        both = product(high_ref[rows, cols], panel[...])
        total = both[:, :width] + both[:, width:] + product(low_ref[rows, cols], panel[:, :width])
        if before_refs:
            total = total + before_refs[at][...]
        out_ref[...] = total


def slots_kernel(tiles, pairs, coords_ref, count_ref, values_ref, embed_ref, grad_ref, forward_ref, backward_ref):
    group, tile, _ = values_ref.shape
    first = pl.program_id(0) * group

    @pl.when(pl.program_id(0) == 0)
    def _():
        forward_ref[...] = jnp.zeros_like(forward_ref)
        backward_ref[...] = jnp.zeros_like(backward_ref)

    for slot in range(group):

        @pl.when(first + slot < count_ref[0, 0])
        def _():
            row_at = row_place(coords_ref[0, 0, 0, first + slot], tiles)
            col_at = col_place(coords_ref[1, 0, 0, first + slot], tiles, pairs)
            rows = pl.ds(pl.multiple_of(row_at * tile, tile), tile)
            cols = pl.ds(pl.multiple_of(col_at * tile, tile), tile)
            high, low = halves(values_ref[slot])
            embed_high, embed_low = halves(embed_ref[cols, :])
            forward_ref[rows, :] += product(high, embed_high) + product(high, embed_low) + product(low, embed_high)
            high, low = halves(values_ref[slot].T)
            grad_high, grad_low = halves(grad_ref[rows, :])
            backward_ref[cols, :] += product(high, grad_high) + product(high, grad_low) + product(low, grad_high)


def swap(x, axis, mask):
    return lax.ppermute(x, axis, [(at, at ^ mask) for at in range(lax.axis_size(axis))])


def call(kernel, out_shape, args, mebibytes=16, flops=0, scratch=(), specs=None, after=None):
    outs = out_shape if isinstance(out_shape, tuple) else (out_shape,)
    specs = specs or [WHOLE] * len(args)
    body = kernel
    if after is not None:
        args, specs = (after, *args), [ANYWHERE, *specs]

        def body(_, *refs):
            kernel(*refs)

    return pl.pallas_call(
        body,
        out_shape=out_shape,
        in_specs=specs,
        out_specs=tuple(WHOLE for _ in outs) if isinstance(out_shape, tuple) else WHOLE,
        scratch_shapes=scratch,
        compiler_params=params(mebibytes),
        cost_estimate=cost(flops, 1024),
    )(*args)


def per_device(embed, cotangent, tile_values, tile_coords, tile_count, row_degree, col_degree):
    shard, width = embed.shape
    capacity, tile = tile_values.shape[2:4]
    n_row, n_col = lax.axis_size("row"), lax.axis_size("col")
    pairs = n_col // 2
    half = pairs // 2
    tiles = shard // tile
    n_rows, n_cols = shard * n_row, shard * n_col
    dense = (n_rows // tile) * (n_cols // tile) <= capacity
    values = tile_values.reshape(tile_values.shape[2:])
    block = jax.ShapeDtypeStruct((shard, width), F32)

    def blocks(count):
        return jax.ShapeDtypeStruct((count, shard, width), F32)

    with jax.named_scope("scale"):
        args = (cotangent, embed, row_degree.reshape(-1, tile), col_degree.reshape(-1, tile), tile_coords)
        grad_scaled, scaled, row_factor, col_factor, plan = call(
            functools.partial(scale_kernel, tiles, pairs),
            (block,) * 4 + (jax.ShapeDtypeStruct((2, capacity), jnp.int32),),
            [pltpu.with_memory_space_constraint(x, pltpu.HBM) for x in args],
            mebibytes=4,
            specs=[pl.BlockSpec(memory_space=pltpu.HBM)] * len(args),
            scratch=[pltpu.VMEM(x.shape, x.dtype) for x in args] + [pltpu.SemaphoreType.DMA((len(args),))],
        )

    with jax.named_scope("gather"):
        crossed = swap(scaled, "col", 2 * half)
        grads = [grad_scaled] + [swap(grad_scaled, "row", k) for k in range(1, n_row)]
        near = {0: scaled}
        mask = half // 2
        while mask:
            near.update({at | mask: swap(x, "col", 2 * mask) for at, x in near.items()})
            mask //= 2

    def gathered(after):
        passed = call(pass_kernel, block, [crossed], after=after)
        late, mask = {0: passed}, half // 2
        while mask:
            late.update({at | mask: swap(x, "col", 2 * mask) for at, x in late.items()})
            mask //= 2
        return passed, [late[at] for at in range(1, half)]

    def stacked(passed, after):
        return call(copy_kernel, blocks(half + 1), [near[at] for at in range(half)] + [passed], after=after)

    def chip_sums(kept, sent, after=None):
        return call(
            pair_kernel,
            (block,) * kept.shape[0],
            (kept, swap(sent, "col", 1)),
            after=after,
        )

    def halved(parts, after):
        parts, got, mask = dict(enumerate(parts)), [], 1
        while mask < half:
            for at in reversed(range(0, half, 2 * mask)):
                arrived = swap(parts.pop(at + mask), "col", 2 * mask)
                if at:
                    parts[at] = call(add_kernel, block, (parts[at], arrived), after=after)
                else:
                    got.append(arrived)
            mask *= 2
        return [parts[0], *got]

    def total(parts, after):
        out, *rest = parts
        for part in rest:
            out = call(add_kernel, block, (out, part), after=after)
        return out

    if dense:
        table = jax.ShapeDtypeStruct((n_rows, n_cols), BF16)
        groups = math.gcd(capacity, 16)
        with jax.named_scope("split"):
            high, low = call(
                split_kernel,
                (table, table),
                (plan, tile_count, pltpu.with_memory_space_constraint(values, pltpu.HBM)),
                mebibytes=32,
                specs=[SCALARS, SCALARS, pl.BlockSpec(memory_space=pltpu.HBM)],
                scratch=[pltpu.VMEM(values.shape, F32), pltpu.SemaphoreType.DMA((groups,))],
            )
        with jax.named_scope("gather"):
            passed, late = gathered(high)
        with jax.named_scope("flip"):
            flipped = call(
                functools.partial(flip_kernel, tile),
                jax.ShapeDtypeStruct((2 * width, n_rows), BF16),
                grads,
                after=passed,
            )
        with jax.named_scope("gather"):
            early = stacked(passed, flipped)
            other_early = swap(early, "col", 1)

        def backward_part(distances, core, after):
            shards = [shard_at(distance, core) for distance in distances]
            return call(
                functools.partial(backward_kernel, shards, tile),
                blocks(len(shards)),
                (flipped, high, low),
                mebibytes=24,
                after=after,
            )

        def shard_at(distance, core):
            count = half + 1
            if distance < count:
                return core * count + distance
            return 2 * count + core * (pairs - count) + distance - count

        def forward_part(embeds, first, before=(), after=None, flops=0):
            count = sum(x.shape[0] for x in embeds)
            return call(
                functools.partial(forward_kernel, first, len(embeds), n_row),
                (block,) * n_row,
                (*embeds, high, low, *before),
                mebibytes=24,
                scratch=[pltpu.VMEM((count * shard, 2 * width), BF16)],
                after=after,
                flops=flops,
            )

        with jax.named_scope("backward"):
            far, close = range(half, pairs), range(half)
            far_sent = backward_part(far, 1, early)
            far_kept = backward_part(far, 0, far_sent)
            sent = backward_part(close, 1, far_kept)
        with jax.named_scope("gather"):
            late = call(copy_kernel, blocks(half - 1), late, after=sent, flops=2 * 10**9)
            other_late = swap(late, "col", 1)
        with jax.named_scope("backward"):
            far_sums = chip_sums(far_kept, far_sent, late)
            kept = backward_part(close, 0, far_sums[0])
        with jax.named_scope("forward"):
            forwards = forward_part([early, other_early], 0, after=kept)
        with jax.named_scope("reduce"):
            crossing = total(halved(far_sums, forwards[0]), forwards[0])
        with jax.named_scope("forward"):
            forwards = forward_part([late, other_late], 2 * (half + 1), forwards, crossing, 2 * 10**9)
        with jax.named_scope("reduce"):
            close_sums = chip_sums(kept, sent, forwards[0])
            after = None
    else:
        group = 8
        with jax.named_scope("gather"):
            passed, late = gathered(plan)
            early = stacked(passed, plan)
            late = call(copy_kernel, blocks(half - 1), late)
            panel = jnp.concatenate([early, swap(early, "col", 1), late, swap(late, "col", 1)])
        with jax.named_scope("slots"):
            forward, backward = pl.pallas_call(
                functools.partial(slots_kernel, tiles, pairs),
                out_shape=(
                    jax.ShapeDtypeStruct((n_rows, width), F32),
                    jax.ShapeDtypeStruct((n_cols, width), F32),
                ),
                grid=(capacity // group,),
                in_specs=[SCALARS, SCALARS, pl.BlockSpec((group, tile, tile), lambda at: (at, 0, 0)), WHOLE, WHOLE],
                out_specs=(WHOLE, WHOLE),
                compiler_params=params(40),
                cost_estimate=cost(12 * values.size * width, values.size * 4),
            )(tile_coords, tile_count, values, panel.reshape(-1, width), jnp.concatenate(grads))
            forwards = list(forward.reshape(n_row, shard, width))
            backward = backward.reshape(n_col, shard, width)
            count = half + 1
            kept, sent = (
                jnp.concatenate(
                    [
                        backward[core * count : (core + 1) * count],
                        backward[2 * count + core * (half - 1) : 2 * count + (core + 1) * (half - 1)],
                    ]
                )
                for core in range(2)
            )
        with jax.named_scope("reduce"):
            far_sums, close_sums = (chip_sums(kept[at : at + half], sent[at : at + half]) for at in (half, 0))
            crossing = total(halved(far_sums, forward), forward)
            after = forward

    with jax.named_scope("reduce"):
        mine, *grad_parts = halved(close_sums, after)
        mine = total([mine, swap(crossing, "col", 2 * half)], None)
        row_parts = [forwards[0]] + [swap(forwards[k], "row", k) for k in range(1, n_row)]

    with jax.named_scope("finish"):
        row_sum = call(sum_kernel, block, row_parts, after=mine)
        return call(
            finish_kernel, (block, block), (row_sum, row_factor, col_factor, mine, *grad_parts), mebibytes=4
        )


def solution(mesh):
    return jax.shard_map(
        per_device,
        mesh=mesh,
        in_specs=(
            P(("row", "col"), None),
            P(("col", "row"), None),
            P("col", "row", None, None, None),
            P(None, "col", "row", None),
            P("col", "row"),
            P(("col", "row")),
            P(("row", "col")),
        ),
        out_specs=(P(("col", "row"), None), P(("row", "col"), None)),
        check_vma=False,
    )
```

```python
import functools
import math

import jax
import jax.numpy as jnp
from jax import lax
from jax.experimental import pallas as pl
from jax.experimental.pallas import tpu as pltpu
from jax.sharding import PartitionSpec as P

F32 = jnp.float32
BF16 = jnp.bfloat16
WHOLE = pl.BlockSpec(memory_space=pltpu.VMEM)
ANYWHERE = pl.BlockSpec(memory_space=pl.ANY)
SCALARS = pl.BlockSpec(memory_space=pltpu.SMEM)


def params(mebibytes):
    return pltpu.CompilerParams(vmem_limit_bytes=mebibytes * 2**20)


def cost(flops, moved):
    return pl.CostEstimate(flops=flops, bytes_accessed=moved, transcendentals=0)


def halves(x):
    high = x.astype(BF16)
    return high, (x - high.astype(F32)).astype(BF16)


def product(left, right):
    return jnp.dot(left, right, preferred_element_type=F32)


def row_factors(degree_ref, at, width):
    factors = lax.rsqrt(degree_ref[at : at + 1, :].astype(F32))
    return jnp.broadcast_to(factors, (width, factors.shape[1])).T


def scale_kernel(tiles, pairs, *refs):
    in_refs, (grad_ref, scaled_ref, row_factor_ref, col_factor_ref, plan_ref) = refs[:5], refs[5:10]
    bufs, sems = refs[10:15], refs[15]
    copies = [pltpu.make_async_copy(*pair, sems.at[at]) for at, pair in enumerate(zip(in_refs, bufs))]
    for copy in copies:
        copy.start()
    for copy in copies:
        copy.wait()
    cotangent, embed, row_degree, col_degree, coords = bufs
    for x_buf, degree_buf, out_ref, factor_ref in (
        (embed, col_degree, scaled_ref, col_factor_ref),
        (cotangent, row_degree, grad_ref, row_factor_ref),
    ):
        tile = degree_buf.shape[1]
        for at in range(degree_buf.shape[0]):
            rows = pl.ds(at * tile, tile)
            factors = row_factors(degree_buf, at, x_buf.shape[1])
            factor_ref[rows, :] = factors
            out_ref[rows, :] = x_buf[rows, :] * factors
    plan_ref[0:1, :] = row_place(coords[0, 0], tiles) * tile
    plan_ref[1:2, :] = col_place(coords[1, 0], tiles, pairs) * tile


def sum_kernel(*refs):
    *part_refs, out_ref = refs
    total = part_refs[0][...]
    for part_ref in part_refs[1:]:
        total = total + part_ref[...]
    out_ref[...] = total


def finish_kernel(row_ref, row_factor_ref, col_factor_ref, *refs):
    *part_refs, row_out_ref, col_out_ref = refs
    row_out_ref[...] = row_ref[...] * row_factor_ref[...]
    sum_kernel(*part_refs, col_out_ref)
    col_out_ref[...] = col_out_ref[...] * col_factor_ref[...]


def add_kernel(x_ref, y_ref, out_ref):
    out_ref[...] = x_ref[...] + y_ref[...]


def pair_kernel(kept_ref, got_ref, *out_refs):
    for at, out_ref in enumerate(out_refs):
        out_ref[...] = kept_ref[at] + got_ref[at]


def pass_kernel(x_ref, out_ref):
    out_ref[...] = x_ref[...]


def copy_kernel(*refs):
    *part_refs, out_ref = refs
    for at, part_ref in enumerate(part_refs):
        out_ref[at] = part_ref[...]


def row_place(tile_at, tiles):
    return tile_at ^ (lax.axis_index("row") * tiles)


def col_shard(distance, core, pairs):
    early = pairs // 2 + 1
    late = 2 * early + core * (pairs - early) + distance - early
    return jnp.where(distance < early, core * early + distance, late)


def col_place(tile_at, tiles, pairs):
    tile_at = tile_at ^ (lax.axis_index("col") * tiles)
    shard = lax.shift_right_logical(tile_at, tiles.bit_length() - 1)
    return col_shard(lax.shift_right_logical(shard, 1), shard & 1, pairs) * tiles + (tile_at & (tiles - 1))


def split_kernel(plan_ref, count_ref, values_ref, high_ref, low_ref, buf, sems):
    capacity, tile, _ = values_ref.shape
    groups = sems.shape[0]
    group = capacity // groups
    count = count_ref[0, 0]

    def copy(at):
        slots = pl.ds(at * group, group)
        return pltpu.make_async_copy(values_ref.at[slots], buf.at[slots], sems.at[at])

    def store(slot, high, low):
        rows = pl.ds(pl.multiple_of(plan_ref[0, slot], tile), tile)
        cols = pl.ds(pl.multiple_of(plan_ref[1, slot], tile), tile)
        high_ref[rows, cols] = high
        low_ref[rows, cols] = low

    for at in range(groups):

        @pl.when(at * group < count)
        def _():
            copy(at).start()

    @pl.loop(count, capacity)
    def _(slot):
        zeros = jnp.zeros((tile, tile), BF16)
        store(slot, zeros, zeros)

    for at in range(groups):

        @pl.when(at * group < count)
        def _():
            copy(at).wait()

        @pl.when((at + 1) * group <= count)
        def _():
            @pl.loop(at * group, (at + 1) * group, unroll=4)
            def _(slot):
                store(slot, *halves(buf[slot]))

        @pl.when((at * group < count) & ((at + 1) * group > count))
        def _():
            @pl.loop(at * group, count)
            def _(slot):
                store(slot, *halves(buf[slot]))


def flip_kernel(tile, *refs):
    *grad_refs, out_ref = refs
    shard, width = grad_refs[0].shape
    for at, grad_ref in enumerate(grad_refs):
        for first in range(0, shard, tile):
            high, low = halves(grad_ref[pl.ds(first, tile), :].T)
            cols = pl.ds(at * shard + first, tile)
            out_ref[:width, cols] = high
            out_ref[width:, cols] = low


def backward_kernel(firsts, tile, grads_ref, high_ref, low_ref, out_ref):
    _, shard, width = out_ref.shape
    for at, first in enumerate(firsts):
        cols = pl.ds(first * shard, shard)
        both = product(grads_ref[...], high_ref[:, cols])
        total = both[:width] + both[width:] + product(grads_ref[:width, :], low_ref[:, cols])
        for row in range(0, shard, tile):
            out_ref[at, pl.ds(row, tile), :] = total[:, row : row + tile].T


def forward_kernel(count, *refs):
    embed_refs, (high_ref, low_ref), out_refs, panel = refs[:count], refs[count : count + 2], refs[count + 2 : -1], refs[-1]
    _, shard, width = embed_refs[0].shape
    done = 0
    for embeds_ref in embed_refs:
        for at in range(embeds_ref.shape[0]):
            high, low = halves(embeds_ref[at])
            panel[pl.ds(done, shard), :width] = high
            panel[pl.ds(done, shard), width:] = low
            done += shard
    for at, out_ref in enumerate(out_refs):
        rows = pl.ds(at * shard, shard)
        both = product(high_ref[rows, :], panel[...])
        out_ref[...] = both[:, :width] + both[:, width:] + product(low_ref[rows, :], panel[:, :width])


def slots_kernel(tiles, pairs, coords_ref, count_ref, values_ref, embed_ref, grad_ref, forward_ref, backward_ref):
    group, tile, _ = values_ref.shape
    first = pl.program_id(0) * group

    @pl.when(pl.program_id(0) == 0)
    def _():
        forward_ref[...] = jnp.zeros_like(forward_ref)
        backward_ref[...] = jnp.zeros_like(backward_ref)

    for slot in range(group):

        @pl.when(first + slot < count_ref[0, 0])
        def _():
            row_at = row_place(coords_ref[0, 0, 0, first + slot], tiles)
            col_at = col_place(coords_ref[1, 0, 0, first + slot], tiles, pairs)
            rows = pl.ds(pl.multiple_of(row_at * tile, tile), tile)
            cols = pl.ds(pl.multiple_of(col_at * tile, tile), tile)
            high, low = halves(values_ref[slot])
            embed_high, embed_low = halves(embed_ref[cols, :])
            forward_ref[rows, :] += product(high, embed_high) + product(high, embed_low) + product(low, embed_high)
            high, low = halves(values_ref[slot].T)
            grad_high, grad_low = halves(grad_ref[rows, :])
            backward_ref[cols, :] += product(high, grad_high) + product(high, grad_low) + product(low, grad_high)


def swap(x, axis, mask):
    return lax.ppermute(x, axis, [(at, at ^ mask) for at in range(lax.axis_size(axis))])


def call(kernel, out_shape, args, mebibytes=16, flops=0, scratch=(), specs=None, after=None):
    outs = out_shape if isinstance(out_shape, tuple) else (out_shape,)
    specs = specs or [WHOLE] * len(args)
    body = kernel
    if after is not None:
        args, specs = (after, *args), [ANYWHERE, *specs]

        def body(_, *refs):
            kernel(*refs)

    return pl.pallas_call(
        body,
        out_shape=out_shape,
        in_specs=specs,
        out_specs=tuple(WHOLE for _ in outs) if isinstance(out_shape, tuple) else WHOLE,
        scratch_shapes=scratch,
        compiler_params=params(mebibytes),
        cost_estimate=cost(flops, 1024),
    )(*args)


def per_device(embed, cotangent, tile_values, tile_coords, tile_count, row_degree, col_degree):
    shard, width = embed.shape
    capacity, tile = tile_values.shape[2:4]
    n_row, n_col = lax.axis_size("row"), lax.axis_size("col")
    pairs = n_col // 2
    half = pairs // 2
    tiles = shard // tile
    n_rows, n_cols = shard * n_row, shard * n_col
    dense = (n_rows // tile) * (n_cols // tile) <= capacity
    values = tile_values.reshape(tile_values.shape[2:])
    block = jax.ShapeDtypeStruct((shard, width), F32)

    def blocks(count):
        return jax.ShapeDtypeStruct((count, shard, width), F32)

    with jax.named_scope("scale"):
        args = (cotangent, embed, row_degree.reshape(-1, tile), col_degree.reshape(-1, tile), tile_coords)
        grad_scaled, scaled, row_factor, col_factor, plan = call(
            functools.partial(scale_kernel, tiles, pairs),
            (block,) * 4 + (jax.ShapeDtypeStruct((2, capacity), jnp.int32),),
            [pltpu.with_memory_space_constraint(x, pltpu.HBM) for x in args],
            mebibytes=4,
            specs=[pl.BlockSpec(memory_space=pltpu.HBM)] * len(args),
            scratch=[pltpu.VMEM(x.shape, x.dtype) for x in args] + [pltpu.SemaphoreType.DMA((len(args),))],
        )

    with jax.named_scope("gather"):
        crossed = swap(scaled, "col", 2 * half)
        grads = [grad_scaled] + [swap(grad_scaled, "row", k) for k in range(1, n_row)]
        near = {0: scaled}
        mask = half // 2
        while mask:
            near.update({at | mask: swap(x, "col", 2 * mask) for at, x in near.items()})
            mask //= 2

    def gathered(after):
        passed = call(pass_kernel, block, [crossed], after=after)
        late, mask = {0: passed}, half // 2
        while mask:
            late.update({at | mask: swap(x, "col", 2 * mask) for at, x in late.items()})
            mask //= 2
        return passed, [late[at] for at in range(1, half)]

    def stacked(passed, after):
        return call(copy_kernel, blocks(half + 1), [near[at] for at in range(half)] + [passed], after=after)

    def chip_sums(kept, sent, after=None):
        return call(
            pair_kernel,
            (block,) * kept.shape[0],
            (kept, swap(sent, "col", 1)),
            after=after,
        )

    def halved(parts, after):
        parts, got, mask = dict(enumerate(parts)), [], 1
        while mask < half:
            for at in reversed(range(0, half, 2 * mask)):
                arrived = swap(parts.pop(at + mask), "col", 2 * mask)
                if at:
                    parts[at] = call(add_kernel, block, (parts[at], arrived), after=after)
                else:
                    got.append(arrived)
            mask *= 2
        return [parts[0], *got]

    def total(parts, after, flops=0):
        out, *rest = parts
        for part in rest:
            out = call(add_kernel, block, (out, part), after=after, flops=flops)
        return out

    if dense:
        table = jax.ShapeDtypeStruct((n_rows, n_cols), BF16)
        groups = math.gcd(capacity, 16)
        with jax.named_scope("split"):
            high, low = call(
                split_kernel,
                (table, table),
                (plan, tile_count, pltpu.with_memory_space_constraint(values, pltpu.HBM)),
                mebibytes=32,
                specs=[SCALARS, SCALARS, pl.BlockSpec(memory_space=pltpu.HBM)],
                scratch=[pltpu.VMEM(values.shape, F32), pltpu.SemaphoreType.DMA((groups,))],
            )
        with jax.named_scope("gather"):
            passed, late = gathered(high)
        with jax.named_scope("flip"):
            flipped = call(
                functools.partial(flip_kernel, tile),
                jax.ShapeDtypeStruct((2 * width, n_rows), BF16),
                grads,
                after=passed,
            )
        with jax.named_scope("gather"):
            early = stacked(passed, flipped)
            other_early = swap(early, "col", 1)

        def backward_part(distances, core, after):
            shards = [shard_at(distance, core) for distance in distances]
            return call(
                functools.partial(backward_kernel, shards, tile),
                blocks(len(shards)),
                (flipped, high, low),
                mebibytes=24,
                after=after,
            )

        def shard_at(distance, core):
            count = half + 1
            if distance < count:
                return core * count + distance
            return 2 * count + core * (pairs - count) + distance - count

        def forward(embeds, after):
            return call(
                functools.partial(forward_kernel, len(embeds)),
                (block,) * n_row,
                (*embeds, high, low),
                mebibytes=24,
                scratch=[pltpu.VMEM((n_cols, 2 * width), BF16)],
                after=after,
            )

        with jax.named_scope("backward"):
            far, close = range(half, pairs), range(half)
            far_sent = backward_part(far, 1, early)
            far_kept = backward_part(far, 0, far_sent)
            sent = backward_part(close, 1, far_kept)
        with jax.named_scope("gather"):
            late = call(copy_kernel, blocks(half - 1), late, after=sent, flops=2 * 10**9)
            other_late = swap(late, "col", 1)
        with jax.named_scope("backward"):
            far_sums = chip_sums(far_kept, far_sent, late)
            kept = backward_part(close, 0, far_sums[0])
        with jax.named_scope("forward"):
            forwards = forward([early, other_early, late, other_late], kept)
        with jax.named_scope("reduce"):
            crossing = total(halved(far_sums, forwards[0]), forwards[0], 1 * 10**9)
        with jax.named_scope("reduce"):
            close_sums = chip_sums(kept, sent, forwards[0])
            after = None
    else:
        group = 8
        with jax.named_scope("gather"):
            passed, late = gathered(plan)
            early = stacked(passed, plan)
            late = call(copy_kernel, blocks(half - 1), late)
            panel = jnp.concatenate([early, swap(early, "col", 1), late, swap(late, "col", 1)])
        with jax.named_scope("slots"):
            forward, backward = pl.pallas_call(
                functools.partial(slots_kernel, tiles, pairs),
                out_shape=(
                    jax.ShapeDtypeStruct((n_rows, width), F32),
                    jax.ShapeDtypeStruct((n_cols, width), F32),
                ),
                grid=(capacity // group,),
                in_specs=[SCALARS, SCALARS, pl.BlockSpec((group, tile, tile), lambda at: (at, 0, 0)), WHOLE, WHOLE],
                out_specs=(WHOLE, WHOLE),
                compiler_params=params(40),
                cost_estimate=cost(12 * values.size * width, values.size * 4),
            )(tile_coords, tile_count, values, panel.reshape(-1, width), jnp.concatenate(grads))
            forwards = list(forward.reshape(n_row, shard, width))
            backward = backward.reshape(n_col, shard, width)
            count = half + 1
            kept, sent = (
                jnp.concatenate(
                    [
                        backward[core * count : (core + 1) * count],
                        backward[2 * count + core * (half - 1) : 2 * count + (core + 1) * (half - 1)],
                    ]
                )
                for core in range(2)
            )
        with jax.named_scope("reduce"):
            far_sums, close_sums = (chip_sums(kept[at : at + half], sent[at : at + half]) for at in (half, 0))
            crossing = total(halved(far_sums, forward), forward)
            after = forward

    with jax.named_scope("reduce"):
        mine, *grad_parts = halved(close_sums, after)
        mine = total([mine, swap(crossing, "col", 2 * half)], None)
        row_parts = [forwards[0]] + [swap(forwards[k], "row", k) for k in range(1, n_row)]

    with jax.named_scope("finish"):
        row_sum = call(sum_kernel, block, row_parts, after=mine)
        return call(
            finish_kernel, (block, block), (row_sum, row_factor, col_factor, mine, *grad_parts), mebibytes=4
        )


def solution(mesh):
    return jax.shard_map(
        per_device,
        mesh=mesh,
        in_specs=(
            P(("row", "col"), None),
            P(("col", "row"), None),
            P("col", "row", None, None, None),
            P(None, "col", "row", None),
            P("col", "row"),
            P(("col", "row")),
            P(("row", "col")),
        ),
        out_specs=(P(("col", "row"), None), P(("row", "col"), None)),
        check_vma=False,
    )
```

```python
import functools
import math

import jax
import jax.numpy as jnp
from jax import lax
from jax.experimental import pallas as pl
from jax.experimental.pallas import tpu as pltpu
from jax.sharding import PartitionSpec as P

F32 = jnp.float32
BF16 = jnp.bfloat16
WHOLE = pl.BlockSpec(memory_space=pltpu.VMEM)
ANYWHERE = pl.BlockSpec(memory_space=pl.ANY)
SCALARS = pl.BlockSpec(memory_space=pltpu.SMEM)


def params(mebibytes):
    return pltpu.CompilerParams(vmem_limit_bytes=mebibytes * 2**20)


def cost(flops, moved):
    return pl.CostEstimate(flops=flops, bytes_accessed=moved, transcendentals=0)


def halves(x):
    high = x.astype(BF16)
    return high, (x - high.astype(F32)).astype(BF16)


def product(left, right):
    return jnp.dot(left, right, preferred_element_type=F32)


def row_factors(degree_ref, at, width):
    factors = lax.rsqrt(degree_ref[at : at + 1, :].astype(F32))
    return jnp.broadcast_to(factors, (width, factors.shape[1])).T


def scale_kernel(tiles, pairs, *refs):
    in_refs, (grad_ref, scaled_ref, row_factor_ref, col_factor_ref, plan_ref) = refs[:5], refs[5:10]
    bufs, sems = refs[10:15], refs[15]
    copies = [pltpu.make_async_copy(*pair, sems.at[at]) for at, pair in enumerate(zip(in_refs, bufs))]
    for copy in copies:
        copy.start()
    for copy in copies:
        copy.wait()
    cotangent, embed, row_degree, col_degree, coords = bufs
    for x_buf, degree_buf, out_ref, factor_ref in (
        (embed, col_degree, scaled_ref, col_factor_ref),
        (cotangent, row_degree, grad_ref, row_factor_ref),
    ):
        tile = degree_buf.shape[1]
        for at in range(degree_buf.shape[0]):
            rows = pl.ds(at * tile, tile)
            factors = row_factors(degree_buf, at, x_buf.shape[1])
            factor_ref[rows, :] = factors
            out_ref[rows, :] = x_buf[rows, :] * factors
    plan_ref[0:1, :] = row_place(coords[0, 0], tiles) * tile
    plan_ref[1:2, :] = col_place(coords[1, 0], tiles, pairs) * tile


def sum_kernel(*refs):
    *part_refs, out_ref = refs
    total = part_refs[0][...]
    for part_ref in part_refs[1:]:
        total = total + part_ref[...]
    out_ref[...] = total


def finish_kernel(row_ref, row_factor_ref, col_factor_ref, *refs):
    *part_refs, row_out_ref, col_out_ref = refs
    row_out_ref[...] = row_ref[...] * row_factor_ref[...]
    sum_kernel(*part_refs, col_out_ref)
    col_out_ref[...] = col_out_ref[...] * col_factor_ref[...]


def add_kernel(x_ref, y_ref, out_ref):
    out_ref[...] = x_ref[...] + y_ref[...]


def pair_kernel(kept_ref, got_ref, *out_refs):
    for at, out_ref in enumerate(out_refs):
        out_ref[...] = kept_ref[at] + got_ref[at]


def pass_kernel(x_ref, out_ref):
    out_ref[...] = x_ref[...]


def copy_kernel(*refs):
    *part_refs, out_ref = refs
    for at, part_ref in enumerate(part_refs):
        out_ref[at] = part_ref[...]


def row_place(tile_at, tiles):
    return tile_at ^ (lax.axis_index("row") * tiles)


def col_shard(distance, core, pairs):
    early = pairs // 2 + 1
    late = 2 * early + core * (pairs - early) + distance - early
    return jnp.where(distance < early, core * early + distance, late)


def col_place(tile_at, tiles, pairs):
    tile_at = tile_at ^ (lax.axis_index("col") * tiles)
    shard = lax.shift_right_logical(tile_at, tiles.bit_length() - 1)
    return col_shard(lax.shift_right_logical(shard, 1), shard & 1, pairs) * tiles + (tile_at & (tiles - 1))


def split_kernel(count_ref, plan_ref, values_ref, high_ref, low_ref, buf, places, sems, place_sem):
    capacity, tile, _ = values_ref.shape
    groups = sems.shape[0]
    group = capacity // groups
    count = count_ref[0, 0]
    live_groups = lax.div(count + (group - 1), group)

    def copy(at):
        slots = pl.ds(at * group, group)
        return pltpu.make_async_copy(values_ref.at[slots], buf.at[slots], sems.at[at])

    def store(slot, high, low):
        rows = pl.ds(pl.multiple_of(places[0, slot], tile), tile)
        cols = pl.ds(pl.multiple_of(places[1, slot], tile), tile)
        high_ref[rows, cols] = high
        low_ref[rows, cols] = low

    @pl.loop(0, live_groups)
    def _(at):
        copy(at).start()

    place_copy = pltpu.make_async_copy(plan_ref, places, place_sem)
    place_copy.start()
    place_copy.wait()

    @pl.loop(live_groups * group, capacity, unroll=1)
    def _(slot):
        zeros = jnp.zeros((tile, tile), BF16)
        store(slot, zeros, zeros)

    @pl.loop(0, live_groups)
    def _(at):
        copy(at).wait()

        @pl.loop(0, group, unroll=math.gcd(group, 8))
        def _(step):
            slot = at * group + step
            store(slot, *halves(jnp.where(slot < count, buf[slot], 0.0)))


def flip_kernel(tile, *refs):
    *grad_refs, out_ref = refs
    shard, width = grad_refs[0].shape
    for at, grad_ref in enumerate(grad_refs):
        for first in range(0, shard, tile):
            high, low = halves(grad_ref[pl.ds(first, tile), :].T)
            cols = pl.ds(at * shard + first, tile)
            out_ref[:width, cols] = high
            out_ref[width:, cols] = low


def backward_kernel(firsts, tile, grads_ref, high_ref, low_ref, out_ref):
    _, shard, width = out_ref.shape
    for at, first in enumerate(firsts):
        cols = pl.ds(first * shard, shard)
        both = product(grads_ref[...], high_ref[:, cols])
        total = both[:width] + both[width:] + product(grads_ref[:width, :], low_ref[:, cols])
        for row in range(0, shard, tile):
            out_ref[at, pl.ds(row, tile), :] = total[:, row : row + tile].T


def forward_kernel(first, count, bands, *refs):
    embed_refs, (high_ref, low_ref) = refs[:count], refs[count : count + 2]
    before_refs, out_refs, panel = refs[count + 2 : -1 - bands], refs[-1 - bands : -1], refs[-1]
    _, shard, width = embed_refs[0].shape
    done = 0
    for embeds_ref in embed_refs:
        for at in range(embeds_ref.shape[0]):
            high, low = halves(embeds_ref[at])
            panel[pl.ds(done, shard), :width] = high
            panel[pl.ds(done, shard), width:] = low
            done += shard
    cols = pl.ds(first * shard, done)
    for at, out_ref in enumerate(out_refs):
        rows = pl.ds(at * shard, shard)
        both = product(high_ref[rows, cols], panel[...])
        total = both[:, :width] + both[:, width:] + product(low_ref[rows, cols], panel[:, :width])
        if before_refs:
            total = total + before_refs[at][...]
        out_ref[...] = total


def slots_kernel(tiles, pairs, coords_ref, count_ref, values_ref, embed_ref, grad_ref, forward_ref, backward_ref):
    group, tile, _ = values_ref.shape
    first = pl.program_id(0) * group

    @pl.when(pl.program_id(0) == 0)
    def _():
        forward_ref[...] = jnp.zeros_like(forward_ref)
        backward_ref[...] = jnp.zeros_like(backward_ref)

    for slot in range(group):

        @pl.when(first + slot < count_ref[0, 0])
        def _():
            row_at = row_place(coords_ref[0, 0, 0, first + slot], tiles)
            col_at = col_place(coords_ref[1, 0, 0, first + slot], tiles, pairs)
            rows = pl.ds(pl.multiple_of(row_at * tile, tile), tile)
            cols = pl.ds(pl.multiple_of(col_at * tile, tile), tile)
            high, low = halves(values_ref[slot])
            embed_high, embed_low = halves(embed_ref[cols, :])
            forward_ref[rows, :] += product(high, embed_high) + product(high, embed_low) + product(low, embed_high)
            high, low = halves(values_ref[slot].T)
            grad_high, grad_low = halves(grad_ref[rows, :])
            backward_ref[cols, :] += product(high, grad_high) + product(high, grad_low) + product(low, grad_high)


def swap(x, axis, mask):
    return lax.ppermute(x, axis, [(at, at ^ mask) for at in range(lax.axis_size(axis))])


def call(kernel, out_shape, args, mebibytes=16, flops=0, scratch=(), specs=None, after=None):
    outs = out_shape if isinstance(out_shape, tuple) else (out_shape,)
    specs = specs or [WHOLE] * len(args)
    body = kernel
    if after is not None:
        args, specs = (after, *args), [ANYWHERE, *specs]

        def body(_, *refs):
            kernel(*refs)

    return pl.pallas_call(
        body,
        out_shape=out_shape,
        in_specs=specs,
        out_specs=tuple(WHOLE for _ in outs) if isinstance(out_shape, tuple) else WHOLE,
        scratch_shapes=scratch,
        compiler_params=params(mebibytes),
        cost_estimate=cost(flops, 1024),
    )(*args)


def per_device(embed, cotangent, tile_values, tile_coords, tile_count, row_degree, col_degree):
    shard, width = embed.shape
    capacity, tile = tile_values.shape[2:4]
    n_row, n_col = lax.axis_size("row"), lax.axis_size("col")
    pairs = n_col // 2
    half = pairs // 2
    tiles = shard // tile
    n_rows, n_cols = shard * n_row, shard * n_col
    dense = (n_rows // tile) * (n_cols // tile) <= capacity
    values = tile_values.reshape(tile_values.shape[2:])
    block = jax.ShapeDtypeStruct((shard, width), F32)

    def blocks(count):
        return jax.ShapeDtypeStruct((count, shard, width), F32)

    with jax.named_scope("scale"):
        args = (cotangent, embed, row_degree.reshape(-1, tile), col_degree.reshape(-1, tile), tile_coords)
        grad_scaled, scaled, row_factor, col_factor, plan = call(
            functools.partial(scale_kernel, tiles, pairs),
            (block,) * 4 + (jax.ShapeDtypeStruct((2, capacity), jnp.int32),),
            [pltpu.with_memory_space_constraint(x, pltpu.HBM) for x in args],
            mebibytes=4,
            specs=[pl.BlockSpec(memory_space=pltpu.HBM)] * len(args),
            scratch=[pltpu.VMEM(x.shape, x.dtype) for x in args] + [pltpu.SemaphoreType.DMA((len(args),))],
        )

    with jax.named_scope("gather"):
        crossed = swap(scaled, "col", 2 * half)
        grads = [grad_scaled] + [swap(grad_scaled, "row", k) for k in range(1, n_row)]
        near = {0: scaled}
        mask = half // 2
        while mask:
            near.update({at | mask: swap(x, "col", 2 * mask) for at, x in near.items()})
            mask //= 2

    def gathered(after):
        passed = call(pass_kernel, block, [crossed], after=after)
        late, mask = {0: passed}, half // 2
        while mask:
            late.update({at | mask: swap(x, "col", 2 * mask) for at, x in late.items()})
            mask //= 2
        return passed, [late[at] for at in range(1, half)]

    def stacked(passed, after):
        return call(copy_kernel, blocks(half + 1), [near[at] for at in range(half)] + [passed], after=after)

    def chip_sums(kept, sent, after=None):
        return call(
            pair_kernel,
            (block,) * kept.shape[0],
            (kept, swap(sent, "col", 1)),
            after=after,
        )

    def halved(parts, after):
        parts, got, mask = dict(enumerate(parts)), [], 1
        while mask < half:
            for at in reversed(range(0, half, 2 * mask)):
                arrived = swap(parts.pop(at + mask), "col", 2 * mask)
                if at:
                    parts[at] = call(add_kernel, block, (parts[at], arrived), after=after)
                else:
                    got.append(arrived)
            mask *= 2
        return [parts[0], *got]

    def total(parts, after):
        out, *rest = parts
        for part in rest:
            out = call(add_kernel, block, (out, part), after=after)
        return out

    if dense:
        table = jax.ShapeDtypeStruct((n_rows, n_cols), BF16)
        groups = math.gcd(capacity, 8)
        with jax.named_scope("split"):
            high, low = call(
                split_kernel,
                (table, table),
                (tile_count, plan, pltpu.with_memory_space_constraint(values, pltpu.HBM)),
                mebibytes=32,
                specs=[SCALARS, WHOLE, pl.BlockSpec(memory_space=pltpu.HBM)],
                scratch=[
                    pltpu.VMEM(values.shape, F32),
                    pltpu.SMEM(plan.shape, jnp.int32),
                    pltpu.SemaphoreType.DMA((groups,)),
                    pltpu.SemaphoreType.DMA,
                ],
            )
        with jax.named_scope("gather"):
            passed, late = gathered(high)
        with jax.named_scope("flip"):
            flipped = call(
                functools.partial(flip_kernel, tile),
                jax.ShapeDtypeStruct((2 * width, n_rows), BF16),
                grads,
                after=passed,
            )
        with jax.named_scope("gather"):
            early = stacked(passed, flipped)
            other_early = swap(early, "col", 1)

        def backward_part(distances, core, after):
            shards = [shard_at(distance, core) for distance in distances]
            return call(
                functools.partial(backward_kernel, shards, tile),
                blocks(len(shards)),
                (flipped, high, low),
                mebibytes=24,
                after=after,
            )

        def shard_at(distance, core):
            count = half + 1
            if distance < count:
                return core * count + distance
            return 2 * count + core * (pairs - count) + distance - count

        def forward_part(embeds, first, before=(), after=None, flops=0):
            count = sum(x.shape[0] for x in embeds)
            return call(
                functools.partial(forward_kernel, first, len(embeds), n_row),
                (block,) * n_row,
                (*embeds, high, low, *before),
                mebibytes=24,
                scratch=[pltpu.VMEM((count * shard, 2 * width), BF16)],
                after=after,
                flops=flops,
            )

        with jax.named_scope("backward"):
            far, close = range(half, pairs), range(half)
            far_sent = backward_part(far, 1, early)
            far_kept = backward_part(far, 0, far_sent)
            sent = backward_part(close, 1, far_kept)
        with jax.named_scope("gather"):
            late = call(copy_kernel, blocks(half - 1), late, after=sent, flops=2 * 10**9)
            other_late = swap(late, "col", 1)
        with jax.named_scope("backward"):
            far_sums = chip_sums(far_kept, far_sent, late)
            kept = backward_part(close, 0, far_sums[0])
        with jax.named_scope("forward"):
            forwards = forward_part([early, other_early], 0, after=kept)
        with jax.named_scope("reduce"):
            crossing = total(halved(far_sums, forwards[0]), forwards[0])
        with jax.named_scope("forward"):
            forwards = forward_part([late, other_late], 2 * (half + 1), forwards, crossing, 2 * 10**9)
        with jax.named_scope("reduce"):
            close_sums = chip_sums(kept, sent, forwards[0])
            after = None
    else:
        group = 8
        with jax.named_scope("gather"):
            passed, late = gathered(plan)
            early = stacked(passed, plan)
            late = call(copy_kernel, blocks(half - 1), late)
            panel = jnp.concatenate([early, swap(early, "col", 1), late, swap(late, "col", 1)])
        with jax.named_scope("slots"):
            forward, backward = pl.pallas_call(
                functools.partial(slots_kernel, tiles, pairs),
                out_shape=(
                    jax.ShapeDtypeStruct((n_rows, width), F32),
                    jax.ShapeDtypeStruct((n_cols, width), F32),
                ),
                grid=(capacity // group,),
                in_specs=[SCALARS, SCALARS, pl.BlockSpec((group, tile, tile), lambda at: (at, 0, 0)), WHOLE, WHOLE],
                out_specs=(WHOLE, WHOLE),
                compiler_params=params(40),
                cost_estimate=cost(12 * values.size * width, values.size * 4),
            )(tile_coords, tile_count, values, panel.reshape(-1, width), jnp.concatenate(grads))
            forwards = list(forward.reshape(n_row, shard, width))
            backward = backward.reshape(n_col, shard, width)
            count = half + 1
            kept, sent = (
                jnp.concatenate(
                    [
                        backward[core * count : (core + 1) * count],
                        backward[2 * count + core * (half - 1) : 2 * count + (core + 1) * (half - 1)],
                    ]
                )
                for core in range(2)
            )
        with jax.named_scope("reduce"):
            far_sums, close_sums = (chip_sums(kept[at : at + half], sent[at : at + half]) for at in (half, 0))
            crossing = total(halved(far_sums, forward), forward)
            after = forward

    with jax.named_scope("reduce"):
        mine, *grad_parts = halved(close_sums, after)
        mine = total([mine, swap(crossing, "col", 2 * half)], None)
        row_parts = [forwards[0]] + [swap(forwards[k], "row", k) for k in range(1, n_row)]

    with jax.named_scope("finish"):
        row_sum = call(sum_kernel, block, row_parts, after=mine)
        return call(
            finish_kernel, (block, block), (row_sum, row_factor, col_factor, mine, *grad_parts), mebibytes=4
        )


def solution(mesh):
    return jax.shard_map(
        per_device,
        mesh=mesh,
        in_specs=(
            P(("row", "col"), None),
            P(("col", "row"), None),
            P("col", "row", None, None, None),
            P(None, "col", "row", None),
            P("col", "row"),
            P(("col", "row")),
            P(("row", "col")),
        ),
        out_specs=(P(("col", "row"), None), P(("row", "col"), None)),
        check_vma=False,
    )
```

```python
import functools
import math

import jax
import jax.numpy as jnp
from jax import lax
from jax.experimental import pallas as pl
from jax.experimental.pallas import tpu as pltpu
from jax.sharding import PartitionSpec as P

F32 = jnp.float32
BF16 = jnp.bfloat16
WHOLE = pl.BlockSpec(memory_space=pltpu.VMEM)
ANYWHERE = pl.BlockSpec(memory_space=pl.ANY)
SCALARS = pl.BlockSpec(memory_space=pltpu.SMEM)


def params(mebibytes):
    return pltpu.CompilerParams(vmem_limit_bytes=mebibytes * 2**20)


def cost(flops, moved):
    return pl.CostEstimate(flops=flops, bytes_accessed=moved, transcendentals=0)


def halves(x):
    high = x.astype(BF16)
    return high, (x - high.astype(F32)).astype(BF16)


def product(left, right):
    return jnp.dot(left, right, preferred_element_type=F32)


def row_factors(degree_ref, at, width):
    factors = lax.rsqrt(degree_ref[at : at + 1, :].astype(F32))
    return jnp.broadcast_to(factors, (width, factors.shape[1])).T


def scale_kernel(tiles, pairs, *refs):
    in_refs, (grad_ref, scaled_ref, row_factor_ref, col_factor_ref, plan_ref) = refs[:5], refs[5:10]
    bufs, sems = refs[10:15], refs[15]
    copies = [pltpu.make_async_copy(*pair, sems.at[at]) for at, pair in enumerate(zip(in_refs, bufs))]
    for copy in copies:
        copy.start()
    for copy in copies:
        copy.wait()
    cotangent, embed, row_degree, col_degree, coords = bufs
    for x_buf, degree_buf, out_ref, factor_ref in (
        (embed, col_degree, scaled_ref, col_factor_ref),
        (cotangent, row_degree, grad_ref, row_factor_ref),
    ):
        tile = degree_buf.shape[1]
        for at in range(degree_buf.shape[0]):
            rows = pl.ds(at * tile, tile)
            factors = row_factors(degree_buf, at, x_buf.shape[1])
            factor_ref[rows, :] = factors
            out_ref[rows, :] = x_buf[rows, :] * factors
    plan_ref[0:1, :] = row_place(coords[0, 0], tiles) * tile
    plan_ref[1:2, :] = col_place(coords[1, 0], tiles, pairs) * tile


def sum_kernel(*refs):
    *part_refs, out_ref = refs
    total = part_refs[0][...]
    for part_ref in part_refs[1:]:
        total = total + part_ref[...]
    out_ref[...] = total


def finish_kernel(row_ref, row_factor_ref, col_factor_ref, *refs):
    *part_refs, row_out_ref, col_out_ref = refs
    row_out_ref[...] = row_ref[...] * row_factor_ref[...]
    sum_kernel(*part_refs, col_out_ref)
    col_out_ref[...] = col_out_ref[...] * col_factor_ref[...]


def add_kernel(x_ref, y_ref, out_ref):
    out_ref[...] = x_ref[...] + y_ref[...]


def pair_kernel(kept_ref, got_ref, *out_refs):
    for at, out_ref in enumerate(out_refs):
        out_ref[...] = kept_ref[at] + got_ref[at]


def pass_kernel(x_ref, out_ref):
    out_ref[...] = x_ref[...]


def stack_kernel(*refs):
    *part_refs, last_ref, out_ref = refs
    for at, part_ref in enumerate(part_refs):
        out_ref[pl.ds(2 * at, 2)] = part_ref[...]
    out_ref[2 * len(part_refs)] = last_ref[...]


def panel_kernel(own_ref, beside_ref, crossed_ref, mine_ref, theirs_ref, own_out_ref, other_out_ref):
    half = own_out_ref.shape[0] - 1
    own_out_ref[0] = own_ref[...]
    other_out_ref[0] = beside_ref[...]
    own_out_ref[half] = crossed_ref[...]
    other_out_ref[half] = theirs_ref[2 * half - 2]
    core = lax.axis_index("col") % 2
    for at in range(1, half):
        first = 2 * at - 2

        @pl.when(core == 1)
        def _():
            own_out_ref[at] = mine_ref[first]
            other_out_ref[at] = mine_ref[first + 1]

        @pl.when(core == 0)
        def _():
            own_out_ref[at] = theirs_ref[first + 1]
            other_out_ref[at] = theirs_ref[first]


def copy_kernel(*refs):
    *part_refs, out_ref = refs
    for at, part_ref in enumerate(part_refs):
        out_ref[at] = part_ref[...]


def row_place(tile_at, tiles):
    return tile_at ^ (lax.axis_index("row") * tiles)


def col_shard(distance, core, pairs):
    early = pairs // 2 + 1
    late = 2 * early + core * (pairs - early) + distance - early
    return jnp.where(distance < early, core * early + distance, late)


def col_place(tile_at, tiles, pairs):
    tile_at = tile_at ^ (lax.axis_index("col") * tiles)
    shard = lax.shift_right_logical(tile_at, tiles.bit_length() - 1)
    return col_shard(lax.shift_right_logical(shard, 1), shard & 1, pairs) * tiles + (tile_at & (tiles - 1))


def split_kernel(count_ref, plan_ref, values_ref, high_ref, low_ref, buf, places, sems, place_sem):
    capacity, tile, _ = values_ref.shape
    groups = sems.shape[0]
    group = capacity // groups
    count = count_ref[0, 0]
    live_groups = lax.div(count + (group - 1), group)

    def copy(at):
        slots = pl.ds(at * group, group)
        return pltpu.make_async_copy(values_ref.at[slots], buf.at[slots], sems.at[at])

    def store(slot, high, low):
        rows = pl.ds(pl.multiple_of(places[0, slot], tile), tile)
        cols = pl.ds(pl.multiple_of(places[1, slot], tile), tile)
        high_ref[rows, cols] = high
        low_ref[rows, cols] = low

    @pl.loop(0, live_groups)
    def _(at):
        copy(at).start()

    place_copy = pltpu.make_async_copy(plan_ref, places, place_sem)
    place_copy.start()
    place_copy.wait()

    @pl.loop(live_groups * group, capacity, unroll=1)
    def _(slot):
        zeros = jnp.zeros((tile, tile), BF16)
        store(slot, zeros, zeros)

    @pl.loop(0, live_groups)
    def _(at):
        copy(at).wait()

        @pl.loop(0, group, unroll=math.gcd(group, 8))
        def _(step):
            slot = at * group + step
            store(slot, *halves(jnp.where(slot < count, buf[slot], 0.0)))


def flip_kernel(tile, *refs):
    *grad_refs, out_ref = refs
    shard, width = grad_refs[0].shape
    for at, grad_ref in enumerate(grad_refs):
        for first in range(0, shard, tile):
            high, low = halves(grad_ref[pl.ds(first, tile), :].T)
            cols = pl.ds(at * shard + first, tile)
            out_ref[:width, cols] = high
            out_ref[width:, cols] = low


def backward_kernel(firsts, tile, grads_ref, high_ref, low_ref, out_ref):
    _, shard, width = out_ref.shape
    for at, first in enumerate(firsts):
        cols = pl.ds(first * shard, shard)
        both = product(grads_ref[...], high_ref[:, cols])
        total = both[:width] + both[width:] + product(grads_ref[:width, :], low_ref[:, cols])
        for row in range(0, shard, tile):
            out_ref[at, pl.ds(row, tile), :] = total[:, row : row + tile].T


def forward_kernel(first, count, bands, *refs):
    embed_refs, (high_ref, low_ref) = refs[:count], refs[count : count + 2]
    before_refs, out_refs, panel = refs[count + 2 : -1 - bands], refs[-1 - bands : -1], refs[-1]
    _, shard, width = embed_refs[0].shape
    done = 0
    for embeds_ref in embed_refs:
        for at in range(embeds_ref.shape[0]):
            high, low = halves(embeds_ref[at])
            panel[pl.ds(done, shard), :width] = high
            panel[pl.ds(done, shard), width:] = low
            done += shard
    cols = pl.ds(first * shard, done)
    for at, out_ref in enumerate(out_refs):
        rows = pl.ds(at * shard, shard)
        both = product(high_ref[rows, cols], panel[...])
        total = both[:, :width] + both[:, width:] + product(low_ref[rows, cols], panel[:, :width])
        if before_refs:
            total = total + before_refs[at][...]
        out_ref[...] = total


def slots_kernel(tiles, pairs, coords_ref, count_ref, values_ref, embed_ref, grad_ref, forward_ref, backward_ref):
    group, tile, _ = values_ref.shape
    first = pl.program_id(0) * group

    @pl.when(pl.program_id(0) == 0)
    def _():
        forward_ref[...] = jnp.zeros_like(forward_ref)
        backward_ref[...] = jnp.zeros_like(backward_ref)

    for slot in range(group):

        @pl.when(first + slot < count_ref[0, 0])
        def _():
            row_at = row_place(coords_ref[0, 0, 0, first + slot], tiles)
            col_at = col_place(coords_ref[1, 0, 0, first + slot], tiles, pairs)
            rows = pl.ds(pl.multiple_of(row_at * tile, tile), tile)
            cols = pl.ds(pl.multiple_of(col_at * tile, tile), tile)
            high, low = halves(values_ref[slot])
            embed_high, embed_low = halves(embed_ref[cols, :])
            forward_ref[rows, :] += product(high, embed_high) + product(high, embed_low) + product(low, embed_high)
            high, low = halves(values_ref[slot].T)
            grad_high, grad_low = halves(grad_ref[rows, :])
            backward_ref[cols, :] += product(high, grad_high) + product(high, grad_low) + product(low, grad_high)


def swap(x, axis, mask):
    return lax.ppermute(x, axis, [(at, at ^ mask) for at in range(lax.axis_size(axis))])


def call(kernel, out_shape, args, mebibytes=16, flops=0, scratch=(), specs=None, after=None):
    outs = out_shape if isinstance(out_shape, tuple) else (out_shape,)
    specs = specs or [WHOLE] * len(args)
    body = kernel
    if after is not None:
        args, specs = (after, *args), [ANYWHERE, *specs]

        def body(_, *refs):
            kernel(*refs)

    return pl.pallas_call(
        body,
        out_shape=out_shape,
        in_specs=specs,
        out_specs=tuple(WHOLE for _ in outs) if isinstance(out_shape, tuple) else WHOLE,
        scratch_shapes=scratch,
        compiler_params=params(mebibytes),
        cost_estimate=cost(flops, 1024),
    )(*args)


def per_device(embed, cotangent, tile_values, tile_coords, tile_count, row_degree, col_degree):
    shard, width = embed.shape
    capacity, tile = tile_values.shape[2:4]
    n_row, n_col = lax.axis_size("row"), lax.axis_size("col")
    pairs = n_col // 2
    half = pairs // 2
    tiles = shard // tile
    n_rows, n_cols = shard * n_row, shard * n_col
    dense = (n_rows // tile) * (n_cols // tile) <= capacity
    values = tile_values.reshape(tile_values.shape[2:])
    block = jax.ShapeDtypeStruct((shard, width), F32)

    def blocks(count):
        return jax.ShapeDtypeStruct((count, shard, width), F32)

    with jax.named_scope("scale"):
        args = (cotangent, embed, row_degree.reshape(-1, tile), col_degree.reshape(-1, tile), tile_coords)
        grad_scaled, scaled, row_factor, col_factor, plan = call(
            functools.partial(scale_kernel, tiles, pairs),
            (block,) * 4 + (jax.ShapeDtypeStruct((2, capacity), jnp.int32),),
            [pltpu.with_memory_space_constraint(x, pltpu.HBM) for x in args],
            mebibytes=4,
            specs=[pl.BlockSpec(memory_space=pltpu.HBM)] * len(args),
            scratch=[pltpu.VMEM(x.shape, x.dtype) for x in args] + [pltpu.SemaphoreType.DMA((len(args),))],
        )

    with jax.named_scope("gather"):
        crossed = swap(scaled, "col", 2 * half)
        grads = [grad_scaled] + [swap(grad_scaled, "row", k) for k in range(1, n_row)]
        beside = swap(scaled, "col", 1)
        near = {0: call(copy_kernel, blocks(2), [scaled, beside])}
        mask = half // 2
        while mask:
            pairs_of_core = [(at, at ^ (2 * mask)) for at in range(1, n_col, 2)]
            near.update({at | mask: lax.ppermute(x, "col", pairs_of_core) for at, x in near.items()})
            mask //= 2

    def gathered(after):
        passed = call(pass_kernel, block, [crossed], after=after)
        late, mask = {0: passed}, half // 2
        while mask:
            late.update({at | mask: swap(x, "col", 2 * mask) for at, x in late.items()})
            mask //= 2
        return passed, [late[at] for at in range(1, half)]

    def panels(passed, after):
        parts = [near[at] for at in range(1, half)]
        mine = call(stack_kernel, blocks(2 * half - 1), [*parts, passed], after=after)
        return call(
            panel_kernel, (blocks(half + 1), blocks(half + 1)), (scaled, beside, passed, mine, swap(mine, "col", 1))
        )

    def chip_sums(kept, sent, after=None):
        return call(
            pair_kernel,
            (block,) * kept.shape[0],
            (kept, swap(sent, "col", 1)),
            after=after,
        )

    def halved(parts, after):
        parts, got, mask = dict(enumerate(parts)), [], 1
        while mask < half:
            for at in reversed(range(0, half, 2 * mask)):
                arrived = swap(parts.pop(at + mask), "col", 2 * mask)
                if at:
                    parts[at] = call(add_kernel, block, (parts[at], arrived), after=after)
                else:
                    got.append(arrived)
            mask *= 2
        return [parts[0], *got]

    def total(parts, after):
        out, *rest = parts
        for part in rest:
            out = call(add_kernel, block, (out, part), after=after)
        return out

    if dense:
        table = jax.ShapeDtypeStruct((n_rows, n_cols), BF16)
        groups = math.gcd(capacity, 8)
        with jax.named_scope("split"):
            high, low = call(
                split_kernel,
                (table, table),
                (tile_count, plan, pltpu.with_memory_space_constraint(values, pltpu.HBM)),
                mebibytes=32,
                specs=[SCALARS, WHOLE, pl.BlockSpec(memory_space=pltpu.HBM)],
                scratch=[
                    pltpu.VMEM(values.shape, F32),
                    pltpu.SMEM(plan.shape, jnp.int32),
                    pltpu.SemaphoreType.DMA((groups,)),
                    pltpu.SemaphoreType.DMA,
                ],
            )
        with jax.named_scope("gather"):
            passed, late = gathered(high)
        with jax.named_scope("flip"):
            flipped = call(
                functools.partial(flip_kernel, tile),
                jax.ShapeDtypeStruct((2 * width, n_rows), BF16),
                grads,
                after=passed,
                flops=2 * 10**9,
            )
        with jax.named_scope("gather"):
            early, other_early = panels(passed, flipped)

        def backward_part(distances, core, after):
            shards = [shard_at(distance, core) for distance in distances]
            return call(
                functools.partial(backward_kernel, shards, tile),
                blocks(len(shards)),
                (flipped, high, low),
                mebibytes=24,
                after=after,
            )

        def shard_at(distance, core):
            count = half + 1
            if distance < count:
                return core * count + distance
            return 2 * count + core * (pairs - count) + distance - count

        def forward_part(embeds, first, before=(), after=None, flops=0):
            count = sum(x.shape[0] for x in embeds)
            return call(
                functools.partial(forward_kernel, first, len(embeds), n_row),
                (block,) * n_row,
                (*embeds, high, low, *before),
                mebibytes=24,
                scratch=[pltpu.VMEM((count * shard, 2 * width), BF16)],
                after=after,
                flops=flops,
            )

        with jax.named_scope("backward"):
            far, close = range(half, pairs), range(half)
            far_sent = backward_part(far, 1, flipped)
            far_kept = backward_part(far, 0, far_sent)
            sent = backward_part(close, 1, far_kept)
        with jax.named_scope("gather"):
            late = call(copy_kernel, blocks(half - 1), late, after=sent, flops=2 * 10**9)
            other_late = swap(late, "col", 1)
        with jax.named_scope("backward"):
            far_sums = chip_sums(far_kept, far_sent, late)
            kept = backward_part(close, 0, far_sums[0])
        with jax.named_scope("forward"):
            forwards = forward_part([early, other_early], 0, after=kept)
        with jax.named_scope("reduce"):
            crossing = total(halved(far_sums, forwards[0]), forwards[0])
        with jax.named_scope("forward"):
            forwards = forward_part([late, other_late], 2 * (half + 1), forwards, crossing, 2 * 10**9)
        with jax.named_scope("reduce"):
            close_sums = chip_sums(kept, sent, forwards[0])
            after = None
    else:
        group = 8
        with jax.named_scope("gather"):
            passed, late = gathered(plan)
            early, other_early = panels(passed, plan)
            late = call(copy_kernel, blocks(half - 1), late)
            panel = jnp.concatenate([early, other_early, late, swap(late, "col", 1)])
        with jax.named_scope("slots"):
            forward, backward = pl.pallas_call(
                functools.partial(slots_kernel, tiles, pairs),
                out_shape=(
                    jax.ShapeDtypeStruct((n_rows, width), F32),
                    jax.ShapeDtypeStruct((n_cols, width), F32),
                ),
                grid=(capacity // group,),
                in_specs=[SCALARS, SCALARS, pl.BlockSpec((group, tile, tile), lambda at: (at, 0, 0)), WHOLE, WHOLE],
                out_specs=(WHOLE, WHOLE),
                compiler_params=params(40),
                cost_estimate=cost(12 * values.size * width, values.size * 4),
            )(tile_coords, tile_count, values, panel.reshape(-1, width), jnp.concatenate(grads))
            forwards = list(forward.reshape(n_row, shard, width))
            backward = backward.reshape(n_col, shard, width)
            count = half + 1
            kept, sent = (
                jnp.concatenate(
                    [
                        backward[core * count : (core + 1) * count],
                        backward[2 * count + core * (half - 1) : 2 * count + (core + 1) * (half - 1)],
                    ]
                )
                for core in range(2)
            )
        with jax.named_scope("reduce"):
            far_sums, close_sums = (chip_sums(kept[at : at + half], sent[at : at + half]) for at in (half, 0))
            crossing = total(halved(far_sums, forward), forward)
            after = forward

    with jax.named_scope("reduce"):
        mine, *grad_parts = halved(close_sums, after)
        mine = total([mine, swap(crossing, "col", 2 * half)], None)
        row_parts = [forwards[0]] + [swap(forwards[k], "row", k) for k in range(1, n_row)]

    with jax.named_scope("finish"):
        row_sum = call(sum_kernel, block, row_parts, after=mine)
        return call(
            finish_kernel, (block, block), (row_sum, row_factor, col_factor, mine, *grad_parts), mebibytes=4
        )


def solution(mesh):
    return jax.shard_map(
        per_device,
        mesh=mesh,
        in_specs=(
            P(("row", "col"), None),
            P(("col", "row"), None),
            P("col", "row", None, None, None),
            P(None, "col", "row", None),
            P("col", "row"),
            P(("col", "row")),
            P(("row", "col")),
        ),
        out_specs=(P(("col", "row"), None), P(("row", "col"), None)),
        check_vma=False,
    )
```

```python
import functools
import math

import jax
import jax.numpy as jnp
from jax import lax
from jax.experimental import pallas as pl
from jax.experimental.pallas import tpu as pltpu
from jax.sharding import PartitionSpec as P

F32 = jnp.float32
BF16 = jnp.bfloat16
WHOLE = pl.BlockSpec(memory_space=pltpu.VMEM)
ANYWHERE = pl.BlockSpec(memory_space=pl.ANY)
SCALARS = pl.BlockSpec(memory_space=pltpu.SMEM)


def params(mebibytes):
    return pltpu.CompilerParams(vmem_limit_bytes=mebibytes * 2**20)


def cost(flops, moved):
    return pl.CostEstimate(flops=flops, bytes_accessed=moved, transcendentals=0)


def halves(x):
    high = x.astype(BF16)
    return high, (x - high.astype(F32)).astype(BF16)


def product(left, right):
    return jnp.dot(left, right, preferred_element_type=F32)


def row_factors(degree_ref, at, width):
    factors = lax.rsqrt(degree_ref[at : at + 1, :].astype(F32))
    return jnp.broadcast_to(factors, (width, factors.shape[1])).T


def scale_kernel(tiles, pairs, *refs):
    in_refs, (grad_ref, scaled_ref, row_factor_ref, col_factor_ref, plan_ref) = refs[:5], refs[5:10]
    bufs, sems = refs[10:15], refs[15]
    copies = [pltpu.make_async_copy(*pair, sems.at[at]) for at, pair in enumerate(zip(in_refs, bufs))]
    for copy in copies:
        copy.start()
    for copy in copies:
        copy.wait()
    cotangent, embed, row_degree, col_degree, coords = bufs
    for x_buf, degree_buf, out_ref, factor_ref in (
        (embed, col_degree, scaled_ref, col_factor_ref),
        (cotangent, row_degree, grad_ref, row_factor_ref),
    ):
        tile = degree_buf.shape[1]
        for at in range(degree_buf.shape[0]):
            rows = pl.ds(at * tile, tile)
            factors = row_factors(degree_buf, at, x_buf.shape[1])
            factor_ref[rows, :] = factors
            out_ref[rows, :] = x_buf[rows, :] * factors
    plan_ref[0:1, :] = row_place(coords[0, 0], tiles) * tile
    plan_ref[1:2, :] = col_place(coords[1, 0], tiles, pairs) * tile


def sum_kernel(*refs):
    *part_refs, out_ref = refs
    total = part_refs[0][...]
    for part_ref in part_refs[1:]:
        total = total + part_ref[...]
    out_ref[...] = total


def finish_kernel(row_ref, row_factor_ref, col_factor_ref, *refs):
    *part_refs, row_out_ref, col_out_ref = refs
    row_out_ref[...] = row_ref[...] * row_factor_ref[...]
    sum_kernel(*part_refs, col_out_ref)
    col_out_ref[...] = col_out_ref[...] * col_factor_ref[...]


def add_kernel(x_ref, y_ref, out_ref):
    out_ref[...] = x_ref[...] + y_ref[...]


def pair_kernel(kept_ref, got_ref, *out_refs):
    for at, out_ref in enumerate(out_refs):
        out_ref[...] = kept_ref[at] + got_ref[at]


def pass_kernel(x_ref, out_ref):
    out_ref[...] = x_ref[...]


def copy_kernel(*refs):
    *part_refs, out_ref = refs
    for at, part_ref in enumerate(part_refs):
        out_ref[at] = part_ref[...]


def row_place(tile_at, tiles):
    return tile_at ^ (lax.axis_index("row") * tiles)


def col_shard(distance, core, pairs):
    early = pairs // 2 + 1
    late = 2 * early + core * (pairs - early) + distance - early
    return jnp.where(distance < early, core * early + distance, late)


def col_place(tile_at, tiles, pairs):
    tile_at = tile_at ^ (lax.axis_index("col") * tiles)
    shard = lax.shift_right_logical(tile_at, tiles.bit_length() - 1)
    return col_shard(lax.shift_right_logical(shard, 1), shard & 1, pairs) * tiles + (tile_at & (tiles - 1))


def split_kernel(count_ref, plan_ref, values_ref, high_ref, low_ref, buf, places, sems, place_sem):
    capacity, tile, _ = values_ref.shape
    groups = sems.shape[0]
    group = capacity // groups
    count = count_ref[0, 0]
    live_groups = lax.div(count + (group - 1), group)

    def copy(at):
        slots = pl.ds(at * group, group)
        return pltpu.make_async_copy(values_ref.at[slots], buf.at[slots], sems.at[at])

    def store(slot, high, low):
        rows = pl.ds(pl.multiple_of(places[0, slot], tile), tile)
        cols = pl.ds(pl.multiple_of(places[1, slot], tile), tile)
        high_ref[rows, cols] = high
        low_ref[rows, cols] = low

    @pl.loop(0, live_groups)
    def _(at):
        copy(at).start()

    place_copy = pltpu.make_async_copy(plan_ref, places, place_sem)
    place_copy.start()
    place_copy.wait()

    @pl.loop(live_groups * group, capacity, unroll=1)
    def _(slot):
        zeros = jnp.zeros((tile, tile), BF16)
        store(slot, zeros, zeros)

    @pl.loop(0, live_groups)
    def _(at):
        copy(at).wait()

        @pl.loop(0, group, unroll=math.gcd(group, 8))
        def _(step):
            slot = at * group + step
            store(slot, *halves(jnp.where(slot < count, buf[slot], 0.0)))


def flip_kernel(tile, *refs):
    *grad_refs, out_ref = refs
    shard, width = grad_refs[0].shape
    for at, grad_ref in enumerate(grad_refs):
        for first in range(0, shard, tile):
            high, low = halves(grad_ref[pl.ds(first, tile), :].T)
            cols = pl.ds(at * shard + first, tile)
            out_ref[:width, cols] = high
            out_ref[width:, cols] = low


def backward_kernel(firsts, tile, grads_ref, high_ref, low_ref, out_ref):
    _, shard, width = out_ref.shape
    for at, first in enumerate(firsts):
        cols = pl.ds(first * shard, shard)
        both = product(grads_ref[...], high_ref[:, cols])
        total = both[:width] + both[width:] + product(grads_ref[:width, :], low_ref[:, cols])
        for row in range(0, shard, tile):
            out_ref[at, pl.ds(row, tile), :] = total[:, row : row + tile].T


def forward_kernel(count, *refs):
    embed_refs, (high_ref, low_ref), out_refs, panel = refs[:count], refs[count : count + 2], refs[count + 2 : -1], refs[-1]
    _, shard, width = embed_refs[0].shape
    done = 0
    for embeds_ref in embed_refs:
        for at in range(embeds_ref.shape[0]):
            high, low = halves(embeds_ref[at])
            panel[pl.ds(done, shard), :width] = high
            panel[pl.ds(done, shard), width:] = low
            done += shard
    for at, out_ref in enumerate(out_refs):
        rows = pl.ds(at * shard, shard)
        both = product(high_ref[rows, :], panel[...])
        out_ref[...] = both[:, :width] + both[:, width:] + product(low_ref[rows, :], panel[:, :width])


def slots_kernel(tiles, pairs, coords_ref, count_ref, values_ref, embed_ref, grad_ref, forward_ref, backward_ref):
    group, tile, _ = values_ref.shape
    first = pl.program_id(0) * group

    @pl.when(pl.program_id(0) == 0)
    def _():
        forward_ref[...] = jnp.zeros_like(forward_ref)
        backward_ref[...] = jnp.zeros_like(backward_ref)

    for slot in range(group):

        @pl.when(first + slot < count_ref[0, 0])
        def _():
            row_at = row_place(coords_ref[0, 0, 0, first + slot], tiles)
            col_at = col_place(coords_ref[1, 0, 0, first + slot], tiles, pairs)
            rows = pl.ds(pl.multiple_of(row_at * tile, tile), tile)
            cols = pl.ds(pl.multiple_of(col_at * tile, tile), tile)
            high, low = halves(values_ref[slot])
            embed_high, embed_low = halves(embed_ref[cols, :])
            forward_ref[rows, :] += product(high, embed_high) + product(high, embed_low) + product(low, embed_high)
            high, low = halves(values_ref[slot].T)
            grad_high, grad_low = halves(grad_ref[rows, :])
            backward_ref[cols, :] += product(high, grad_high) + product(high, grad_low) + product(low, grad_high)


def swap(x, axis, mask):
    return lax.ppermute(x, axis, [(at, at ^ mask) for at in range(lax.axis_size(axis))])


def call(kernel, out_shape, args, mebibytes=16, flops=0, scratch=(), specs=None, after=None):
    outs = out_shape if isinstance(out_shape, tuple) else (out_shape,)
    specs = specs or [WHOLE] * len(args)
    body = kernel
    if after is not None:
        args, specs = (after, *args), [ANYWHERE, *specs]

        def body(_, *refs):
            kernel(*refs)

    return pl.pallas_call(
        body,
        out_shape=out_shape,
        in_specs=specs,
        out_specs=tuple(WHOLE for _ in outs) if isinstance(out_shape, tuple) else WHOLE,
        scratch_shapes=scratch,
        compiler_params=params(mebibytes),
        cost_estimate=cost(flops, 1024),
    )(*args)


def per_device(embed, cotangent, tile_values, tile_coords, tile_count, row_degree, col_degree):
    shard, width = embed.shape
    capacity, tile = tile_values.shape[2:4]
    n_row, n_col = lax.axis_size("row"), lax.axis_size("col")
    pairs = n_col // 2
    half = pairs // 2
    tiles = shard // tile
    n_rows, n_cols = shard * n_row, shard * n_col
    dense = (n_rows // tile) * (n_cols // tile) <= capacity
    values = tile_values.reshape(tile_values.shape[2:])
    block = jax.ShapeDtypeStruct((shard, width), F32)

    def blocks(count):
        return jax.ShapeDtypeStruct((count, shard, width), F32)

    with jax.named_scope("scale"):
        args = (cotangent, embed, row_degree.reshape(-1, tile), col_degree.reshape(-1, tile), tile_coords)
        grad_scaled, scaled, row_factor, col_factor, plan = call(
            functools.partial(scale_kernel, tiles, pairs),
            (block,) * 4 + (jax.ShapeDtypeStruct((2, capacity), jnp.int32),),
            [pltpu.with_memory_space_constraint(x, pltpu.HBM) for x in args],
            mebibytes=4,
            specs=[pl.BlockSpec(memory_space=pltpu.HBM)] * len(args),
            scratch=[pltpu.VMEM(x.shape, x.dtype) for x in args] + [pltpu.SemaphoreType.DMA((len(args),))],
        )

    with jax.named_scope("gather"):
        crossed = swap(scaled, "col", 2 * half)
        grads = [grad_scaled] + [swap(grad_scaled, "row", k) for k in range(1, n_row)]
        near = {0: scaled}
        mask = half // 2
        while mask:
            near.update({at | mask: swap(x, "col", 2 * mask) for at, x in near.items()})
            mask //= 2

    def gathered(after):
        passed = call(pass_kernel, block, [crossed], after=after)
        late, mask = {0: passed}, half // 2
        while mask:
            late.update({at | mask: swap(x, "col", 2 * mask) for at, x in late.items()})
            mask //= 2
        return passed, [late[at] for at in range(1, half)]

    def stacked(passed, after):
        return call(copy_kernel, blocks(half + 1), [near[at] for at in range(half)] + [passed], after=after)

    def chip_sums(kept, sent, after=None):
        return call(
            pair_kernel,
            (block,) * kept.shape[0],
            (kept, swap(sent, "col", 1)),
            after=after,
        )

    def halved(parts, after):
        parts, got, mask = dict(enumerate(parts)), [], 1
        while mask < half:
            for at in reversed(range(0, half, 2 * mask)):
                arrived = swap(parts.pop(at + mask), "col", 2 * mask)
                if at:
                    parts[at] = call(add_kernel, block, (parts[at], arrived), after=after)
                else:
                    got.append(arrived)
            mask *= 2
        return [parts[0], *got]

    def total(parts, after, flops=0):
        out, *rest = parts
        for part in rest:
            out = call(add_kernel, block, (out, part), after=after, flops=flops)
        return out

    if dense:
        table = jax.ShapeDtypeStruct((n_rows, n_cols), BF16)
        groups = math.gcd(capacity, 8)
        with jax.named_scope("split"):
            high, low = call(
                split_kernel,
                (table, table),
                (tile_count, plan, pltpu.with_memory_space_constraint(values, pltpu.HBM)),
                mebibytes=32,
                specs=[SCALARS, WHOLE, pl.BlockSpec(memory_space=pltpu.HBM)],
                scratch=[
                    pltpu.VMEM(values.shape, F32),
                    pltpu.SMEM(plan.shape, jnp.int32),
                    pltpu.SemaphoreType.DMA((groups,)),
                    pltpu.SemaphoreType.DMA,
                ],
            )
        with jax.named_scope("gather"):
            passed, late = gathered(high)
        with jax.named_scope("flip"):
            flipped = call(
                functools.partial(flip_kernel, tile),
                jax.ShapeDtypeStruct((2 * width, n_rows), BF16),
                grads,
                after=passed,
            )
        with jax.named_scope("gather"):
            early = stacked(passed, flipped)
            other_early = swap(early, "col", 1)

        def backward_part(distances, core, after):
            shards = [shard_at(distance, core) for distance in distances]
            return call(
                functools.partial(backward_kernel, shards, tile),
                blocks(len(shards)),
                (flipped, high, low),
                mebibytes=24,
                after=after,
            )

        def shard_at(distance, core):
            count = half + 1
            if distance < count:
                return core * count + distance
            return 2 * count + core * (pairs - count) + distance - count

        def forward(embeds, after):
            return call(
                functools.partial(forward_kernel, len(embeds)),
                (block,) * n_row,
                (*embeds, high, low),
                mebibytes=24,
                scratch=[pltpu.VMEM((n_cols, 2 * width), BF16)],
                after=after,
            )

        with jax.named_scope("backward"):
            far, close = range(half, pairs), range(half)
            far_sent = backward_part(far, 1, early)
            far_kept = backward_part(far, 0, far_sent)
            sent = backward_part(close, 1, far_kept)
            kept = backward_part(close, 0, sent)
        with jax.named_scope("gather"):
            late = call(copy_kernel, blocks(half - 1), late, after=kept, flops=2 * 10**9)
            other_late = swap(late, "col", 1)
        with jax.named_scope("backward"):
            far_sums = chip_sums(far_kept, far_sent, late)
        with jax.named_scope("forward"):
            forwards = forward([early, other_early, late, other_late], far_sums[0])
        with jax.named_scope("reduce"):
            crossing = total(halved(far_sums, forwards[0]), forwards[0], 10**9)
        with jax.named_scope("reduce"):
            close_sums = chip_sums(kept, sent, forwards[0])
            after = None
    else:
        group = 8
        with jax.named_scope("gather"):
            passed, late = gathered(plan)
            early = stacked(passed, plan)
            late = call(copy_kernel, blocks(half - 1), late)
            panel = jnp.concatenate([early, swap(early, "col", 1), late, swap(late, "col", 1)])
        with jax.named_scope("slots"):
            forward, backward = pl.pallas_call(
                functools.partial(slots_kernel, tiles, pairs),
                out_shape=(
                    jax.ShapeDtypeStruct((n_rows, width), F32),
                    jax.ShapeDtypeStruct((n_cols, width), F32),
                ),
                grid=(capacity // group,),
                in_specs=[SCALARS, SCALARS, pl.BlockSpec((group, tile, tile), lambda at: (at, 0, 0)), WHOLE, WHOLE],
                out_specs=(WHOLE, WHOLE),
                compiler_params=params(40),
                cost_estimate=cost(12 * values.size * width, values.size * 4),
            )(tile_coords, tile_count, values, panel.reshape(-1, width), jnp.concatenate(grads))
            forwards = list(forward.reshape(n_row, shard, width))
            backward = backward.reshape(n_col, shard, width)
            count = half + 1
            kept, sent = (
                jnp.concatenate(
                    [
                        backward[core * count : (core + 1) * count],
                        backward[2 * count + core * (half - 1) : 2 * count + (core + 1) * (half - 1)],
                    ]
                )
                for core in range(2)
            )
        with jax.named_scope("reduce"):
            far_sums, close_sums = (chip_sums(kept[at : at + half], sent[at : at + half]) for at in (half, 0))
            crossing = total(halved(far_sums, forward), forward)
            after = forward

    with jax.named_scope("reduce"):
        mine, *grad_parts = halved(close_sums, after)
        first = [swap(forwards[k], "row", k) for k in range(1, n_row - 1)]
        row_sum = call(sum_kernel, block, [forwards[0], *first])
        mine = total([mine, swap(crossing, "col", 2 * half)], row_sum)
        row_sum = call(sum_kernel, block, [row_sum, swap(forwards[-1], "row", n_row - 1)], after=mine)
        return call(
            finish_kernel, (block, block), (row_sum, row_factor, col_factor, mine, *grad_parts), mebibytes=4
        )


def solution(mesh):
    return jax.shard_map(
        per_device,
        mesh=mesh,
        in_specs=(
            P(("row", "col"), None),
            P(("col", "row"), None),
            P("col", "row", None, None, None),
            P(None, "col", "row", None),
            P("col", "row"),
            P(("col", "row")),
            P(("row", "col")),
        ),
        out_specs=(P(("col", "row"), None), P(("row", "col"), None)),
        check_vma=False,
    )
```

```python
import functools
import math

import jax
import jax.numpy as jnp
from jax import lax
from jax.experimental import pallas as pl
from jax.experimental.pallas import tpu as pltpu
from jax.sharding import PartitionSpec as P

F32 = jnp.float32
BF16 = jnp.bfloat16
WHOLE = pl.BlockSpec(memory_space=pltpu.VMEM)
ANYWHERE = pl.BlockSpec(memory_space=pl.ANY)
SCALARS = pl.BlockSpec(memory_space=pltpu.SMEM)


def params(mebibytes):
    return pltpu.CompilerParams(vmem_limit_bytes=mebibytes * 2**20)


def cost(flops, moved):
    return pl.CostEstimate(flops=flops, bytes_accessed=moved, transcendentals=0)


def halves(x):
    high = x.astype(BF16)
    return high, (x - high.astype(F32)).astype(BF16)


def product(left, right):
    return jnp.dot(left, right, preferred_element_type=F32)


def row_factors(degree_ref, at, width):
    factors = lax.rsqrt(degree_ref[at : at + 1, :].astype(F32))
    return jnp.broadcast_to(factors, (width, factors.shape[1])).T


def scale_kernel(tiles, pairs, *refs):
    in_refs, (grad_ref, scaled_ref, row_factor_ref, col_factor_ref, plan_ref) = refs[:5], refs[5:10]
    bufs, sems = refs[10:15], refs[15]
    copies = [pltpu.make_async_copy(*pair, sems.at[at]) for at, pair in enumerate(zip(in_refs, bufs))]
    for copy in copies:
        copy.start()
    for copy in copies:
        copy.wait()
    cotangent, embed, row_degree, col_degree, coords = bufs
    for x_buf, degree_buf, out_ref, factor_ref in (
        (embed, col_degree, scaled_ref, col_factor_ref),
        (cotangent, row_degree, grad_ref, row_factor_ref),
    ):
        tile = degree_buf.shape[1]
        for at in range(degree_buf.shape[0]):
            rows = pl.ds(at * tile, tile)
            factors = row_factors(degree_buf, at, x_buf.shape[1])
            factor_ref[rows, :] = factors
            out_ref[rows, :] = x_buf[rows, :] * factors
    plan_ref[0:1, :] = row_place(coords[0, 0], tiles) * tile
    plan_ref[1:2, :] = col_place(coords[1, 0], tiles, pairs) * tile


def sum_kernel(*refs):
    *part_refs, out_ref = refs
    total = part_refs[0][...]
    for part_ref in part_refs[1:]:
        total = total + part_ref[...]
    out_ref[...] = total


def finish_kernel(row_ref, row_factor_ref, col_factor_ref, *refs):
    *part_refs, row_out_ref, col_out_ref = refs
    row_out_ref[...] = row_ref[...] * row_factor_ref[...]
    sum_kernel(*part_refs, col_out_ref)
    col_out_ref[...] = col_out_ref[...] * col_factor_ref[...]


def add_kernel(x_ref, y_ref, out_ref):
    out_ref[...] = x_ref[...] + y_ref[...]


def pair_kernel(kept_ref, got_ref, *out_refs):
    for at, out_ref in enumerate(out_refs):
        out_ref[...] = kept_ref[at] + got_ref[at]


def pass_kernel(x_ref, out_ref):
    out_ref[...] = x_ref[...]


def copy_kernel(*refs):
    *part_refs, out_ref = refs
    for at, part_ref in enumerate(part_refs):
        out_ref[at] = part_ref[...]


def row_place(tile_at, tiles):
    return tile_at ^ (lax.axis_index("row") * tiles)


def col_shard(distance, core, pairs):
    early = pairs // 2 + 1
    late = 2 * early + core * (pairs - early) + distance - early
    return jnp.where(distance < early, core * early + distance, late)


def col_place(tile_at, tiles, pairs):
    tile_at = tile_at ^ (lax.axis_index("col") * tiles)
    shard = lax.shift_right_logical(tile_at, tiles.bit_length() - 1)
    return col_shard(lax.shift_right_logical(shard, 1), shard & 1, pairs) * tiles + (tile_at & (tiles - 1))


def split_kernel(count_ref, plan_ref, values_ref, high_ref, low_ref, buf, places, sems, place_sem):
    capacity, tile, _ = values_ref.shape
    groups = sems.shape[0]
    group = capacity // groups
    count = count_ref[0, 0]
    live_groups = lax.div(count + (group - 1), group)

    def copy(at):
        slots = pl.ds(at * group, group)
        return pltpu.make_async_copy(values_ref.at[slots], buf.at[slots], sems.at[at])

    def store(slot, high, low):
        rows = pl.ds(pl.multiple_of(places[0, slot], tile), tile)
        cols = pl.ds(pl.multiple_of(places[1, slot], tile), tile)
        high_ref[rows, cols] = high
        low_ref[rows, cols] = low

    @pl.loop(0, live_groups)
    def _(at):
        copy(at).start()

    place_copy = pltpu.make_async_copy(plan_ref, places, place_sem)
    place_copy.start()
    place_copy.wait()

    @pl.loop(live_groups * group, capacity, unroll=1)
    def _(slot):
        zeros = jnp.zeros((tile, tile), BF16)
        store(slot, zeros, zeros)

    @pl.loop(0, live_groups)
    def _(at):
        copy(at).wait()

        @pl.loop(0, group, unroll=math.gcd(group, 8))
        def _(step):
            slot = at * group + step
            store(slot, *halves(jnp.where(slot < count, buf[slot], 0.0)))


def flip_kernel(tile, *refs):
    *grad_refs, out_ref = refs
    shard, width = grad_refs[0].shape
    for at, grad_ref in enumerate(grad_refs):
        for first in range(0, shard, tile):
            high, low = halves(grad_ref[pl.ds(first, tile), :].T)
            cols = pl.ds(at * shard + first, tile)
            out_ref[:width, cols] = high
            out_ref[width:, cols] = low


def backward_kernel(firsts, tile, grads_ref, high_ref, low_ref, out_ref):
    _, shard, width = out_ref.shape
    for at, first in enumerate(firsts):
        cols = pl.ds(first * shard, shard)
        both = product(grads_ref[...], high_ref[:, cols])
        total = both[:width] + both[width:] + product(grads_ref[:width, :], low_ref[:, cols])
        for row in range(0, shard, tile):
            out_ref[at, pl.ds(row, tile), :] = total[:, row : row + tile].T


def forward_kernel(count, *refs):
    embed_refs, (high_ref, low_ref), out_refs, panel = refs[:count], refs[count : count + 2], refs[count + 2 : -1], refs[-1]
    _, shard, width = embed_refs[0].shape
    done = 0
    for embeds_ref in embed_refs:
        for at in range(embeds_ref.shape[0]):
            high, low = halves(embeds_ref[at])
            panel[pl.ds(done, shard), :width] = high
            panel[pl.ds(done, shard), width:] = low
            done += shard
    for at, out_ref in enumerate(out_refs):
        rows = pl.ds(at * shard, shard)
        both = product(high_ref[rows, :], panel[...])
        out_ref[...] = both[:, :width] + both[:, width:] + product(low_ref[rows, :], panel[:, :width])


def slots_kernel(tiles, pairs, coords_ref, count_ref, values_ref, embed_ref, grad_ref, forward_ref, backward_ref):
    group, tile, _ = values_ref.shape
    first = pl.program_id(0) * group

    @pl.when(pl.program_id(0) == 0)
    def _():
        forward_ref[...] = jnp.zeros_like(forward_ref)
        backward_ref[...] = jnp.zeros_like(backward_ref)

    for slot in range(group):

        @pl.when(first + slot < count_ref[0, 0])
        def _():
            row_at = row_place(coords_ref[0, 0, 0, first + slot], tiles)
            col_at = col_place(coords_ref[1, 0, 0, first + slot], tiles, pairs)
            rows = pl.ds(pl.multiple_of(row_at * tile, tile), tile)
            cols = pl.ds(pl.multiple_of(col_at * tile, tile), tile)
            high, low = halves(values_ref[slot])
            embed_high, embed_low = halves(embed_ref[cols, :])
            forward_ref[rows, :] += product(high, embed_high) + product(high, embed_low) + product(low, embed_high)
            high, low = halves(values_ref[slot].T)
            grad_high, grad_low = halves(grad_ref[rows, :])
            backward_ref[cols, :] += product(high, grad_high) + product(high, grad_low) + product(low, grad_high)


def swap(x, axis, mask):
    return lax.ppermute(x, axis, [(at, at ^ mask) for at in range(lax.axis_size(axis))])


def call(kernel, out_shape, args, mebibytes=16, flops=0, scratch=(), specs=None, after=None):
    outs = out_shape if isinstance(out_shape, tuple) else (out_shape,)
    specs = specs or [WHOLE] * len(args)
    body = kernel
    if after is not None:
        args, specs = (after, *args), [ANYWHERE, *specs]

        def body(_, *refs):
            kernel(*refs)

    return pl.pallas_call(
        body,
        out_shape=out_shape,
        in_specs=specs,
        out_specs=tuple(WHOLE for _ in outs) if isinstance(out_shape, tuple) else WHOLE,
        scratch_shapes=scratch,
        compiler_params=params(mebibytes),
        cost_estimate=cost(flops, 1024),
    )(*args)


def per_device(embed, cotangent, tile_values, tile_coords, tile_count, row_degree, col_degree):
    shard, width = embed.shape
    capacity, tile = tile_values.shape[2:4]
    n_row, n_col = lax.axis_size("row"), lax.axis_size("col")
    pairs = n_col // 2
    half = pairs // 2
    tiles = shard // tile
    n_rows, n_cols = shard * n_row, shard * n_col
    dense = (n_rows // tile) * (n_cols // tile) <= capacity
    values = tile_values.reshape(tile_values.shape[2:])
    block = jax.ShapeDtypeStruct((shard, width), F32)

    def blocks(count):
        return jax.ShapeDtypeStruct((count, shard, width), F32)

    with jax.named_scope("scale"):
        args = (cotangent, embed, row_degree.reshape(-1, tile), col_degree.reshape(-1, tile), tile_coords)
        grad_scaled, scaled, row_factor, col_factor, plan = call(
            functools.partial(scale_kernel, tiles, pairs),
            (block,) * 4 + (jax.ShapeDtypeStruct((2, capacity), jnp.int32),),
            [pltpu.with_memory_space_constraint(x, pltpu.HBM) for x in args],
            mebibytes=4,
            specs=[pl.BlockSpec(memory_space=pltpu.HBM)] * len(args),
            scratch=[pltpu.VMEM(x.shape, x.dtype) for x in args] + [pltpu.SemaphoreType.DMA((len(args),))],
        )

    with jax.named_scope("gather"):
        crossed = swap(scaled, "col", 2 * half)
        grads = [grad_scaled] + [swap(grad_scaled, "row", k) for k in range(1, n_row)]
        near = {0: scaled}
        mask = half // 2
        while mask:
            near.update({at | mask: swap(x, "col", 2 * mask) for at, x in near.items()})
            mask //= 2

    def gathered(after):
        passed = call(pass_kernel, block, [crossed], after=after)
        late, mask = {0: passed}, half // 2
        while mask:
            late.update({at | mask: swap(x, "col", 2 * mask) for at, x in late.items()})
            mask //= 2
        return passed, [late[at] for at in range(1, half)]

    def stacked(passed, after):
        return call(copy_kernel, blocks(half + 1), [near[at] for at in range(half)] + [passed], after=after)

    def chip_sums(kept, sent, after=None):
        return call(
            pair_kernel,
            (block,) * kept.shape[0],
            (kept, swap(sent, "col", 1)),
            after=after,
        )

    def halved(parts, after):
        parts, got, mask = dict(enumerate(parts)), [], 1
        while mask < half:
            for at in reversed(range(0, half, 2 * mask)):
                arrived = swap(parts.pop(at + mask), "col", 2 * mask)
                if at:
                    parts[at] = call(add_kernel, block, (parts[at], arrived), after=after)
                else:
                    got.append(arrived)
            mask *= 2
        return [parts[0], *got]

    def total(parts, after, flops=0):
        out, *rest = parts
        for part in rest:
            out = call(add_kernel, block, (out, part), after=after, flops=flops)
        return out

    if dense:
        table = jax.ShapeDtypeStruct((n_rows, n_cols), BF16)
        groups = math.gcd(capacity, 8)
        with jax.named_scope("split"):
            high, low = call(
                split_kernel,
                (table, table),
                (tile_count, plan, pltpu.with_memory_space_constraint(values, pltpu.HBM)),
                mebibytes=32,
                specs=[SCALARS, WHOLE, pl.BlockSpec(memory_space=pltpu.HBM)],
                scratch=[
                    pltpu.VMEM(values.shape, F32),
                    pltpu.SMEM(plan.shape, jnp.int32),
                    pltpu.SemaphoreType.DMA((groups,)),
                    pltpu.SemaphoreType.DMA,
                ],
            )
        with jax.named_scope("gather"):
            passed, late = gathered(high)
        with jax.named_scope("flip"):
            flipped = call(
                functools.partial(flip_kernel, tile),
                jax.ShapeDtypeStruct((2 * width, n_rows), BF16),
                grads,
                after=passed,
            )
        with jax.named_scope("gather"):
            early = stacked(passed, flipped)
            other_early = swap(early, "col", 1)

        def backward_part(distances, core, after):
            shards = [shard_at(distance, core) for distance in distances]
            return call(
                functools.partial(backward_kernel, shards, tile),
                blocks(len(shards)),
                (flipped, high, low),
                mebibytes=24,
                after=after,
            )

        def shard_at(distance, core):
            count = half + 1
            if distance < count:
                return core * count + distance
            return 2 * count + core * (pairs - count) + distance - count

        def forward(embeds, after):
            return call(
                functools.partial(forward_kernel, len(embeds)),
                (block,) * n_row,
                (*embeds, high, low),
                mebibytes=24,
                scratch=[pltpu.VMEM((n_cols, 2 * width), BF16)],
                after=after,
            )

        with jax.named_scope("backward"):
            far, close = range(half, pairs), range(half)
            far_sent = backward_part(far, 1, early)
            far_kept = backward_part(far, 0, far_sent)
            sent = backward_part(close, 1, far_kept)
            kept = backward_part(close, 0, sent)
        with jax.named_scope("gather"):
            late = call(copy_kernel, blocks(half - 1), late, after=kept, flops=2 * 10**9)
            other_late = swap(late, "col", 1)
        with jax.named_scope("backward"):
            far_sums = chip_sums(far_kept, far_sent, late)
        with jax.named_scope("forward"):
            forwards = forward([early, other_early, late, other_late], far_sums[0])
        with jax.named_scope("reduce"):
            crossing = total(halved(far_sums, forwards[0]), forwards[0], 10**9)
        with jax.named_scope("reduce"):
            close_sums = chip_sums(kept, sent, forwards[0])
            after = None
    else:
        group = 8
        with jax.named_scope("gather"):
            passed, late = gathered(plan)
            early = stacked(passed, plan)
            late = call(copy_kernel, blocks(half - 1), late)
            panel = jnp.concatenate([early, swap(early, "col", 1), late, swap(late, "col", 1)])
        with jax.named_scope("slots"):
            forward, backward = pl.pallas_call(
                functools.partial(slots_kernel, tiles, pairs),
                out_shape=(
                    jax.ShapeDtypeStruct((n_rows, width), F32),
                    jax.ShapeDtypeStruct((n_cols, width), F32),
                ),
                grid=(capacity // group,),
                in_specs=[SCALARS, SCALARS, pl.BlockSpec((group, tile, tile), lambda at: (at, 0, 0)), WHOLE, WHOLE],
                out_specs=(WHOLE, WHOLE),
                compiler_params=params(40),
                cost_estimate=cost(12 * values.size * width, values.size * 4),
            )(tile_coords, tile_count, values, panel.reshape(-1, width), jnp.concatenate(grads))
            forwards = list(forward.reshape(n_row, shard, width))
            backward = backward.reshape(n_col, shard, width)
            count = half + 1
            kept, sent = (
                jnp.concatenate(
                    [
                        backward[core * count : (core + 1) * count],
                        backward[2 * count + core * (half - 1) : 2 * count + (core + 1) * (half - 1)],
                    ]
                )
                for core in range(2)
            )
        with jax.named_scope("reduce"):
            far_sums, close_sums = (chip_sums(kept[at : at + half], sent[at : at + half]) for at in (half, 0))
            crossing = total(halved(far_sums, forward), forward)
            after = forward

    with jax.named_scope("reduce"):
        mine, *grad_parts = halved(close_sums, after)
        row_sum = call(sum_kernel, block, [forwards[0], swap(forwards[1], "row", 1)])
        mine = total([mine, swap(crossing, "col", 2 * half)], row_sum, 10**9)
        row_sum = call(sum_kernel, block, [row_sum] + [swap(forwards[k], "row", k) for k in range(2, n_row)], after=mine)
        return call(
            finish_kernel, (block, block), (row_sum, row_factor, col_factor, mine, *grad_parts), mebibytes=4
        )


def solution(mesh):
    return jax.shard_map(
        per_device,
        mesh=mesh,
        in_specs=(
            P(("row", "col"), None),
            P(("col", "row"), None),
            P("col", "row", None, None, None),
            P(None, "col", "row", None),
            P("col", "row"),
            P(("col", "row")),
            P(("row", "col")),
        ),
        out_specs=(P(("col", "row"), None), P(("row", "col"), None)),
        check_vma=False,
    )
```

```python
import functools
import math

import jax
import jax.numpy as jnp
from jax import lax
from jax.experimental import pallas as pl
from jax.experimental.pallas import tpu as pltpu
from jax.sharding import PartitionSpec as P

F32 = jnp.float32
BF16 = jnp.bfloat16
WHOLE = pl.BlockSpec(memory_space=pltpu.VMEM)
ANYWHERE = pl.BlockSpec(memory_space=pl.ANY)
SCALARS = pl.BlockSpec(memory_space=pltpu.SMEM)


def params(mebibytes):
    return pltpu.CompilerParams(vmem_limit_bytes=mebibytes * 2**20)


def cost(flops, moved):
    return pl.CostEstimate(flops=flops, bytes_accessed=moved, transcendentals=0)


def halves(x):
    high = x.astype(BF16)
    return high, (x - high.astype(F32)).astype(BF16)


def product(left, right):
    return jnp.dot(left, right, preferred_element_type=F32)


def row_factors(degree_ref, at, width):
    factors = lax.rsqrt(degree_ref[at : at + 1, :].astype(F32))
    return jnp.broadcast_to(factors, (width, factors.shape[1])).T


def scale_kernel(tiles, pairs, *refs):
    in_refs, (grad_ref, scaled_ref, row_factor_ref, col_factor_ref, plan_ref) = refs[:5], refs[5:10]
    bufs, sems = refs[10:15], refs[15]
    copies = [pltpu.make_async_copy(*pair, sems.at[at]) for at, pair in enumerate(zip(in_refs, bufs))]
    for copy in copies:
        copy.start()
    for copy in copies:
        copy.wait()
    cotangent, embed, row_degree, col_degree, coords = bufs
    for x_buf, degree_buf, out_ref, factor_ref in (
        (embed, col_degree, scaled_ref, col_factor_ref),
        (cotangent, row_degree, grad_ref, row_factor_ref),
    ):
        tile = degree_buf.shape[1]
        for at in range(degree_buf.shape[0]):
            rows = pl.ds(at * tile, tile)
            factors = row_factors(degree_buf, at, x_buf.shape[1])
            factor_ref[rows, :] = factors
            out_ref[rows, :] = x_buf[rows, :] * factors
    plan_ref[0:1, :] = row_place(coords[0, 0], tiles) * tile
    plan_ref[1:2, :] = col_place(coords[1, 0], tiles, pairs) * tile


def sum_kernel(*refs):
    *part_refs, out_ref = refs
    total = part_refs[0][...]
    for part_ref in part_refs[1:]:
        total = total + part_ref[...]
    out_ref[...] = total


def finish_kernel(row_ref, row_factor_ref, col_factor_ref, *refs):
    *part_refs, row_out_ref, col_out_ref = refs
    row_out_ref[...] = row_ref[...] * row_factor_ref[...]
    sum_kernel(*part_refs, col_out_ref)
    col_out_ref[...] = col_out_ref[...] * col_factor_ref[...]


def add_kernel(x_ref, y_ref, out_ref):
    out_ref[...] = x_ref[...] + y_ref[...]


def pair_kernel(kept_ref, got_ref, *out_refs):
    for at, out_ref in enumerate(out_refs):
        out_ref[...] = kept_ref[at] + got_ref[at]


def pass_kernel(x_ref, out_ref):
    out_ref[...] = x_ref[...]


def copy_kernel(*refs):
    *part_refs, out_ref = refs
    for at, part_ref in enumerate(part_refs):
        out_ref[at] = part_ref[...]


def row_place(tile_at, tiles):
    return tile_at ^ (lax.axis_index("row") * tiles)


def col_shard(distance, core, pairs):
    early = pairs // 2 + 1
    late = 2 * early + core * (pairs - early) + distance - early
    return jnp.where(distance < early, core * early + distance, late)


def col_place(tile_at, tiles, pairs):
    tile_at = tile_at ^ (lax.axis_index("col") * tiles)
    shard = lax.shift_right_logical(tile_at, tiles.bit_length() - 1)
    return col_shard(lax.shift_right_logical(shard, 1), shard & 1, pairs) * tiles + (tile_at & (tiles - 1))


def split_kernel(count_ref, plan_ref, values_ref, high_ref, low_ref, buf, places, sems, place_sem):
    capacity, tile, _ = values_ref.shape
    groups = sems.shape[0]
    group = capacity // groups
    count = count_ref[0, 0]
    live_groups = lax.div(count + (group - 1), group)

    def copy(at):
        slots = pl.ds(at * group, group)
        return pltpu.make_async_copy(values_ref.at[slots], buf.at[slots], sems.at[at])

    def store(slot, high, low):
        rows = pl.ds(pl.multiple_of(places[0, slot], tile), tile)
        cols = pl.ds(pl.multiple_of(places[1, slot], tile), tile)
        high_ref[rows, cols] = high
        low_ref[rows, cols] = low

    @pl.loop(0, live_groups)
    def _(at):
        copy(at).start()

    place_copy = pltpu.make_async_copy(plan_ref, places, place_sem)
    place_copy.start()
    place_copy.wait()

    @pl.loop(live_groups * group, capacity, unroll=1)
    def _(slot):
        zeros = jnp.zeros((tile, tile), BF16)
        store(slot, zeros, zeros)

    @pl.loop(0, live_groups)
    def _(at):
        copy(at).wait()

        @pl.loop(0, group, unroll=math.gcd(group, 8))
        def _(step):
            slot = at * group + step
            store(slot, *halves(jnp.where(slot < count, buf[slot], 0.0)))


def flip_kernel(tile, *refs):
    *grad_refs, out_ref = refs
    shard, width = grad_refs[0].shape
    for at, grad_ref in enumerate(grad_refs):
        for first in range(0, shard, tile):
            high, low = halves(grad_ref[pl.ds(first, tile), :].T)
            cols = pl.ds(at * shard + first, tile)
            out_ref[:width, cols] = high
            out_ref[width:, cols] = low


def backward_kernel(firsts, tile, grads_ref, high_ref, low_ref, out_ref):
    _, shard, width = out_ref.shape
    for at, first in enumerate(firsts):
        cols = pl.ds(first * shard, shard)
        both = product(grads_ref[...], high_ref[:, cols])
        total = both[:width] + both[width:] + product(grads_ref[:width, :], low_ref[:, cols])
        for row in range(0, shard, tile):
            out_ref[at, pl.ds(row, tile), :] = total[:, row : row + tile].T


def forward_kernel(count, *refs):
    embed_refs, (high_ref, low_ref), out_refs, panel = refs[:count], refs[count : count + 2], refs[count + 2 : -1], refs[-1]
    _, shard, width = embed_refs[0].shape
    done = 0
    for embeds_ref in embed_refs:
        for at in range(embeds_ref.shape[0]):
            high, low = halves(embeds_ref[at])
            panel[pl.ds(done, shard), :width] = high
            panel[pl.ds(done, shard), width:] = low
            done += shard
    for at, out_ref in enumerate(out_refs):
        rows = pl.ds(at * shard, shard)
        both = product(high_ref[rows, :], panel[...])
        out_ref[...] = both[:, :width] + both[:, width:] + product(low_ref[rows, :], panel[:, :width])


def slots_kernel(tiles, pairs, coords_ref, count_ref, values_ref, embed_ref, grad_ref, forward_ref, backward_ref):
    group, tile, _ = values_ref.shape
    first = pl.program_id(0) * group

    @pl.when(pl.program_id(0) == 0)
    def _():
        forward_ref[...] = jnp.zeros_like(forward_ref)
        backward_ref[...] = jnp.zeros_like(backward_ref)

    for slot in range(group):

        @pl.when(first + slot < count_ref[0, 0])
        def _():
            row_at = row_place(coords_ref[0, 0, 0, first + slot], tiles)
            col_at = col_place(coords_ref[1, 0, 0, first + slot], tiles, pairs)
            rows = pl.ds(pl.multiple_of(row_at * tile, tile), tile)
            cols = pl.ds(pl.multiple_of(col_at * tile, tile), tile)
            high, low = halves(values_ref[slot])
            embed_high, embed_low = halves(embed_ref[cols, :])
            forward_ref[rows, :] += product(high, embed_high) + product(high, embed_low) + product(low, embed_high)
            high, low = halves(values_ref[slot].T)
            grad_high, grad_low = halves(grad_ref[rows, :])
            backward_ref[cols, :] += product(high, grad_high) + product(high, grad_low) + product(low, grad_high)


def swap(x, axis, mask):
    return lax.ppermute(x, axis, [(at, at ^ mask) for at in range(lax.axis_size(axis))])


def call(kernel, out_shape, args, mebibytes=16, flops=0, scratch=(), specs=None, after=None):
    outs = out_shape if isinstance(out_shape, tuple) else (out_shape,)
    specs = specs or [WHOLE] * len(args)
    body = kernel
    if after is not None:
        args, specs = (after, *args), [ANYWHERE, *specs]

        def body(_, *refs):
            kernel(*refs)

    return pl.pallas_call(
        body,
        out_shape=out_shape,
        in_specs=specs,
        out_specs=tuple(WHOLE for _ in outs) if isinstance(out_shape, tuple) else WHOLE,
        scratch_shapes=scratch,
        compiler_params=params(mebibytes),
        cost_estimate=cost(flops, 1024),
    )(*args)


def per_device(embed, cotangent, tile_values, tile_coords, tile_count, row_degree, col_degree):
    shard, width = embed.shape
    capacity, tile = tile_values.shape[2:4]
    n_row, n_col = lax.axis_size("row"), lax.axis_size("col")
    pairs = n_col // 2
    half = pairs // 2
    tiles = shard // tile
    n_rows, n_cols = shard * n_row, shard * n_col
    dense = (n_rows // tile) * (n_cols // tile) <= capacity
    values = tile_values.reshape(tile_values.shape[2:])
    block = jax.ShapeDtypeStruct((shard, width), F32)

    def blocks(count):
        return jax.ShapeDtypeStruct((count, shard, width), F32)

    with jax.named_scope("scale"):
        args = (cotangent, embed, row_degree.reshape(-1, tile), col_degree.reshape(-1, tile), tile_coords)
        grad_scaled, scaled, row_factor, col_factor, plan = call(
            functools.partial(scale_kernel, tiles, pairs),
            (block,) * 4 + (jax.ShapeDtypeStruct((2, capacity), jnp.int32),),
            [pltpu.with_memory_space_constraint(x, pltpu.HBM) for x in args],
            mebibytes=4,
            specs=[pl.BlockSpec(memory_space=pltpu.HBM)] * len(args),
            scratch=[pltpu.VMEM(x.shape, x.dtype) for x in args] + [pltpu.SemaphoreType.DMA((len(args),))],
        )

    with jax.named_scope("gather"):
        crossed = swap(scaled, "col", 2 * half)
        grads = [grad_scaled] + [swap(grad_scaled, "row", k) for k in range(1, n_row)]
        near = {0: scaled}
        mask = half // 2
        while mask:
            near.update({at | mask: swap(x, "col", 2 * mask) for at, x in near.items()})
            mask //= 2

    def gathered(after):
        passed = call(pass_kernel, block, [crossed], after=after)
        late, mask = {0: passed}, half // 2
        while mask:
            late.update({at | mask: swap(x, "col", 2 * mask) for at, x in late.items()})
            mask //= 2
        return passed, [late[at] for at in range(1, half)]

    def stacked(passed, after):
        return call(copy_kernel, blocks(half + 1), [near[at] for at in range(half)] + [passed], after=after)

    def chip_sums(kept, sent, after=None):
        return call(
            pair_kernel,
            (block,) * kept.shape[0],
            (kept, swap(sent, "col", 1)),
            after=after,
        )

    def halved(parts, after):
        parts, got, mask = dict(enumerate(parts)), [], 1
        while mask < half:
            for at in reversed(range(0, half, 2 * mask)):
                arrived = swap(parts.pop(at + mask), "col", 2 * mask)
                if at:
                    parts[at] = call(add_kernel, block, (parts[at], arrived), after=after)
                else:
                    got.append(arrived)
            mask *= 2
        return [parts[0], *got]

    def total(parts, after, flops=0):
        out, *rest = parts
        for part in rest:
            out = call(add_kernel, block, (out, part), after=after, flops=flops)
        return out

    if dense:
        table = jax.ShapeDtypeStruct((n_rows, n_cols), BF16)
        groups = math.gcd(capacity, 8)
        with jax.named_scope("split"):
            high, low = call(
                split_kernel,
                (table, table),
                (tile_count, plan, pltpu.with_memory_space_constraint(values, pltpu.HBM)),
                mebibytes=32,
                specs=[SCALARS, WHOLE, pl.BlockSpec(memory_space=pltpu.HBM)],
                scratch=[
                    pltpu.VMEM(values.shape, F32),
                    pltpu.SMEM(plan.shape, jnp.int32),
                    pltpu.SemaphoreType.DMA((groups,)),
                    pltpu.SemaphoreType.DMA,
                ],
            )
        with jax.named_scope("gather"):
            passed, late = gathered(high)
        with jax.named_scope("flip"):
            after = passed
            for at in range(1, n_row - 1):
                after = grads[at] = call(pass_kernel, block, [grads[at]], after=after)
            flipped = call(
                functools.partial(flip_kernel, tile),
                jax.ShapeDtypeStruct((2 * width, n_rows), BF16),
                grads,
                after=after,
            )
        with jax.named_scope("gather"):
            early = stacked(passed, flipped)
            other_early = swap(early, "col", 1)

        def backward_part(distances, core, after):
            shards = [shard_at(distance, core) for distance in distances]
            return call(
                functools.partial(backward_kernel, shards, tile),
                blocks(len(shards)),
                (flipped, high, low),
                mebibytes=24,
                after=after,
            )

        def shard_at(distance, core):
            count = half + 1
            if distance < count:
                return core * count + distance
            return 2 * count + core * (pairs - count) + distance - count

        def forward(embeds, after):
            return call(
                functools.partial(forward_kernel, len(embeds)),
                (block,) * n_row,
                (*embeds, high, low),
                mebibytes=24,
                scratch=[pltpu.VMEM((n_cols, 2 * width), BF16)],
                after=after,
            )

        with jax.named_scope("backward"):
            far, close = range(half, pairs), range(half)
            far_sent = backward_part(far, 1, early)
            far_kept = backward_part(far, 0, far_sent)
            sent = backward_part(close, 1, far_kept)
            kept = backward_part(close, 0, sent)
        with jax.named_scope("gather"):
            late = call(copy_kernel, blocks(half - 1), late, after=kept, flops=2 * 10**9)
            other_late = swap(late, "col", 1)
        with jax.named_scope("backward"):
            far_sums = chip_sums(far_kept, far_sent, late)
        with jax.named_scope("forward"):
            forwards = forward([early, other_early, late, other_late], far_sums[0])
        with jax.named_scope("reduce"):
            crossing = total(halved(far_sums, forwards[0]), forwards[0], 10**9)
        with jax.named_scope("reduce"):
            close_sums = chip_sums(kept, sent, forwards[0])
            after = None
    else:
        group = 8
        with jax.named_scope("gather"):
            passed, late = gathered(plan)
            early = stacked(passed, plan)
            late = call(copy_kernel, blocks(half - 1), late)
            panel = jnp.concatenate([early, swap(early, "col", 1), late, swap(late, "col", 1)])
        with jax.named_scope("slots"):
            forward, backward = pl.pallas_call(
                functools.partial(slots_kernel, tiles, pairs),
                out_shape=(
                    jax.ShapeDtypeStruct((n_rows, width), F32),
                    jax.ShapeDtypeStruct((n_cols, width), F32),
                ),
                grid=(capacity // group,),
                in_specs=[SCALARS, SCALARS, pl.BlockSpec((group, tile, tile), lambda at: (at, 0, 0)), WHOLE, WHOLE],
                out_specs=(WHOLE, WHOLE),
                compiler_params=params(40),
                cost_estimate=cost(12 * values.size * width, values.size * 4),
            )(tile_coords, tile_count, values, panel.reshape(-1, width), jnp.concatenate(grads))
            forwards = list(forward.reshape(n_row, shard, width))
            backward = backward.reshape(n_col, shard, width)
            count = half + 1
            kept, sent = (
                jnp.concatenate(
                    [
                        backward[core * count : (core + 1) * count],
                        backward[2 * count + core * (half - 1) : 2 * count + (core + 1) * (half - 1)],
                    ]
                )
                for core in range(2)
            )
        with jax.named_scope("reduce"):
            far_sums, close_sums = (chip_sums(kept[at : at + half], sent[at : at + half]) for at in (half, 0))
            crossing = total(halved(far_sums, forward), forward)
            after = forward

    with jax.named_scope("reduce"):
        mine, *grad_parts = halved(close_sums, after)
        first = [swap(forwards[k], "row", k) for k in range(1, n_row - 1)]
        row_sum = call(sum_kernel, block, [forwards[0], *first])
        mine = total([mine, swap(crossing, "col", 2 * half)], row_sum)
        row_sum = call(sum_kernel, block, [row_sum, swap(forwards[-1], "row", n_row - 1)], after=mine)
        return call(
            finish_kernel, (block, block), (row_sum, row_factor, col_factor, mine, *grad_parts), mebibytes=4
        )


def solution(mesh):
    return jax.shard_map(
        per_device,
        mesh=mesh,
        in_specs=(
            P(("row", "col"), None),
            P(("col", "row"), None),
            P("col", "row", None, None, None),
            P(None, "col", "row", None),
            P("col", "row"),
            P(("col", "row")),
            P(("row", "col")),
        ),
        out_specs=(P(("col", "row"), None), P(("row", "col"), None)),
        check_vma=False,
    )
```

```python
import functools
import math

import jax
import jax.numpy as jnp
from jax import lax
from jax.experimental import pallas as pl
from jax.experimental.pallas import tpu as pltpu
from jax.sharding import PartitionSpec as P

F32 = jnp.float32
BF16 = jnp.bfloat16
WHOLE = pl.BlockSpec(memory_space=pltpu.VMEM)
ANYWHERE = pl.BlockSpec(memory_space=pl.ANY)
SCALARS = pl.BlockSpec(memory_space=pltpu.SMEM)


def params(mebibytes):
    return pltpu.CompilerParams(vmem_limit_bytes=mebibytes * 2**20)


def cost(flops, moved):
    return pl.CostEstimate(flops=flops, bytes_accessed=moved, transcendentals=0)


def halves(x):
    high = x.astype(BF16)
    return high, (x - high.astype(F32)).astype(BF16)


def product(left, right):
    return jnp.dot(left, right, preferred_element_type=F32)


def row_factors(degree_ref, at, width):
    factors = lax.rsqrt(degree_ref[at : at + 1, :].astype(F32))
    return jnp.broadcast_to(factors, (width, factors.shape[1])).T


def scale_kernel(tiles, pairs, *refs):
    in_refs, (grad_ref, scaled_ref, row_factor_ref, col_factor_ref, plan_ref) = refs[:5], refs[5:10]
    bufs, sems = refs[10:15], refs[15]
    copies = [pltpu.make_async_copy(*pair, sems.at[at]) for at, pair in enumerate(zip(in_refs, bufs))]
    for copy in copies:
        copy.start()
    for copy in copies:
        copy.wait()
    cotangent, embed, row_degree, col_degree, coords = bufs
    for x_buf, degree_buf, out_ref, factor_ref in (
        (embed, col_degree, scaled_ref, col_factor_ref),
        (cotangent, row_degree, grad_ref, row_factor_ref),
    ):
        tile = degree_buf.shape[1]
        for at in range(degree_buf.shape[0]):
            rows = pl.ds(at * tile, tile)
            factors = row_factors(degree_buf, at, x_buf.shape[1])
            factor_ref[rows, :] = factors
            out_ref[rows, :] = x_buf[rows, :] * factors
    plan_ref[0:1, :] = row_place(coords[0, 0], tiles) * tile
    plan_ref[1:2, :] = col_place(coords[1, 0], tiles, pairs) * tile


def sum_kernel(*refs):
    *part_refs, out_ref = refs
    total = part_refs[0][...]
    for part_ref in part_refs[1:]:
        total = total + part_ref[...]
    out_ref[...] = total


def finish_kernel(row_ref, row_factor_ref, col_factor_ref, *refs):
    *part_refs, row_out_ref, col_out_ref = refs
    row_out_ref[...] = row_ref[...] * row_factor_ref[...]
    sum_kernel(*part_refs, col_out_ref)
    col_out_ref[...] = col_out_ref[...] * col_factor_ref[...]


def add_kernel(x_ref, y_ref, out_ref):
    out_ref[...] = x_ref[...] + y_ref[...]


def pair_kernel(kept_ref, got_ref, *out_refs):
    for at, out_ref in enumerate(out_refs):
        out_ref[...] = kept_ref[at] + got_ref[at]


def pass_kernel(x_ref, out_ref):
    out_ref[...] = x_ref[...]


def copy_kernel(*refs):
    *part_refs, out_ref = refs
    for at, part_ref in enumerate(part_refs):
        out_ref[at] = part_ref[...]


def row_place(tile_at, tiles):
    return tile_at ^ (lax.axis_index("row") * tiles)


def col_shard(distance, core, pairs):
    early = pairs // 2 + 1
    late = 2 * early + core * (pairs - early) + distance - early
    return jnp.where(distance < early, core * early + distance, late)


def col_place(tile_at, tiles, pairs):
    tile_at = tile_at ^ (lax.axis_index("col") * tiles)
    shard = lax.shift_right_logical(tile_at, tiles.bit_length() - 1)
    return col_shard(lax.shift_right_logical(shard, 1), shard & 1, pairs) * tiles + (tile_at & (tiles - 1))


def split_kernel(count_ref, plan_ref, values_ref, high_ref, low_ref, buf, places, sems, place_sem):
    capacity, tile, _ = values_ref.shape
    groups = sems.shape[0]
    group = capacity // groups
    count = count_ref[0, 0]
    live_groups = lax.div(count + (group - 1), group)

    def copy(at):
        slots = pl.ds(at * group, group)
        return pltpu.make_async_copy(values_ref.at[slots], buf.at[slots], sems.at[at])

    def store(slot, high, low):
        rows = pl.ds(pl.multiple_of(places[0, slot], tile), tile)
        cols = pl.ds(pl.multiple_of(places[1, slot], tile), tile)
        high_ref[rows, cols] = high
        low_ref[rows, cols] = low

    @pl.loop(0, live_groups)
    def _(at):
        copy(at).start()

    place_copy = pltpu.make_async_copy(plan_ref, places, place_sem)
    place_copy.start()
    place_copy.wait()

    @pl.loop(live_groups * group, capacity, unroll=1)
    def _(slot):
        zeros = jnp.zeros((tile, tile), BF16)
        store(slot, zeros, zeros)

    @pl.loop(0, live_groups)
    def _(at):
        copy(at).wait()

        @pl.loop(0, group, unroll=math.gcd(group, 8))
        def _(step):
            slot = at * group + step
            store(slot, *halves(jnp.where(slot < count, buf[slot], 0.0)))


def flip_kernel(tile, *refs):
    *grad_refs, out_ref = refs
    shard, width = grad_refs[0].shape
    for at, grad_ref in enumerate(grad_refs):
        for first in range(0, shard, tile):
            high, low = halves(grad_ref[pl.ds(first, tile), :].T)
            cols = pl.ds(at * shard + first, tile)
            out_ref[:width, cols] = high
            out_ref[width:, cols] = low


def backward_kernel(firsts, tile, grads_ref, high_ref, low_ref, out_ref):
    _, shard, width = out_ref.shape
    for at, first in enumerate(firsts):
        cols = pl.ds(first * shard, shard)
        both = product(grads_ref[...], high_ref[:, cols])
        total = both[:width] + both[width:] + product(grads_ref[:width, :], low_ref[:, cols])
        for row in range(0, shard, tile):
            out_ref[at, pl.ds(row, tile), :] = total[:, row : row + tile].T


def forward_kernel(count, *refs):
    embed_refs, (high_ref, low_ref), out_refs, panel = refs[:count], refs[count : count + 2], refs[count + 2 : -1], refs[-1]
    _, shard, width = embed_refs[0].shape
    done = 0
    for embeds_ref in embed_refs:
        for at in range(embeds_ref.shape[0]):
            high, low = halves(embeds_ref[at])
            panel[pl.ds(done, shard), :width] = high
            panel[pl.ds(done, shard), width:] = low
            done += shard
    for at, out_ref in enumerate(out_refs):
        rows = pl.ds(at * shard, shard)
        both = product(high_ref[rows, :], panel[...])
        out_ref[...] = both[:, :width] + both[:, width:] + product(low_ref[rows, :], panel[:, :width])


def slots_kernel(tiles, pairs, coords_ref, count_ref, values_ref, embed_ref, grad_ref, forward_ref, backward_ref):
    group, tile, _ = values_ref.shape
    first = pl.program_id(0) * group

    @pl.when(pl.program_id(0) == 0)
    def _():
        forward_ref[...] = jnp.zeros_like(forward_ref)
        backward_ref[...] = jnp.zeros_like(backward_ref)

    for slot in range(group):

        @pl.when(first + slot < count_ref[0, 0])
        def _():
            row_at = row_place(coords_ref[0, 0, 0, first + slot], tiles)
            col_at = col_place(coords_ref[1, 0, 0, first + slot], tiles, pairs)
            rows = pl.ds(pl.multiple_of(row_at * tile, tile), tile)
            cols = pl.ds(pl.multiple_of(col_at * tile, tile), tile)
            high, low = halves(values_ref[slot])
            embed_high, embed_low = halves(embed_ref[cols, :])
            forward_ref[rows, :] += product(high, embed_high) + product(high, embed_low) + product(low, embed_high)
            high, low = halves(values_ref[slot].T)
            grad_high, grad_low = halves(grad_ref[rows, :])
            backward_ref[cols, :] += product(high, grad_high) + product(high, grad_low) + product(low, grad_high)


def swap(x, axis, mask):
    return lax.ppermute(x, axis, [(at, at ^ mask) for at in range(lax.axis_size(axis))])


def call(kernel, out_shape, args, mebibytes=16, flops=0, scratch=(), specs=None, after=None):
    outs = out_shape if isinstance(out_shape, tuple) else (out_shape,)
    specs = specs or [WHOLE] * len(args)
    body = kernel
    if after is not None:
        args, specs = (after, *args), [ANYWHERE, *specs]

        def body(_, *refs):
            kernel(*refs)

    return pl.pallas_call(
        body,
        out_shape=out_shape,
        in_specs=specs,
        out_specs=tuple(WHOLE for _ in outs) if isinstance(out_shape, tuple) else WHOLE,
        scratch_shapes=scratch,
        compiler_params=params(mebibytes),
        cost_estimate=cost(flops, 1024),
    )(*args)


def per_device(embed, cotangent, tile_values, tile_coords, tile_count, row_degree, col_degree):
    shard, width = embed.shape
    capacity, tile = tile_values.shape[2:4]
    n_row, n_col = lax.axis_size("row"), lax.axis_size("col")
    pairs = n_col // 2
    half = pairs // 2
    tiles = shard // tile
    n_rows, n_cols = shard * n_row, shard * n_col
    dense = (n_rows // tile) * (n_cols // tile) <= capacity
    values = tile_values.reshape(tile_values.shape[2:])
    block = jax.ShapeDtypeStruct((shard, width), F32)

    def blocks(count):
        return jax.ShapeDtypeStruct((count, shard, width), F32)

    with jax.named_scope("scale"):
        args = (cotangent, embed, row_degree.reshape(-1, tile), col_degree.reshape(-1, tile), tile_coords)
        grad_scaled, scaled, row_factor, col_factor, plan = call(
            functools.partial(scale_kernel, tiles, pairs),
            (block,) * 4 + (jax.ShapeDtypeStruct((2, capacity), jnp.int32),),
            [pltpu.with_memory_space_constraint(x, pltpu.HBM) for x in args],
            mebibytes=4,
            specs=[pl.BlockSpec(memory_space=pltpu.HBM)] * len(args),
            scratch=[pltpu.VMEM(x.shape, x.dtype) for x in args] + [pltpu.SemaphoreType.DMA((len(args),))],
        )

    with jax.named_scope("gather"):
        crossed = swap(scaled, "col", 2 * half)
        grads = [grad_scaled] + [swap(grad_scaled, "row", k) for k in range(1, n_row)]
        near = {0: scaled}
        mask = half // 2
        while mask:
            near.update({at | mask: swap(x, "col", 2 * mask) for at, x in near.items()})
            mask //= 2

    def gathered(after):
        passed = call(pass_kernel, block, [crossed], after=after)
        late, mask = {0: passed}, half // 2
        while mask:
            late.update({at | mask: swap(x, "col", 2 * mask) for at, x in late.items()})
            mask //= 2
        return passed, [late[at] for at in range(1, half)]

    def stacked(passed, after):
        return call(copy_kernel, blocks(half + 1), [near[at] for at in range(half)] + [passed], after=after)

    def chip_sums(kept, sent, after=None):
        return call(
            pair_kernel,
            (block,) * kept.shape[0],
            (kept, swap(sent, "col", 1)),
            after=after,
        )

    def halved(parts, after):
        parts, got, mask = dict(enumerate(parts)), [], 1
        while mask < half:
            for at in reversed(range(0, half, 2 * mask)):
                arrived = swap(parts.pop(at + mask), "col", 2 * mask)
                if at:
                    parts[at] = call(add_kernel, block, (parts[at], arrived), after=after)
                else:
                    got.append(arrived)
            mask *= 2
        return [parts[0], *got]

    def total(parts, after, flops=0):
        out, *rest = parts
        for part in rest:
            out = call(add_kernel, block, (out, part), after=after, flops=flops)
        return out

    if dense:
        table = jax.ShapeDtypeStruct((n_rows, n_cols), BF16)
        groups = math.gcd(capacity, 8)
        with jax.named_scope("split"):
            high, low = call(
                split_kernel,
                (table, table),
                (tile_count, plan, pltpu.with_memory_space_constraint(values, pltpu.HBM)),
                mebibytes=32,
                specs=[SCALARS, WHOLE, pl.BlockSpec(memory_space=pltpu.HBM)],
                scratch=[
                    pltpu.VMEM(values.shape, F32),
                    pltpu.SMEM(plan.shape, jnp.int32),
                    pltpu.SemaphoreType.DMA((groups,)),
                    pltpu.SemaphoreType.DMA,
                ],
            )
        with jax.named_scope("gather"):
            passed, late = gathered(high)
        with jax.named_scope("flip"):
            after = passed
            for at in range(1, n_row - 1):
                after = grads[at] = call(pass_kernel, block, [grads[at]], after=after)
            flipped = call(
                functools.partial(flip_kernel, tile),
                jax.ShapeDtypeStruct((2 * width, n_rows), BF16),
                grads,
                after=after,
            )
        with jax.named_scope("gather"):
            early = stacked(passed, flipped)
            other_early = swap(early, "col", 1)

        def backward_part(distances, core, after):
            shards = [shard_at(distance, core) for distance in distances]
            return call(
                functools.partial(backward_kernel, shards, tile),
                blocks(len(shards)),
                (flipped, high, low),
                mebibytes=24,
                after=after,
            )

        def shard_at(distance, core):
            count = half + 1
            if distance < count:
                return core * count + distance
            return 2 * count + core * (pairs - count) + distance - count

        def forward(embeds, after):
            return call(
                functools.partial(forward_kernel, len(embeds)),
                (block,) * n_row,
                (*embeds, high, low),
                mebibytes=24,
                scratch=[pltpu.VMEM((n_cols, 2 * width), BF16)],
                after=after,
            )

        with jax.named_scope("backward"):
            far, close = range(half, pairs), range(half)
            far_sent = backward_part(far, 1, early)
            far_kept = backward_part(far, 0, far_sent)
            sent = backward_part(close, 1, far_kept)
            kept = backward_part(close, 0, sent)
        with jax.named_scope("gather"):
            late = call(copy_kernel, blocks(half - 1), late, after=kept, flops=2 * 10**9)
            other_late = swap(late, "col", 1)
        with jax.named_scope("backward"):
            far_sums = chip_sums(far_kept, far_sent, late)
        with jax.named_scope("forward"):
            forwards = forward([early, other_early, late, other_late], far_sums[0])
        with jax.named_scope("reduce"):
            crossing = total(halved(far_sums, forwards[0]), forwards[0], 10**9)
        with jax.named_scope("reduce"):
            close_sums = chip_sums(kept, sent, forwards[0])
            after = None
    else:
        group = 8
        with jax.named_scope("gather"):
            passed, late = gathered(plan)
            early = stacked(passed, plan)
            late = call(copy_kernel, blocks(half - 1), late)
            panel = jnp.concatenate([early, swap(early, "col", 1), late, swap(late, "col", 1)])
        with jax.named_scope("slots"):
            forward, backward = pl.pallas_call(
                functools.partial(slots_kernel, tiles, pairs),
                out_shape=(
                    jax.ShapeDtypeStruct((n_rows, width), F32),
                    jax.ShapeDtypeStruct((n_cols, width), F32),
                ),
                grid=(capacity // group,),
                in_specs=[SCALARS, SCALARS, pl.BlockSpec((group, tile, tile), lambda at: (at, 0, 0)), WHOLE, WHOLE],
                out_specs=(WHOLE, WHOLE),
                compiler_params=params(40),
                cost_estimate=cost(12 * values.size * width, values.size * 4),
            )(tile_coords, tile_count, values, panel.reshape(-1, width), jnp.concatenate(grads))
            forwards = list(forward.reshape(n_row, shard, width))
            backward = backward.reshape(n_col, shard, width)
            count = half + 1
            kept, sent = (
                jnp.concatenate(
                    [
                        backward[core * count : (core + 1) * count],
                        backward[2 * count + core * (half - 1) : 2 * count + (core + 1) * (half - 1)],
                    ]
                )
                for core in range(2)
            )
        with jax.named_scope("reduce"):
            far_sums, close_sums = (chip_sums(kept[at : at + half], sent[at : at + half]) for at in (half, 0))
            crossing = total(halved(far_sums, forward), forward)
            after = forward

    with jax.named_scope("reduce"):
        mine, *grad_parts = halved(close_sums, after)
        mine = total([mine, swap(crossing, "col", 2 * half)], None, 2 * 10**9)
        row_parts = [forwards[0]] + [swap(forwards[k], "row", k) for k in range(1, n_row)]
        row_sum = call(sum_kernel, block, row_parts, after=mine)
        return call(
            finish_kernel, (block, block), (row_sum, row_factor, col_factor, mine, *grad_parts), mebibytes=4
        )


def solution(mesh):
    return jax.shard_map(
        per_device,
        mesh=mesh,
        in_specs=(
            P(("row", "col"), None),
            P(("col", "row"), None),
            P("col", "row", None, None, None),
            P(None, "col", "row", None),
            P("col", "row"),
            P(("col", "row")),
            P(("row", "col")),
        ),
        out_specs=(P(("col", "row"), None), P(("row", "col"), None)),
        check_vma=False,
    )
```
